32 devices in a mesh: lat: 4 (over y, x), lon: 8 (over z, core).
Axes of the slice: x: 2, y: 2, z: 4, core: 2. Of those that a mesh axis runs over, the one named last changes fastest.
Arguments:
- obs_features: bfloat16 [65536, 128], P(('lat', 'lon')), may hold values from -6 to 6
- obs_dest: int32 [65536, 1], P(('lat', 'lon')), may hold values from 0 to 31; in each aligned block of 2048 rows (0 to 2047, 2048 to 4095, ...) at most 128 rows name the same one
- obs_cells: int32 [65536, 4], P(('lat', 'lon')), may hold values from 0 to 8099, as said below
- obs_gauss: int32 [65536, 4], P(('lat', 'lon')), may hold values from 0 to 31
- row_counts: int32 [32], P(('lat', 'lon')), may hold values from 512 to 2048, as said below
- background: bfloat16 [360, 720, 256], P('lat', 'lon'), may hold values from -6 to 6
- w_in: bfloat16 [128, 256], replicated, may hold values from -0.5 to 0.5
- w_bg: bfloat16 [256, 256], replicated, may hold values from -0.375 to 0.375
- w_dens: float32 [256], replicated, may hold values from -6 to 6
- conv_one: bfloat16 [3, 3, 256, 256], replicated, may hold values from -0.125 to 0.125
- conv_two: bfloat16 [3, 3, 256, 256], replicated, may hold values from -0.125 to 0.125
Outputs:
- encoded: bfloat16 [360, 720, 256], P('lat', 'lon')
The draws below stay inside these ranges and needn't reach their ends.
Inputs may be any that keep to these rules, and one draw needn't show every extreme that they name: `obs_cells`: each row names the four cells of a 2 by 2 square of its destination tile of 90 x 90 cells, flattened row-major: c, c + 1, c + 90, c + 91. `obs_dest`: among the rows of one device, no tile is named by more than 128 rows; some tile is named by exactly 128. `row_counts`: some device has all 2048 rows live.
All inputs are finite; a program needn't handle non-finite values.
Results may differ from the reference program's by a relative error of at most 0.0054.
Values may be sent and summed in bfloat16 or wider, within the bound.
No kernel may reach another device: no remote copies, remote signals or barrier semaphores. Data moves between devices by JAX's collectives and lax.ppermute only.
A program may use at most 192 MiB of HBM per device.

```python
import math
import jax
import jax.numpy as jnp
import numpy as np
from jax import lax

CH = 256
FEAT = 128
LAT_DEV = 90
LON_DEV = 90
ROWS_DEV = 2048
KCELL = 4
GBINS = 32
LAT_ALL = 360
LON_ALL = 720
OBS = 65536
CAP = 128
DEVICES = 32


def draw_obs_cells(key, part):
    key = jax.random.fold_in(key, 11)
    first, second = jax.random.split(key)
    base_lat = jax.random.randint(first, (OBS,), 0, LAT_DEV - 1)
    base_lon = jax.random.randint(second, (OBS,), 0, LON_DEV - 1)
    base_lat = base_lat.at[0].set(LAT_DEV - 2).at[1].set(0)
    base_lon = base_lon.at[0].set(LON_DEV - 2).at[1].set(0)
    base = base_lat * LON_DEV + base_lon
    return jnp.stack([base, base + 1, base + LON_DEV, base + LON_DEV + 1], axis=1).astype(jnp.int32)


def draw_row_counts(key, part):
    key = jax.random.fold_in(key, 23)
    first, second = jax.random.split(key)
    counts = jax.random.randint(first, (DEVICES,), ROWS_DEV // 4, ROWS_DEV + 1)
    picked = jax.random.randint(second, (), 0, DEVICES)
    places = jnp.arange(DEVICES)
    counts = jnp.where(places == picked, ROWS_DEV, counts)
    counts = jnp.where(places == (picked + 1) % DEVICES, ROWS_DEV // 4, counts)
    return counts.astype(jnp.int32)


def plant(values, key, smallest, largest):
    longest = values.shape.index(max(values.shape))
    spots = []
    for shift in (0, 1):
        where = [jax.random.randint(jax.random.fold_in(key, axis), (), 0, length) for axis, length in enumerate(values.shape)]
        where[longest] = (where[longest] + shift) % values.shape[longest]
        spots.append(tuple(where))
    return values.at[spots[0]].set(smallest).at[spots[1]].set(largest)


def steps_of(rng, shape, cuts, least, top_value):
    def one(position, parts):
        draws = jax.random.uniform(jax.random.fold_in(jax.random.fold_in(rng, 6), position), (parts,), jnp.float32, least / len(cuts), top_value / len(cuts))
        return jnp.repeat(jnp.exp(draws), shape[position] // parts).reshape((-1,) + (1,) * (len(shape) - position - 1))

    gain = one(*cuts[0])
    for cut in cuts[1:]:
        gain = gain * one(*cut)
    return gain


def routed_block(own_key, own, number, rows, number_of, top, reach, lean):
    order = jax.random.permutation(own_key, number_of)
    crowded, usual = portions_of(number_of, rows * top, reach, lean, True), portions_of(number_of, rows * top, reach, lean, False)
    places = jnp.arange(number_of)

    def named(sizes, turn):
        used = int((sizes > 0).sum())
        fixed = max(1, used // 4)
        shifted = fixed + (places - fixed + turn * (used - fixed)) % max(1, number_of - fixed)
        return jnp.zeros((number_of,), jnp.int32).at[order[jnp.where(places < fixed, places, shifted)]].set(jnp.asarray(sizes, jnp.int32))

    sizes = jnp.where(number % 4 == 0, named(crowded, number // 4), named(usual, number - number // 4 - 1))
    mixed = jax.random.permutation(jax.random.fold_in(own, 3), number_of)
    giver, receiver = mixed[0:number_of // 2 * 2:2], mixed[1:number_of // 2 * 2:2]
    margin = jnp.minimum(sizes[giver] - 1, reach - sizes[receiver]) // 2
    margin = jnp.where((giver == order[0]) | (receiver == order[0]) | (sizes[receiver] == 0), 0, jnp.maximum(margin, 0))
    shifted = jax.random.randint(jax.random.fold_in(own, 4), (number_of // 2,), 0, 1 << 20) % (margin + 1)
    sizes = sizes.at[giver].add(-shifted).at[receiver].add(shifted)
    members = jnp.searchsorted(jnp.cumsum(sizes), jnp.arange(rows * top), side="right").astype(jnp.int32)
    table = members.reshape(top, rows).T
    table = table[jax.random.permutation(jax.random.fold_in(own, 1), rows)]
    turn = jax.random.randint(jax.random.fold_in(own, 2), (rows, 1), 0, top)
    return jnp.take_along_axis(table, (jnp.arange(top)[None, :] + turn) % top, axis=1)


def portions_of(amount, total, reach, slope, full):
    loads = [(1 << 20) // math.isqrt(grade ** slope) + 1 for grade in range(1, amount + 1)]
    largest = reach if full else min(reach, max(-(-total // amount), total * loads[0] // sum(loads)))
    least = 1 if total - largest >= amount - 1 else 0
    holding, surplus = [largest] + [least] * (amount - 1), total - largest - least * (amount - 1)
    while surplus > 0:
        free = [i for i in range(1, amount) if holding[i] < largest] or [i for i in range(1, amount) if holding[i] < reach]
        whole, remaining = sum([loads[i] for i in free]), surplus
        for i in free:
            extra = min(reach - holding[i], max(1, remaining * loads[i] // whole), surplus)
            holding[i] = holding[i] + extra
            surplus = surplus - extra
    return np.array(holding)


def bell_draw(own_key, shape, width, limit, cuts=(), kind=jnp.bfloat16):
    level = steps_of(own_key, shape, cuts, -0.22, 0.18) if cuts else 1.0
    drawn = jax.random.normal(own_key, shape, jnp.float32) * width * level
    return jnp.minimum(jnp.maximum(drawn, -limit), limit).astype(kind)


def setup_inputs(seed: int = 0) -> dict:
    keys = jax.random.split(jax.random.key(seed), 12)
    obs_features = bell_draw(keys[0], (OBS, FEAT), 1.0, 6.0, ((0, 32),))
    obs_dest_keys = jax.random.split(jax.random.fold_in(keys[1], 1), OBS // ROWS_DEV)
    obs_dest_turns = jax.random.permutation(jax.random.fold_in(keys[1], 3), OBS // ROWS_DEV)
    obs_dest = jax.vmap(lambda own, number: routed_block(jax.random.fold_in(keys[1], 2), own, number, ROWS_DEV, DEVICES, 1, CAP, 2))(obs_dest_keys, obs_dest_turns).reshape((OBS, 1))
    obs_cells = draw_obs_cells(jax.random.fold_in(keys[11], 71), 0)
    obs_gauss = plant(jax.random.randint(keys[3], (OBS, KCELL), 0, GBINS), jax.random.fold_in(keys[3], 1), 0, GBINS - 1).astype(jnp.int32)
    row_counts = draw_row_counts(jax.random.fold_in(keys[11], 71), 0)
    background = bell_draw(keys[5], (LAT_ALL, LON_ALL, CH), 1.0, 6.0, ((0, 4), (1, 8)))
    w_in = bell_draw(keys[6], (FEAT, CH), FEAT ** -0.5, 0.5)
    w_bg = bell_draw(keys[7], (CH, CH), CH ** -0.5, 0.375)
    w_dens = bell_draw(keys[8], (CH,), 1.0, 6.0, (), jnp.float32)
    conv_one = bell_draw(keys[9], (3, 3, CH, CH), (9 * CH) ** -0.5, 0.125)
    conv_two = bell_draw(keys[10], (3, 3, CH, CH), (9 * CH) ** -0.5, 0.125)
    return dict(obs_features=obs_features, obs_dest=obs_dest, obs_cells=obs_cells, obs_gauss=obs_gauss, row_counts=row_counts, background=background, w_in=w_in, w_bg=w_bg, w_dens=w_dens, conv_one=conv_one, conv_two=conv_two)


def pad_field(field):
    half = LON_ALL // 2
    top = jnp.roll(field[0:1], half, axis=1)
    bottom = jnp.roll(field[-1:], half, axis=1)
    tall = jnp.concatenate([top, field, bottom], axis=0)
    return jnp.concatenate([tall[:, -1:], tall, tall[:, :1]], axis=1)


def convolve(field, weights):
    padded = pad_field(field)
    total = jnp.zeros((LAT_ALL * LON_ALL, CH), jnp.float32)
    for row_off in range(3):
        for col_off in range(3):
            window = padded[row_off:row_off + LAT_ALL, col_off:col_off + LON_ALL].reshape(LAT_ALL * LON_ALL, CH)
            total = total + jnp.dot(window, weights[row_off, col_off], preferred_element_type=jnp.float32)
    return total.reshape(LAT_ALL, LON_ALL, CH)


def reference(obs_features, obs_dest, obs_cells, obs_gauss, row_counts, background, w_in, w_bg, w_dens, conv_one, conv_two):
    nrows = obs_features.shape[0]
    index = jnp.arange(nrows, dtype=jnp.int32)
    live = (index % ROWS_DEV < row_counts[index // ROWS_DEV]).astype(jnp.float32)
    ratio = obs_gauss.astype(jnp.float32) / GBINS
    weight = (jnp.exp(-3.0 * ratio * ratio) * live[:, None]).astype(jnp.bfloat16)
    weight = lax.optimization_barrier(weight).astype(jnp.float32)
    dest = obs_dest[:, 0]
    sectors = LON_ALL // LON_DEV
    lat_pos = (dest // sectors)[:, None] * LAT_DEV + obs_cells // LON_DEV
    lon_pos = (dest % sectors)[:, None] * LON_DEV + obs_cells % LON_DEV
    flat = (lat_pos * LON_ALL + lon_pos).astype(jnp.int32)
    feats = obs_features.astype(jnp.float32)
    cells = LAT_ALL * LON_ALL
    sums = jnp.zeros((cells, FEAT), jnp.float32)
    density = jnp.zeros((cells,), jnp.float32)
    for slot in range(KCELL):
        sums = sums + jax.ops.segment_sum(weight[:, slot, None] * feats, flat[:, slot], num_segments=cells)
        density = density + jax.ops.segment_sum(weight[:, slot], flat[:, slot], num_segments=cells)
    normalized = (sums / (density + 1.0)[:, None]).astype(jnp.bfloat16)
    back_flat = background.reshape(cells, CH)
    start = jnp.dot(normalized, w_in, preferred_element_type=jnp.float32)
    start = start + jnp.dot(back_flat, w_bg, preferred_element_type=jnp.float32)
    start = start + density[:, None] * w_dens[None, :]
    first = start.astype(jnp.bfloat16).reshape(LAT_ALL, LON_ALL, CH)
    hidden = jax.nn.gelu(convolve(first, conv_one)).astype(jnp.bfloat16)
    return (first.astype(jnp.float32) + convolve(hidden, conv_two)).astype(jnp.bfloat16)
```

```python
import functools

import jax
import jax.numpy as jnp
from jax import lax
from jax.experimental import pallas as pl
from jax.experimental.pallas import tpu as pltpu
from jax.sharding import PartitionSpec as P

KCELL = 4
GBINS = 32
META = 16
GROUP = 6
CHUNK = 256
BF = jnp.bfloat16
F32 = jnp.float32


def params(mib):
    return pltpu.CompilerParams(vmem_limit_bytes=mib * 1024 * 1024)


def dot(a, b):
    return jnp.dot(a, b, preferred_element_type=F32)


def pack_kernel(devices, cap, cols, count_ref, dest_ref, cells_ref, gauss_ref, feat_ref, send_ref, ext_ref):
    nrows, nfeat = feat_ref.shape
    step = 256
    dest = dest_ref[...]
    row_id = lax.broadcasted_iota(jnp.int32, (1, nrows), 1)
    dest = jnp.where(row_id < count_ref[0], dest, devices)
    earlier = (
        lax.broadcasted_iota(jnp.int32, (step, step), 0) < lax.broadcasted_iota(jnp.int32, (step, step), 1)
    ).astype(F32).astype(BF)
    tile_id = lax.broadcasted_iota(jnp.int32, (devices, step), 0)
    carry = jnp.zeros((devices, 1), F32)
    ranks = []
    for begin in range(0, nrows, step):
        hot = (tile_id == dest[:, begin : begin + step]).astype(F32)
        before = dot(hot.astype(BF), earlier) + carry
        ranks.append(jnp.sum(before * hot, axis=0, keepdims=True))
        carry = carry + jnp.sum(hot, axis=1, keepdims=True)
    rank = jnp.concatenate(ranks, axis=1)
    base = cells_ref[0:1, :]
    lat = jnp.floor((base.astype(F32) + 0.5) * (1.0 / cols))
    lon = base.astype(F32) - lat * cols
    ratio = gauss_ref[...].astype(F32) * (1.0 / GBINS)
    weight = jnp.exp(-3.0 * ratio * ratio)
    meta = jnp.concatenate([lat, lon, weight, jnp.zeros((nfeat - 2 - KCELL, nrows), F32)], axis=0)
    ext_ref[:, :nfeat] = feat_ref[...]
    ext_ref[:, nfeat:] = meta.T.astype(BF)
    slot = lax.broadcasted_iota(jnp.int32, (cap, nrows), 0).astype(F32)

    def one(d, _):
        key = jnp.where(dest == d, rank, -1.0)
        pick = (slot == key).astype(F32).astype(BF)
        got = dot(pick, ext_ref[...])
        send_ref[d, 0:cap, :] = got[:, :nfeat].astype(BF)
        side = got[:, nfeat:]
        if cap < nfeat:
            side = jnp.concatenate([side, jnp.zeros((nfeat - cap, nfeat), F32)], axis=0)
        send_ref[d, cap : cap + META, :] = side.T[0:META].astype(BF)
        return 0

    lax.fori_loop(0, devices, one, 0)


def pack(count, dest, cells, gauss, feats, devices, cap, cols):
    nrows, nfeat = feats.shape
    return pl.pallas_call(
        functools.partial(pack_kernel, devices, cap, cols),
        out_shape=jax.ShapeDtypeStruct((devices, cap + META, nfeat), BF),
        in_specs=[pl.BlockSpec(memory_space=pltpu.SMEM)] + [pl.BlockSpec(memory_space=pltpu.VMEM)] * 4,
        out_specs=pl.BlockSpec(memory_space=pltpu.VMEM),
        scratch_shapes=[pltpu.VMEM((nrows, 2 * nfeat), BF)],
        compiler_params=params(48),
    )(count, dest, cells, gauss, feats)


def grid_kernel(
    devices, cap, wide, recv_ref, back_ref, w_in_ref, w_bg_ref, w_dens_ref, first_ref, edge_ref,
    feat_ref, meta_ref, acc_ref, back_scr, edge_scr, count_ref,
):
    group = pl.program_id(0)
    nfeat = recv_ref.shape[2]
    rows, cols, chans = back_ref.shape
    tiles = meta_ref.shape[0]

    @pl.when(group == 0)
    def _():
        meta_ref[...] = jnp.zeros(meta_ref.shape, F32)
        feat_ref[:, nfeat:] = jnp.ones((feat_ref.shape[0], nfeat), BF)
        lane = lax.broadcasted_iota(jnp.int32, (8, nfeat), 1)

        def count(s, _):
            side = recv_ref[s, cap : cap + META, :].astype(F32)
            count_ref[s] = jnp.sum((side[2:3] > 0).astype(jnp.int32))
            return 0

        lax.fori_loop(0, devices, count, 0, unroll=devices <= 32)

        def compact(s, begin):
            begin = pl.multiple_of(begin, 16)
            feat_ref[pl.ds(begin, cap), 0:nfeat] = recv_ref[s, 0:cap, :]
            side = recv_ref[s, cap : cap + META, :].astype(F32)[0:8]
            tile, shift = begin // nfeat, begin % nfeat
            moved = pltpu.roll(side, shift, axis=1)
            meta_ref[tile] = jnp.where(lane >= shift, moved, meta_ref[tile])
            meta_ref[tile + 1] = jnp.where(lane < shift, moved, 0.0)
            return begin + (count_ref[s] + 15) // 16 * 16

        total = lax.fori_loop(0, devices, compact, 0)
        last = pl.multiple_of(total, 16)
        feat_ref[pl.ds(last, CHUNK), 0:nfeat] = jnp.zeros((CHUNK, nfeat), BF)
        count_ref[devices] = (total + CHUNK - 1) // CHUNK

    acc_ref[...] = jnp.zeros(acc_ref.shape, F32)
    col_id = lax.broadcasted_iota(jnp.int32, (wide, CHUNK), 0).astype(F32)

    def chunk(k, _):
        side = jnp.concatenate([meta_ref[k * (CHUNK // nfeat) + q] for q in range(CHUNK // nfeat)], axis=1)
        lat, lon = side[0:1], side[1:2]
        here = (col_id == lon + 2.0).astype(F32).astype(BF)
        after = (col_id == lon + 3.0).astype(F32).astype(BF)
        parts = []
        for i in range(rows):
            row = (group * rows + i).astype(F32)
            same, above = lat == row, lat == row - 1.0
            left = jnp.where(same, side[2:3], jnp.where(above, side[4:5], 0.0)).astype(BF)
            right = jnp.where(same, side[3:4], jnp.where(above, side[5:6], 0.0)).astype(BF)
            parts.append(here * left + after * right)
        spread = jnp.concatenate(parts, axis=0)
        begin = pl.multiple_of(k * CHUNK, CHUNK)
        acc_ref[...] += dot(spread, feat_ref[pl.ds(begin, CHUNK), :])
        return 0

    lax.fori_loop(0, count_ref[devices], chunk, 0)
    for i in range(rows):
        back_scr[i * wide : i * wide + cols, :] = back_ref[i]
    start = pltpu.roll(dot(back_scr[...], w_bg_ref[...]), 2, axis=0)
    density = acc_ref[:, nfeat:]
    normalized = (acc_ref[:, :nfeat] / (density + 1.0)).astype(BF)
    start = start + dot(normalized, w_in_ref[...])
    start = start + jnp.concatenate([density] * (chans // nfeat), axis=1) * w_dens_ref[...]
    first = start.astype(BF)
    for i in range(rows):
        first_ref[i] = first[i * wide : (i + 1) * wide]
        for k, col in enumerate((2, 3, cols, cols + 1)):
            edge_scr[k, pl.ds(group * rows + i, 1), :] = start[i * wide + col : i * wide + col + 1]

    @pl.when(group == pl.num_programs(0) - 1)
    def _():
        edge_ref[...] = edge_scr[...].astype(BF)


def gridded(recv, background, w_in, w_bg, w_dens, cap, wide):
    devices, _, nfeat = recv.shape
    lat_rows, cols, chans = background.shape
    slots = devices * cap
    tall = -(-lat_rows // 16) * 16
    whole = pl.BlockSpec(memory_space=pltpu.VMEM)
    return pl.pallas_call(
        functools.partial(grid_kernel, devices, cap, wide),
        grid=(lat_rows // GROUP,),
        out_shape=(
            jax.ShapeDtypeStruct((lat_rows, wide, chans), BF),
            jax.ShapeDtypeStruct((4, tall, chans), BF),
        ),
        in_specs=[
            whole,
            pl.BlockSpec((GROUP, cols, chans), lambda g: (g, 0, 0)),
            whole,
            whole,
            whole,
        ],
        out_specs=(
            pl.BlockSpec((GROUP, wide, chans), lambda g: (g, 0, 0)),
            pl.BlockSpec((4, tall, chans), lambda g: (0, 0, 0)),
        ),
        scratch_shapes=[
            pltpu.VMEM((slots + 2 * CHUNK, 2 * nfeat), BF),
            pltpu.VMEM((slots // nfeat + 4, 8, nfeat), F32),
            pltpu.VMEM((GROUP * wide, 2 * nfeat), F32),
            pltpu.VMEM((GROUP * wide, chans), BF),
            pltpu.VMEM((4, tall, chans), F32),
            pltpu.SMEM((devices + 1,), jnp.int32),
        ],
        compiler_params=params(48),
    )(recv, background, w_in, w_bg, w_dens)


def three(value):
    size = value.shape[0]
    return [value.astype(BF), pltpu.roll(value, size - 1, axis=0).astype(BF), pltpu.roll(value, size - 2, axis=0).astype(BF)]


def conv_kernel(
    pole_ref, first_ref, west_ref, east_ref, north_ref, south_ref, one_ref, two_ref, out_ref,
    wide_in, wide_hid, cols_scr,
):
    group = pl.program_id(0)
    lat_rows, wide, chans = first_ref.shape
    rows, cols, _ = out_ref.shape
    block = rows * wide

    def put(ref, begin, size, value):
        for b, part in enumerate(three(value)):
            ref[pl.ds(begin, size), b * chans : (b + 1) * chans] = part

    @pl.when(group == 0)
    def _():
        cols_scr[0:2] = west_ref[...].astype(F32)
        cols_scr[2:4] = east_ref[...].astype(F32)
        row_id = lax.broadcasted_iota(jnp.int32, (wide, chans), 0)

        def load(r, _):
            value = first_ref[r].astype(F32)
            for k, col in enumerate((0, 1, cols + 2, cols + 3)):
                value = jnp.where(row_id == col, cols_scr[k, pl.ds(r, 1), :], value)
            put(wide_in, pl.multiple_of((r + 2) * wide, 16), wide, value)
            return 0

        lax.fori_loop(0, lat_rows, load, 0)
        put(wide_in, wide, wide, north_ref[0].astype(F32))
        put(wide_in, 0, wide, north_ref[1].astype(F32))
        put(wide_in, (lat_rows + 2) * wide, wide, south_ref[0].astype(F32))
        put(wide_in, (lat_rows + 3) * wide, wide, south_ref[1].astype(F32))
        for side, begin in ((0, 0), (1, lat_rows + 1)):
            total = jnp.zeros((wide, chans), F32)
            for a in range(3):
                pick = jnp.where(pole_ref[side] == 1, 2 - a, a)
                total = total + dot(wide_in[(begin + a) * wide : (begin + a + 1) * wide, :], one_ref[pick])
            put(wide_hid, begin * wide, wide, jax.nn.gelu(total))

        def hidden(g, _):
            begin = pl.multiple_of((g * rows + 1) * wide, 16)
            total = dot(wide_in[pl.ds(begin, block), :], one_ref[0])
            total = total + dot(wide_in[pl.ds(begin + wide, block), :], one_ref[1])
            total = total + dot(wide_in[pl.ds(begin + 2 * wide, block), :], one_ref[2])
            put(wide_hid, begin, block, jax.nn.gelu(total))
            return 0

        lax.fori_loop(0, lat_rows // rows, hidden, 0)

    begin = pl.multiple_of(group * block, 16)
    total = wide_in[pl.ds(begin + 2 * wide, block), 2 * chans :].astype(F32)
    total = total + dot(wide_hid[pl.ds(begin, block), :], two_ref[0])
    total = total + dot(wide_hid[pl.ds(begin + wide, block), :], two_ref[1])
    total = total + dot(wide_hid[pl.ds(begin + 2 * wide, block), :], two_ref[2])
    result = total.astype(BF)
    for i in range(rows):
        out_ref[i] = result[i * wide : i * wide + cols]


def convolved(poles, first, west, east, north, south, one, two, cols):
    lat_rows, wide, chans = first.shape
    whole = pl.BlockSpec(memory_space=pltpu.VMEM)
    return pl.pallas_call(
        conv_kernel,
        grid=(lat_rows // GROUP,),
        out_shape=jax.ShapeDtypeStruct((lat_rows, cols, chans), BF),
        in_specs=[pl.BlockSpec(memory_space=pltpu.SMEM)] + [whole] * 7,
        out_specs=pl.BlockSpec((GROUP, cols, chans), lambda g: (g, 0, 0)),
        scratch_shapes=[
            pltpu.VMEM(((lat_rows + 4) * wide, 3 * chans), BF),
            pltpu.VMEM(((lat_rows + 2) * wide, 3 * chans), BF),
            pltpu.VMEM((4, west.shape[1], chans), F32),
        ],
        compiler_params=params(60),
    )(poles, first, west, east, north, south, one, two)


def row_pairs(lat_count, lon_count):
    half = lon_count // 2

    def flat(lat, lon):
        return lat * lon_count + lon % lon_count

    inner, outer = [], []
    for lon in range(lon_count):
        for lat in range(0, lat_count, 2):
            inner += [(flat(lat, lon), flat(lat + 1, lon)), (flat(lat + 1, lon), flat(lat, lon))]
        for lat in range(1, lat_count - 1, 2):
            outer += [(flat(lat, lon), flat(lat + 1, lon)), (flat(lat + 1, lon), flat(lat, lon))]
        outer += [(flat(lat, lon), flat(lat, lon + half)) for lat in (0, lat_count - 1)]
    return inner, outer


def shards(
    obs_features,
    obs_dest,
    obs_cells,
    obs_gauss,
    row_counts,
    background,
    w_in,
    w_bg,
    w_dens,
    conv_one,
    conv_two,
):
    nrows, nfeat = obs_features.shape
    lat_rows, cols, chans = background.shape
    axes = ("lat", "lon")
    devices = lax.axis_size(axes)
    lat_count, lon_count = lax.axis_size("lat"), lax.axis_size("lon")
    cap = 2 * nrows // devices
    wide = -(-(cols + 4) // 16) * 16
    send = pack(
        row_counts, obs_dest.reshape(1, nrows), obs_cells.T, obs_gauss.T, obs_features, devices, cap, cols
    )
    recv = lax.all_to_all(send, axes, split_axis=0, concat_axis=0, tiled=True)
    first, edges = gridded(recv, background, w_in, w_bg, w_dens.reshape(1, chans), cap, wide)
    west = lax.ppermute(edges[2:4], "lon", [(i, (i + 1) % lon_count) for i in range(lon_count)])
    east = lax.ppermute(edges[0:2], "lon", [((i + 1) % lon_count, i) for i in range(lon_count)])
    lat_index = lax.axis_index("lat")
    even = lat_index % 2 == 0

    def rows_at(near, far):
        body = jnp.stack([first[near], first[far]])[:, 2 : cols + 2]
        left = jnp.stack([west[:, near], west[:, far]])
        right = jnp.stack([east[:, near], east[:, far]])
        fill = jnp.zeros((2, wide - cols - 4, chans), BF)
        return jnp.concatenate([left, body, right, fill], axis=1)

    top, bottom = rows_at(0, 1), rows_at(lat_rows - 1, lat_rows - 2)
    inner, outer = row_pairs(lat_count, lon_count)
    by_inner = lax.ppermute(jnp.where(even, bottom, top), axes, inner)
    by_outer = lax.ppermute(jnp.where(even, top, bottom), axes, outer)
    north = jnp.where(even, by_outer, by_inner)
    south = jnp.where(even, by_inner, by_outer)
    poles = jnp.stack([lat_index == 0, lat_index == lat_count - 1]).astype(jnp.int32)
    return convolved(
        poles,
        first,
        west,
        east,
        north,
        south,
        conv_one.reshape(3, 3 * chans, chans),
        conv_two.reshape(3, 3 * chans, chans),
        cols,
    )


def solution(mesh):
    rows = P(("lat", "lon"), None)
    in_specs = (rows, rows, rows, rows, P(("lat", "lon")), P("lat", "lon", None), P(), P(), P(), P(), P())
    return jax.shard_map(
        shards, mesh=mesh, in_specs=in_specs, out_specs=P("lat", "lon", None), check_vma=False
    )
```

```python
import functools

import jax
import jax.numpy as jnp
from jax import lax
from jax.experimental import pallas as pl
from jax.experimental.pallas import tpu as pltpu
from jax.sharding import PartitionSpec as P

KCELL = 4
GBINS = 32
META = 16
GROUP = 6
BAND = 18
CHUNK = 256
BF = jnp.bfloat16
F32 = jnp.float32


def params(mib):
    return pltpu.CompilerParams(vmem_limit_bytes=mib * 1024 * 1024)


def dot(a, b):
    return jnp.dot(a, b, preferred_element_type=F32)


def pack_kernel(
    devices, cap, cols, bands, count_ref, dest_ref, cells_ref, gauss_ref, feat_ref, send_ref,
    ext_ref, hot_ref, sorted_ref, place_ref, place_smem, sem,
):
    nrows, nfeat = feat_ref.shape
    step = 256
    classes = 2 * bands
    kinds = devices * classes
    dest = dest_ref[...]
    row_id = lax.broadcasted_iota(jnp.int32, (1, nrows), 1)
    base = cells_ref[0:1, :].astype(F32)
    lat = jnp.floor((base + 0.5) * (1.0 / cols))
    lon = base - lat * cols
    band = jnp.floor((lat + 0.5) * (1.0 / BAND))
    kind = 2.0 * band + (lat == band * BAND + (BAND - 1)).astype(F32)
    kind = dest * classes + kind.astype(jnp.int32)
    kind = jnp.where(row_id < count_ref[0], kind, kinds)
    ratio = gauss_ref[...].astype(F32) * (1.0 / GBINS)
    weight = jnp.exp(-3.0 * ratio * ratio)
    meta = jnp.concatenate([lat, lon, weight, jnp.zeros((nfeat - 2 - KCELL, nrows), F32)], axis=0)
    ext_ref[:, :nfeat] = feat_ref[...]
    ext_ref[:, nfeat:] = meta.T.astype(BF)
    hot_ref[...] = (lax.broadcasted_iota(jnp.int32, (kinds, nrows), 0) == kind).astype(F32).astype(BF)
    counts = dot(hot_ref[...], jnp.ones((nrows, nfeat), BF))
    ka = lax.broadcasted_iota(jnp.int32, (kinds, kinds), 0)
    kb = lax.broadcasted_iota(jnp.int32, (kinds, kinds), 1)
    da, db = ka // classes, kb // classes
    within = ((da == db) & (kb < ka)).astype(F32).astype(BF)
    together = (da == db).astype(F32).astype(BF)
    ahead = ((db < da) & (kb % classes == 0)).astype(F32).astype(BF)
    loads = dot(together, counts.astype(BF))
    padded = jnp.floor((loads + 7.0) * 0.125) * 8.0
    begins = dot(ahead, padded.astype(BF))
    mine = begins + dot(within, counts.astype(BF))
    kind_id = lax.broadcasted_iota(jnp.int32, (kinds, nfeat), 0)
    lane_id = lax.broadcasted_iota(jnp.int32, (kinds, nfeat), 1)
    lead = kind_id == lane_id * classes
    place_ref[0:1, :] = jnp.sum(jnp.where(lead, begins, 0.0), axis=0, keepdims=True).astype(jnp.int32)
    place_ref[1:2, :] = jnp.sum(jnp.where(lead, loads, 0.0), axis=0, keepdims=True).astype(jnp.int32)
    copy = pltpu.make_async_copy(place_ref, place_smem, sem)
    copy.start()
    earlier = (
        lax.broadcasted_iota(jnp.int32, (step, step), 0) < lax.broadcasted_iota(jnp.int32, (step, step), 1)
    ).astype(F32).astype(BF)
    carry = mine[:, 0:1]
    places = []
    for begin in range(0, nrows, step):
        hot = hot_ref[:, begin : begin + step]
        before = dot(hot, earlier) + carry
        hot = hot.astype(F32)
        places.append(
            jnp.sum(before * hot, axis=0, keepdims=True) + jnp.sum(hot, axis=0, keepdims=True) - 1.0
        )
        carry = carry + jnp.sum(hot, axis=1, keepdims=True)
    place = jnp.concatenate(places, axis=1)
    live = row_id < count_ref[0]
    place = jnp.where(live, place, -1.0)
    slot = lax.broadcasted_iota(jnp.int32, (step, nrows), 0).astype(F32)
    span = sorted_ref.shape[0]
    for k in range(-(-(nrows + 8 * devices) // step)):
        pick = (slot == place - k * step).astype(F32).astype(BF)
        sorted_ref[k * step : (k + 1) * step, :] = dot(pick, ext_ref[...])
    tail = -(-(nrows + 8 * devices) // step) * step
    sorted_ref[tail:span, :] = jnp.zeros((span - tail, 2 * nfeat), F32)
    copy.wait()
    side_lane = lax.broadcasted_iota(jnp.int32, (META, nfeat), 1)

    def one(d, _):
        begin = pl.multiple_of(place_smem[0, d], 8)
        got = sorted_ref[pl.ds(begin, cap), :]
        send_ref[d, 0:cap, :] = got[:, :nfeat].astype(BF)
        side = got[:, nfeat:]
        if cap < nfeat:
            side = jnp.concatenate([side, jnp.zeros((nfeat - cap, nfeat), F32)], axis=0)
        side = jnp.where(side_lane < place_smem[1, d], side.T[0:META], 0.0)
        send_ref[d, cap : cap + META, :] = side.astype(BF)
        return 0

    lax.fori_loop(0, devices, one, 0, unroll=4)


def pack(count, dest, cells, gauss, feats, devices, cap, cols, bands):
    nrows, nfeat = feats.shape
    span = -(-(nrows + 8 * devices) // 256) * 256 + cap
    kinds = devices * 2 * bands
    return pl.pallas_call(
        functools.partial(pack_kernel, devices, cap, cols, bands),
        out_shape=jax.ShapeDtypeStruct((devices, cap + META, nfeat), BF),
        in_specs=[pl.BlockSpec(memory_space=pltpu.SMEM)] + [pl.BlockSpec(memory_space=pltpu.VMEM)] * 4,
        out_specs=pl.BlockSpec(memory_space=pltpu.VMEM),
        scratch_shapes=[
            pltpu.VMEM((nrows, 2 * nfeat), BF),
            pltpu.VMEM((kinds, nrows), BF),
            pltpu.VMEM((span, 2 * nfeat), F32),
            pltpu.VMEM((8, nfeat), jnp.int32),
            pltpu.SMEM((8, nfeat), jnp.int32),
            pltpu.SemaphoreType.DMA,
        ],
        compiler_params=params(56),
    )(count, dest, cells, gauss, feats)


def grid_kernel(
    devices, cap, wide, lat_bands, recv_ref, back_ref, w_in_ref, w_bg_ref, w_dens_ref, first_ref, edge_ref,
    rows_ref, lats_ref, feat_ref, meta_ref, acc_ref, back_scr, edge_scr, ends_ref, ends_smem, sem,
):
    band = pl.program_id(0)
    bands = pl.num_programs(0)
    nfeat = recv_ref.shape[2]
    rows, cols, chans = back_ref.shape
    slots = devices * cap

    @pl.when(band == 0)
    def _():
        feat_ref[...] = jnp.zeros(feat_ref.shape, F32)
        rows_ref[slots:, :] = jnp.zeros((rows_ref.shape[0] - slots, nfeat), F32)

        def widen(s, _):
            rows_ref[pl.ds(pl.multiple_of(s * cap, cap), cap), :] = recv_ref[s, 0:cap, :].astype(F32)
            side = recv_ref[s, cap : cap + META, :].astype(F32)
            lats_ref[pl.ds(s, 1), :] = jnp.where(side[2:3] > 0, side[0:1], 1e6)
            return 0

        lax.fori_loop(0, devices, widen, 0, unroll=4)
        lats = lats_ref[...]
        lane = lax.broadcasted_iota(jnp.int32, (devices, nfeat), 1)
        ends = jnp.zeros((devices, nfeat), F32)
        for b in range(lat_bands):
            low = jnp.sum((lats < b * rows - 1.0).astype(F32), axis=1, keepdims=True)
            high = jnp.sum((lats < (b + 1.0) * rows).astype(F32), axis=1, keepdims=True)
            ends = jnp.where(lane == 2 * b, low, jnp.where(lane == 2 * b + 1, high, ends))
        ends_ref[...] = ends.astype(jnp.int32)
        copy = pltpu.make_async_copy(ends_ref, ends_smem, sem)
        copy.start()
        copy.wait()

    meta_ref[...] = jnp.zeros(meta_ref.shape, F32)
    lane = lax.broadcasted_iota(jnp.int32, (8, nfeat), 1)

    def compact(s, out):
        out = pl.multiple_of(out, 8)
        low, high = ends_smem[s, 2 * band], ends_smem[s, 2 * band + 1]
        source = pl.multiple_of(low // 8 * 8, 8)
        feat_ref[pl.ds(out, cap), :] = rows_ref[pl.ds(pl.multiple_of(s * cap + source, 8), cap), :]
        side = recv_ref[s, cap : cap + META, :].astype(F32)[0:8]
        side = jnp.where((lane >= low) & (lane < high), side, 0.0)
        shift = out - source + nfeat
        tile, shift = shift // nfeat, shift % nfeat
        moved = pltpu.roll(side, shift, axis=1)
        meta_ref[tile] += jnp.where(lane >= shift, moved, 0.0)
        meta_ref[tile + 1] += jnp.where(lane < shift, moved, 0.0)
        return out + (high - source + 7) // 8 * 8

    total = lax.fori_loop(0, devices, compact, 0, unroll=4)
    acc_ref[...] = jnp.zeros(acc_ref.shape, F32)
    col_id = lax.broadcasted_iota(jnp.int32, (wide, CHUNK), 0).astype(F32)

    def chunk(k, _):
        side = jnp.concatenate(
            [meta_ref[1 + k * (CHUNK // nfeat) + q] for q in range(CHUNK // nfeat)], axis=1
        )
        lat, lon = side[0:1], side[1:2]
        here = (col_id == lon + 2.0).astype(F32).astype(BF)
        after = (col_id == lon + 3.0).astype(F32).astype(BF)
        parts = []
        for i in range(rows):
            row = (band * rows + i).astype(F32)
            same, above = lat == row, lat == row - 1.0
            left = jnp.where(same, side[2:3], jnp.where(above, side[4:5], 0.0)).astype(BF)
            right = jnp.where(same, side[3:4], jnp.where(above, side[5:6], 0.0)).astype(BF)
            parts.append(here * left + after * right)
        spread = jnp.concatenate(parts, axis=0)
        begin = pl.multiple_of(k * CHUNK, CHUNK)
        values = jnp.concatenate(
            [feat_ref[pl.ds(begin, CHUNK), :].astype(BF), jnp.ones((CHUNK, nfeat), BF)], axis=1
        )
        acc_ref[...] += dot(spread, values)
        return 0

    lax.fori_loop(0, (total + CHUNK - 1) // CHUNK, chunk, 0)
    for g in range(0, rows, GROUP):
        for i in range(GROUP):
            back_scr[i * wide : i * wide + cols, :] = back_ref[g + i]
        sums = acc_ref[g * wide : (g + GROUP) * wide, :]
        start = pltpu.roll(dot(back_scr[...], w_bg_ref[...]), 2, axis=0)
        density = sums[:, nfeat:]
        normalized = (sums[:, :nfeat] / (density + 1.0)).astype(BF)
        start = start + dot(normalized, w_in_ref[...])
        start = start + jnp.concatenate([density] * (chans // nfeat), axis=1) * w_dens_ref[...]
        first = start.astype(BF)
        for i in range(GROUP):
            first_ref[band * rows + g + i] = first[i * wide : (i + 1) * wide]
            for k, col in enumerate((2, 3, cols, cols + 1)):
                edge_scr[k, pl.ds(band * rows + g + i, 1), :] = start[i * wide + col : i * wide + col + 1]

    @pl.when(band == bands - 1)
    def _():
        edge_ref[...] = edge_scr[...].astype(BF)


def gridded(recv, background, w_in, w_bg, w_dens, cap, wide):
    devices, _, nfeat = recv.shape
    lat_rows, cols, chans = background.shape
    slots = devices * cap
    tall = -(-lat_rows // 16) * 16
    whole = pl.BlockSpec(memory_space=pltpu.VMEM)
    return pl.pallas_call(
        functools.partial(grid_kernel, devices, cap, wide, lat_rows // BAND),
        grid=(lat_rows // BAND,),
        out_shape=(
            jax.ShapeDtypeStruct((lat_rows, wide, chans), BF),
            jax.ShapeDtypeStruct((4, tall, chans), BF),
        ),
        in_specs=[
            whole,
            pl.BlockSpec((BAND, cols, chans), lambda g: (g, 0, 0)),
            whole,
            whole,
            whole,
        ],
        out_specs=(whole, whole),
        scratch_shapes=[
            pltpu.VMEM((slots + cap, nfeat), F32),
            pltpu.VMEM((devices, nfeat), F32),
            pltpu.VMEM((slots + cap + CHUNK, nfeat), F32),
            pltpu.VMEM((slots // nfeat + 6, 8, nfeat), F32),
            pltpu.VMEM((BAND * wide, 2 * nfeat), F32),
            pltpu.VMEM((GROUP * wide, chans), BF),
            pltpu.VMEM((4, tall, chans), F32),
            pltpu.VMEM((devices, nfeat), jnp.int32),
            pltpu.SMEM((devices, nfeat), jnp.int32),
            pltpu.SemaphoreType.DMA,
        ],
        compiler_params=params(40),
    )(recv, background, w_in, w_bg, w_dens)


def three(value):
    size = value.shape[0]
    return [value.astype(BF), pltpu.roll(value, size - 1, axis=0).astype(BF), pltpu.roll(value, size - 2, axis=0).astype(BF)]


def conv_kernel(
    pole_ref, first_ref, west_ref, east_ref, north_ref, south_ref, one_ref, two_ref, out_ref,
    wide_in, wide_hid, cols_scr,
):
    group = pl.program_id(0)
    lat_rows, wide, chans = first_ref.shape
    rows, cols, _ = out_ref.shape
    block = rows * wide

    def put(ref, begin, size, value):
        for b, part in enumerate(three(value)):
            ref[pl.ds(begin, size), b * chans : (b + 1) * chans] = part

    @pl.when(group == 0)
    def _():
        cols_scr[0:2] = west_ref[...].astype(F32)
        cols_scr[2:4] = east_ref[...].astype(F32)
        row_id = lax.broadcasted_iota(jnp.int32, (wide, chans), 0)

        def load(r, _):
            value = first_ref[r].astype(F32)
            for k, col in enumerate((0, 1, cols + 2, cols + 3)):
                value = jnp.where(row_id == col, cols_scr[k, pl.ds(r, 1), :], value)
            put(wide_in, pl.multiple_of((r + 2) * wide, 16), wide, value)
            return 0

        lax.fori_loop(0, lat_rows, load, 0)
        put(wide_in, wide, wide, north_ref[0].astype(F32))
        put(wide_in, 0, wide, north_ref[1].astype(F32))
        put(wide_in, (lat_rows + 2) * wide, wide, south_ref[0].astype(F32))
        put(wide_in, (lat_rows + 3) * wide, wide, south_ref[1].astype(F32))
        for side, begin in ((0, 0), (1, lat_rows + 1)):
            total = jnp.zeros((wide, chans), F32)
            for a in range(3):
                pick = jnp.where(pole_ref[side] == 1, 2 - a, a)
                total = total + dot(wide_in[(begin + a) * wide : (begin + a + 1) * wide, :], one_ref[pick])
            put(wide_hid, begin * wide, wide, jax.nn.gelu(total))

        def hidden(g, _):
            begin = pl.multiple_of((g * rows + 1) * wide, 16)
            total = dot(wide_in[pl.ds(begin, block), :], one_ref[0])
            total = total + dot(wide_in[pl.ds(begin + wide, block), :], one_ref[1])
            total = total + dot(wide_in[pl.ds(begin + 2 * wide, block), :], one_ref[2])
            put(wide_hid, begin, block, jax.nn.gelu(total))
            return 0

        lax.fori_loop(0, lat_rows // rows, hidden, 0)

    begin = pl.multiple_of(group * block, 16)
    total = wide_in[pl.ds(begin + 2 * wide, block), 2 * chans :].astype(F32)
    total = total + dot(wide_hid[pl.ds(begin, block), :], two_ref[0])
    total = total + dot(wide_hid[pl.ds(begin + wide, block), :], two_ref[1])
    total = total + dot(wide_hid[pl.ds(begin + 2 * wide, block), :], two_ref[2])
    result = total.astype(BF)
    for i in range(rows):
        out_ref[i] = result[i * wide : i * wide + cols]


def convolved(poles, first, west, east, north, south, one, two, cols):
    lat_rows, wide, chans = first.shape
    whole = pl.BlockSpec(memory_space=pltpu.VMEM)
    return pl.pallas_call(
        conv_kernel,
        grid=(lat_rows // GROUP,),
        out_shape=jax.ShapeDtypeStruct((lat_rows, cols, chans), BF),
        in_specs=[pl.BlockSpec(memory_space=pltpu.SMEM)] + [whole] * 7,
        out_specs=pl.BlockSpec((GROUP, cols, chans), lambda g: (g, 0, 0)),
        scratch_shapes=[
            pltpu.VMEM(((lat_rows + 4) * wide, 3 * chans), BF),
            pltpu.VMEM(((lat_rows + 2) * wide, 3 * chans), BF),
            pltpu.VMEM((4, west.shape[1], chans), F32),
        ],
        compiler_params=params(44),
    )(poles, first, west, east, north, south, one, two)


def row_pairs(lat_count, lon_count):
    half = lon_count // 2

    def flat(lat, lon):
        return lat * lon_count + lon % lon_count

    inner, outer = [], []
    for lon in range(lon_count):
        for lat in range(0, lat_count, 2):
            inner += [(flat(lat, lon), flat(lat + 1, lon)), (flat(lat + 1, lon), flat(lat, lon))]
        for lat in range(1, lat_count - 1, 2):
            outer += [(flat(lat, lon), flat(lat + 1, lon)), (flat(lat + 1, lon), flat(lat, lon))]
        outer += [(flat(lat, lon), flat(lat, lon + half)) for lat in (0, lat_count - 1)]
    return inner, outer


def shards(
    obs_features,
    obs_dest,
    obs_cells,
    obs_gauss,
    row_counts,
    background,
    w_in,
    w_bg,
    w_dens,
    conv_one,
    conv_two,
):
    nrows, nfeat = obs_features.shape
    lat_rows, cols, chans = background.shape
    axes = ("lat", "lon")
    devices = lax.axis_size(axes)
    lat_count, lon_count = lax.axis_size("lat"), lax.axis_size("lon")
    cap = 2 * nrows // devices
    wide = -(-(cols + 4) // 16) * 16
    send = pack(
        row_counts, obs_dest.reshape(1, nrows), obs_cells.T, obs_gauss.T, obs_features, devices, cap, cols,
        lat_rows // BAND,
    )
    recv = lax.all_to_all(send, axes, split_axis=0, concat_axis=0, tiled=True)
    first, edges = gridded(recv, background, w_in, w_bg, w_dens.reshape(1, chans), cap, wide)
    west = lax.ppermute(edges[2:4], "lon", [(i, (i + 1) % lon_count) for i in range(lon_count)])
    east = lax.ppermute(edges[0:2], "lon", [((i + 1) % lon_count, i) for i in range(lon_count)])
    lat_index = lax.axis_index("lat")
    even = lat_index % 2 == 0

    def rows_at(near, far):
        body = jnp.stack([first[near], first[far]])[:, 2 : cols + 2]
        left = jnp.stack([west[:, near], west[:, far]])
        right = jnp.stack([east[:, near], east[:, far]])
        fill = jnp.zeros((2, wide - cols - 4, chans), BF)
        return jnp.concatenate([left, body, right, fill], axis=1)

    top, bottom = rows_at(0, 1), rows_at(lat_rows - 1, lat_rows - 2)
    inner, outer = row_pairs(lat_count, lon_count)
    by_inner = lax.ppermute(jnp.where(even, bottom, top), axes, inner)
    by_outer = lax.ppermute(jnp.where(even, top, bottom), axes, outer)
    north = jnp.where(even, by_outer, by_inner)
    south = jnp.where(even, by_inner, by_outer)
    poles = jnp.stack([lat_index == 0, lat_index == lat_count - 1]).astype(jnp.int32)
    return convolved(
        poles,
        first,
        west,
        east,
        north,
        south,
        conv_one.reshape(3, 3 * chans, chans),
        conv_two.reshape(3, 3 * chans, chans),
        cols,
    )


def solution(mesh):
    rows = P(("lat", "lon"), None)
    in_specs = (rows, rows, rows, rows, P(("lat", "lon")), P("lat", "lon", None), P(), P(), P(), P(), P())
    return jax.shard_map(
        shards, mesh=mesh, in_specs=in_specs, out_specs=P("lat", "lon", None), check_vma=False
    )
```

```python
import functools

import jax
import jax.numpy as jnp
from jax import lax
from jax.experimental import pallas as pl
from jax.experimental.pallas import tpu as pltpu
from jax.sharding import PartitionSpec as P

KCELL = 4
GBINS = 32
META = 16
GROUP = 6
BAND = 18
CHUNK = 256
FINISH = 15
BF = jnp.bfloat16
F32 = jnp.float32


def params(mib):
    return pltpu.CompilerParams(vmem_limit_bytes=mib * 1024 * 1024)


def dot(a, b):
    return jnp.dot(a, b, preferred_element_type=F32)


def pack_kernel(
    devices, cap, cols, bands, count_ref, dest_ref, cells_ref, gauss_ref, feat_ref, send_ref,
    ext_ref, hot_ref, sorted_ref, place_ref, place_smem, sem,
):
    nrows, nfeat = feat_ref.shape
    step = 256
    classes = 2 * bands
    kinds = devices * classes
    dest = dest_ref[...]
    row_id = lax.broadcasted_iota(jnp.int32, (1, nrows), 1)
    base = cells_ref[0:1, :].astype(F32)
    lat = jnp.floor((base + 0.5) * (1.0 / cols))
    lon = base - lat * cols
    band = jnp.floor((lat + 0.5) * (1.0 / BAND))
    kind = 2.0 * band + (lat == band * BAND + (BAND - 1)).astype(F32)
    kind = dest * classes + kind.astype(jnp.int32)
    kind = jnp.where(row_id < count_ref[0], kind, kinds)
    ratio = gauss_ref[...].astype(F32) * (1.0 / GBINS)
    weight = jnp.exp(-3.0 * ratio * ratio)
    meta = jnp.concatenate([lat, lon, weight, jnp.zeros((nfeat - 2 - KCELL, nrows), F32)], axis=0)
    ext_ref[:, :nfeat] = feat_ref[...]
    ext_ref[:, nfeat:] = meta.T.astype(BF)
    hot_ref[...] = (lax.broadcasted_iota(jnp.int32, (kinds, nrows), 0) == kind).astype(F32).astype(BF)
    counts = dot(hot_ref[...], jnp.ones((nrows, nfeat), BF))
    ka = lax.broadcasted_iota(jnp.int32, (kinds, kinds), 0)
    kb = lax.broadcasted_iota(jnp.int32, (kinds, kinds), 1)
    da, db = ka // classes, kb // classes
    within = ((da == db) & (kb < ka)).astype(F32).astype(BF)
    together = (da == db).astype(F32).astype(BF)
    ahead = ((db < da) & (kb % classes == 0)).astype(F32).astype(BF)
    loads = dot(together, counts.astype(BF))
    padded = jnp.floor((loads + 7.0) * 0.125) * 8.0
    begins = dot(ahead, padded.astype(BF))
    mine = begins + dot(within, counts.astype(BF))
    kind_id = lax.broadcasted_iota(jnp.int32, (kinds, nfeat), 0)
    lane_id = lax.broadcasted_iota(jnp.int32, (kinds, nfeat), 1)
    lead = kind_id == lane_id * classes
    place_ref[0:1, :] = jnp.sum(jnp.where(lead, begins, 0.0), axis=0, keepdims=True).astype(jnp.int32)
    place_ref[1:2, :] = jnp.sum(jnp.where(lead, loads, 0.0), axis=0, keepdims=True).astype(jnp.int32)
    copy = pltpu.make_async_copy(place_ref, place_smem, sem)
    copy.start()
    earlier = (
        lax.broadcasted_iota(jnp.int32, (step, step), 0) < lax.broadcasted_iota(jnp.int32, (step, step), 1)
    ).astype(F32).astype(BF)
    carry = mine[:, 0:1]
    places = []
    for begin in range(0, nrows, step):
        hot = hot_ref[:, begin : begin + step]
        before = dot(hot, earlier) + carry
        hot = hot.astype(F32)
        places.append(
            jnp.sum(before * hot, axis=0, keepdims=True) + jnp.sum(hot, axis=0, keepdims=True) - 1.0
        )
        carry = carry + jnp.sum(hot, axis=1, keepdims=True)
    place = jnp.concatenate(places, axis=1)
    live = row_id < count_ref[0]
    place = jnp.where(live, place, -1.0)
    slot = lax.broadcasted_iota(jnp.int32, (step, nrows), 0).astype(F32)
    span = sorted_ref.shape[0]
    for k in range(-(-(nrows + 8 * devices) // step)):
        pick = (slot == place - k * step).astype(F32).astype(BF)
        sorted_ref[k * step : (k + 1) * step, :] = dot(pick, ext_ref[...])
    tail = -(-(nrows + 8 * devices) // step) * step
    sorted_ref[tail:span, :] = jnp.zeros((span - tail, 2 * nfeat), F32)
    copy.wait()
    side_lane = lax.broadcasted_iota(jnp.int32, (META, nfeat), 1)

    def one(d, _):
        begin = pl.multiple_of(place_smem[0, d], 8)
        got = sorted_ref[pl.ds(begin, cap), :]
        send_ref[d, 0:cap, :] = got[:, :nfeat].astype(BF)
        side = got[:, nfeat:]
        if cap < nfeat:
            side = jnp.concatenate([side, jnp.zeros((nfeat - cap, nfeat), F32)], axis=0)
        side = jnp.where(side_lane < place_smem[1, d], side.T[0:META], 0.0)
        send_ref[d, cap : cap + META, :] = side.astype(BF)
        return 0

    lax.fori_loop(0, devices, one, 0, unroll=4)


def pack(count, dest, cells, gauss, feats, devices, cap, cols, bands):
    nrows, nfeat = feats.shape
    span = -(-(nrows + 8 * devices) // 256) * 256 + cap
    kinds = devices * 2 * bands
    return pl.pallas_call(
        functools.partial(pack_kernel, devices, cap, cols, bands),
        out_shape=jax.ShapeDtypeStruct((devices, cap + META, nfeat), BF),
        in_specs=[pl.BlockSpec(memory_space=pltpu.SMEM)] + [pl.BlockSpec(memory_space=pltpu.VMEM)] * 4,
        out_specs=pl.BlockSpec(memory_space=pltpu.VMEM),
        scratch_shapes=[
            pltpu.VMEM((nrows, 2 * nfeat), BF),
            pltpu.VMEM((kinds, nrows), BF),
            pltpu.VMEM((span, 2 * nfeat), F32),
            pltpu.VMEM((8, nfeat), jnp.int32),
            pltpu.SMEM((8, nfeat), jnp.int32),
            pltpu.SemaphoreType.DMA,
        ],
        compiler_params=params(56),
    )(count, dest, cells, gauss, feats)


def back_kernel(wide, back_ref, w_in_ref, w_bg_ref, w_dens_ref, out_ref, w_in_out, w_dens_out, scr):
    band = pl.program_id(0)
    rows, cols, chans = back_ref.shape
    for i in range(rows):
        scr[i * wide : i * wide + cols, :] = back_ref[i]
    begin = pl.multiple_of(band * rows * wide, 16)
    out_ref[pl.ds(begin, rows * wide), :] = pltpu.roll(dot(scr[...], w_bg_ref[...]), 2, axis=0)
    w_in_out[...] = w_in_ref[...]
    w_dens_out[...] = w_dens_ref[...]


def projected(background, w_in, w_bg, w_dens, wide):
    lat_rows, cols, chans = background.shape
    whole = pl.BlockSpec(memory_space=pltpu.VMEM)
    return pl.pallas_call(
        functools.partial(back_kernel, wide),
        grid=(lat_rows // BAND,),
        out_shape=(
            jax.ShapeDtypeStruct((lat_rows * wide, chans), F32),
            jax.ShapeDtypeStruct(w_in.shape, BF),
            jax.ShapeDtypeStruct(w_dens.shape, F32),
        ),
        in_specs=[pl.BlockSpec((BAND, cols, chans), lambda g: (g, 0, 0)), whole, whole, whole],
        out_specs=(whole, whole, whole),
        scratch_shapes=[pltpu.VMEM((BAND * wide, chans), BF)],
        compiler_params=params(24),
    )(background, w_in, w_bg, w_dens)


def grid_kernel(
    devices, cap, wide, cols, lat_bands, recv_ref, back_ref, w_in_ref, w_dens_ref,
    first_ref, west_ref, east_ref, inner_ref, outer_ref, corner_ref,
    rows_ref, lats_ref, feat_ref, meta_ref, acc_ref, edge_scr, ends_ref, ends_smem, sem,
):
    band = pl.program_id(0)
    bands = pl.num_programs(0)
    nfeat = recv_ref.shape[2]
    lat_rows, _, chans = first_ref.shape
    rows = lat_rows // lat_bands
    slots = devices * cap

    @pl.when(band == 0)
    def _():
        feat_ref[...] = jnp.zeros(feat_ref.shape, F32)
        rows_ref[slots:, :] = jnp.zeros((rows_ref.shape[0] - slots, nfeat), F32)

        def widen(s, _):
            rows_ref[pl.ds(pl.multiple_of(s * cap, cap), cap), :] = recv_ref[s, 0:cap, :].astype(F32)
            side = recv_ref[s, cap : cap + META, :].astype(F32)
            lats_ref[pl.ds(s, 1), :] = jnp.where(side[2:3] > 0, side[0:1], 1e6)
            return 0

        lax.fori_loop(0, devices, widen, 0, unroll=4)
        lats = lats_ref[...]
        lane = lax.broadcasted_iota(jnp.int32, (devices, nfeat), 1)
        ends = jnp.zeros((devices, nfeat), F32)
        for b in range(lat_bands):
            low = jnp.sum((lats < b * rows - 1.0).astype(F32), axis=1, keepdims=True)
            high = jnp.sum((lats < (b + 1.0) * rows).astype(F32), axis=1, keepdims=True)
            ends = jnp.where(lane == 2 * b, low, jnp.where(lane == 2 * b + 1, high, ends))
        ends_ref[...] = ends.astype(jnp.int32)
        copy = pltpu.make_async_copy(ends_ref, ends_smem, sem)
        copy.start()
        copy.wait()

    meta_ref[...] = jnp.zeros(meta_ref.shape, F32)
    lane = lax.broadcasted_iota(jnp.int32, (8, nfeat), 1)

    def compact(s, out):
        out = pl.multiple_of(out, 8)
        low, high = ends_smem[s, 2 * band], ends_smem[s, 2 * band + 1]
        source = pl.multiple_of(low // 8 * 8, 8)
        feat_ref[pl.ds(out, cap), :] = rows_ref[pl.ds(pl.multiple_of(s * cap + source, 8), cap), :]
        side = recv_ref[s, cap : cap + META, :].astype(F32)[0:8]
        side = jnp.where((lane >= low) & (lane < high), side, 0.0)
        shift = out - source + nfeat
        tile, shift = shift // nfeat, shift % nfeat
        moved = pltpu.roll(side, shift, axis=1)
        meta_ref[tile] += jnp.where(lane >= shift, moved, 0.0)
        meta_ref[tile + 1] += jnp.where(lane < shift, moved, 0.0)
        return out + (high - source + 7) // 8 * 8

    total = lax.fori_loop(0, devices, compact, 0, unroll=4)
    acc_ref[...] = jnp.zeros(acc_ref.shape, F32)
    col_id = lax.broadcasted_iota(jnp.int32, (wide, CHUNK), 0).astype(F32)

    def chunk(k, _):
        side = jnp.concatenate(
            [meta_ref[1 + k * (CHUNK // nfeat) + q] for q in range(CHUNK // nfeat)], axis=1
        )
        lat, lon = side[0:1], side[1:2]
        here = (col_id == lon + 2.0).astype(F32).astype(BF)
        after = (col_id == lon + 3.0).astype(F32).astype(BF)
        parts = []
        for i in range(rows):
            row = (band * rows + i).astype(F32)
            same, above = lat == row, lat == row - 1.0
            left = jnp.where(same, side[2:3], jnp.where(above, side[4:5], 0.0)).astype(BF)
            right = jnp.where(same, side[3:4], jnp.where(above, side[5:6], 0.0)).astype(BF)
            parts.append(here * left + after * right)
        spread = jnp.concatenate(parts, axis=0)
        begin = pl.multiple_of(k * CHUNK, CHUNK)
        values = jnp.concatenate(
            [feat_ref[pl.ds(begin, CHUNK), :].astype(BF), jnp.ones((CHUNK, nfeat), BF)], axis=1
        )
        acc_ref[...] += dot(spread, values)
        return 0

    lax.fori_loop(0, (total + CHUNK - 1) // CHUNK, chunk, 0)
    for g in range(0, rows, GROUP):
        sums = acc_ref[g * wide : (g + GROUP) * wide, :]
        begin = pl.multiple_of((band * rows + g) * wide, 16)
        start = back_ref[pl.ds(begin, GROUP * wide), :]
        density = sums[:, nfeat:]
        normalized = (sums[:, :nfeat] / (density + 1.0)).astype(BF)
        start = start + dot(normalized, w_in_ref[...])
        start = start + jnp.concatenate([density] * (chans // nfeat), axis=1) * w_dens_ref[...]
        first = start.astype(BF)
        for i in range(GROUP):
            first_ref[band * rows + g + i] = first[i * wide : (i + 1) * wide]
            for k, col in enumerate((2, 3, cols, cols + 1)):
                edge_scr[k, pl.ds(band * rows + g + i, 1), :] = start[i * wide + col : i * wide + col + 1]

    @pl.when(band == bands - 1)
    def _():
        west_ref[...] = edge_scr[0:2].astype(BF)
        east_ref[...] = edge_scr[2:4].astype(BF)
        even = lax.axis_index("lat") % 2 == 0
        for k in range(2):
            top, bottom = first_ref[k].astype(F32), first_ref[lat_rows - 1 - k].astype(F32)
            inner = jnp.where(even, bottom, top).astype(BF)
            outer = jnp.where(even, top, bottom).astype(BF)
            inner_ref[k] = inner
            outer_ref[k] = outer
            corner_ref[0, k] = inner[:16]
            corner_ref[1, k] = inner[wide - 16 :]
            corner_ref[2, k] = outer[:16]
            corner_ref[3, k] = outer[wide - 16 :]


def gridded(recv, back, w_in, w_dens, cap, wide, lat_rows, cols):
    devices, _, nfeat = recv.shape
    chans = back.shape[1]
    slots = devices * cap
    tall = -(-lat_rows // 16) * 16
    whole = pl.BlockSpec(memory_space=pltpu.VMEM)
    return pl.pallas_call(
        functools.partial(grid_kernel, devices, cap, wide, cols, lat_rows // BAND),
        grid=(lat_rows // BAND,),
        out_shape=(
            jax.ShapeDtypeStruct((lat_rows, wide, chans), BF),
            jax.ShapeDtypeStruct((2, tall, chans), BF),
            jax.ShapeDtypeStruct((2, tall, chans), BF),
            jax.ShapeDtypeStruct((2, wide, chans), BF),
            jax.ShapeDtypeStruct((2, wide, chans), BF),
            jax.ShapeDtypeStruct((4, 2, 16, chans), BF),
        ),
        in_specs=[whole] * 4,
        out_specs=(whole,) * 6,
        scratch_shapes=[
            pltpu.VMEM((slots + cap, nfeat), F32),
            pltpu.VMEM((devices, nfeat), F32),
            pltpu.VMEM((slots + cap + CHUNK, nfeat), F32),
            pltpu.VMEM((slots // nfeat + 6, 8, nfeat), F32),
            pltpu.VMEM((BAND * wide, 2 * nfeat), F32),
            pltpu.VMEM((4, tall, chans), F32),
            pltpu.VMEM((devices, nfeat), jnp.int32),
            pltpu.SMEM((devices, nfeat), jnp.int32),
            pltpu.SemaphoreType.DMA,
        ],
        compiler_params=params(32),
    )(recv, back, w_in, w_dens)


def put(ref, begin, value):
    size, chans = value.shape
    for b in range(3):
        part = value if b == 0 else pltpu.roll(value, size - b, axis=0)
        ref[pl.ds(begin, size), b * chans : (b + 1) * chans] = part.astype(BF)


def taps(ref, begin, size, wide, w_ref):
    field = jnp.concatenate([ref[pl.ds(begin + a * wide, size), :] for a in range(3)], axis=1)
    return dot(field, w_ref[...].reshape(field.shape[1], w_ref.shape[2]))


def inside_kernel(split, first_ref, one_ref, hid_ref, field):
    lat_rows, wide, chans = first_ref.shape

    def load(r, _):
        put(field, pl.multiple_of(r * wide, 16), first_ref[r].astype(F32))
        return 0

    lax.fori_loop(0, lat_rows, load, 0, unroll=6)
    size = (lat_rows - 2) // split * wide

    def hidden(g, _):
        begin = pl.multiple_of(g * size, 16)
        total = taps(field, begin, size, wide, one_ref)
        put(hid_ref, pl.multiple_of(begin + 2 * wide, 16), jax.nn.gelu(total))
        return 0

    lax.fori_loop(0, split, hidden, 0)


def inside(first, one):
    lat_rows, wide, chans = first.shape
    whole = pl.BlockSpec(memory_space=pltpu.VMEM)
    split = next(n for n in (4, 2, 1) if (lat_rows - 2) % n == 0)
    return pl.pallas_call(
        functools.partial(inside_kernel, split),
        out_shape=jax.ShapeDtypeStruct(((lat_rows + 2) * wide, 3 * chans), BF),
        in_specs=[whole] * 2,
        out_specs=whole,
        scratch_shapes=[pltpu.VMEM((lat_rows * wide, 3 * chans), BF)],
        compiler_params=params(30),
    )(first, one)


def finish_kernel(
    lat_count, hid_in, first_ref, own_west, own_east, west_ref, east_ref, inner_ref, outer_ref,
    inner_left, inner_right, outer_left, outer_right, one_ref, two_ref, out_ref, hid_ref, rim, cols_scr,
):
    group = pl.program_id(0)
    lat_rows, wide, chans = first_ref.shape
    rows, cols, _ = out_ref.shape
    block = rows * wide

    @pl.when(group == 0)
    def _():
        lat_index = lax.axis_index("lat")
        even = lat_index % 2 == 0
        row_id = lax.broadcasted_iota(jnp.int32, (wide, chans), 0)
        short_id = lax.broadcasted_iota(jnp.int32, (16, chans), 0)

        def edge_row(first_half, k):
            def pick(inner, outer):
                return jnp.where(even == first_half, outer[k].astype(F32), inner[k].astype(F32))

            middle = pick(inner_ref, outer_ref)
            left = pltpu.roll(pick(inner_left, outer_left), (wide - cols) % 16, axis=0)
            right = pltpu.roll(pick(inner_right, outer_right), (cols - (wide - 16)) % 16, axis=0)
            head = jnp.where(short_id < 2, left, middle[:16])
            at = short_id + (wide - 16)
            tail = jnp.where((at == cols + 2) | (at == cols + 3), right, middle[wide - 16 :])
            return jnp.concatenate([head, middle[16 : wide - 16], tail], axis=0)

        def own_row(r):
            value = first_ref[r].astype(F32)
            sides = [west_ref[0], west_ref[1], east_ref[0], east_ref[1]]
            for side, col in zip(sides, (0, 1, cols + 2, cols + 3)):
                value = jnp.where(row_id == col, side.astype(F32)[r : r + 1], value)
            return value

        lines = [edge_row(True, 1), edge_row(True, 0), own_row(0), own_row(1)]
        lines += [own_row(lat_rows - 2), own_row(lat_rows - 1), edge_row(False, 0), edge_row(False, 1)]
        for n, line in enumerate(lines):
            put(rim, n * wide, line)
        for begin, index, pole in ((0, 0, lat_index == 0), (5, lat_rows + 1, lat_index == lat_count - 1)):
            total = jnp.zeros((wide, chans), F32)
            for a in range(3):
                tap = jnp.where(pole, 2 - a, a)
                total = total + dot(rim[(begin + a) * wide : (begin + a + 1) * wide, :], one_ref[tap])
            put(hid_ref, index * wide, jax.nn.gelu(total))
        total = jnp.zeros((2 * wide, chans), F32)
        for a in range(3):
            pair = [rim[(n + a) * wide : (n + a + 1) * wide, :] for n in (1, 4)]
            total = total + dot(jnp.concatenate(pair, axis=0), one_ref[a])
        total = jax.nn.gelu(total)
        put(hid_ref, wide, total[:wide])
        put(hid_ref, lat_rows * wide, total[wide:])

        lines = [west_ref[0], west_ref[1], own_west[0], own_west[1]]
        lines += [own_east[0], own_east[1], east_ref[0], east_ref[1]]
        windows = [jnp.concatenate(lines[n : n + 3], axis=1) for n in (0, 1, 4, 5)]
        windows = jnp.concatenate(windows, axis=0)
        size = windows.shape[0]
        total = pltpu.roll(dot(windows, one_ref[0]), 1, axis=0) + dot(windows, one_ref[1])
        total = total + pltpu.roll(dot(windows, one_ref[2]), size - 1, axis=0)
        total = jax.nn.gelu(total)
        tall = size // 4
        for n in range(4):
            cols_scr[n] = total[n * tall : (n + 1) * tall]
        last = wide - 16

        def patch(r, _):
            fixes = [cols_scr[n, pl.ds(r, 1), :] for n in range(4)]
            begin = pl.multiple_of((r + 1) * wide, 16)
            for b in range(3):
                lanes = slice(b * chans, (b + 1) * chans)
                for start in (0, last):
                    edits = [
                        (col - b - start, fix)
                        for col, fix in zip((0, 1, cols, cols + 1), fixes)
                        if 0 <= col - b - start < 16
                    ]
                    if edits:
                        value = hid_ref[pl.ds(begin + start, 16), lanes].astype(F32)
                        for at, fix in edits:
                            value = jnp.where(short_id == at, fix, value)
                        hid_ref[pl.ds(begin + start, 16), lanes] = value.astype(BF)
            return 0

        lax.fori_loop(1, lat_rows - 1, patch, 0, unroll=8)

    begin = pl.multiple_of(group * block, 16)
    total = taps(hid_ref, begin, block, wide, two_ref)
    own = first_ref[pl.ds(group * rows, rows)].reshape(block, chans).astype(F32)
    total = total + pltpu.roll(own, block - 2, axis=0)
    result = total.astype(BF)
    for i in range(rows):
        out_ref[i] = result[i * wide : i * wide + cols]


def finished(hid, first, sides, one, two, cols, lat_count):
    lat_rows, wide, chans = first.shape
    whole = pl.BlockSpec(memory_space=pltpu.VMEM)
    out, _ = pl.pallas_call(
        functools.partial(finish_kernel, lat_count),
        grid=(lat_rows // FINISH,),
        out_shape=(
            jax.ShapeDtypeStruct((lat_rows, cols, chans), BF),
            jax.ShapeDtypeStruct(hid.shape, BF),
        ),
        in_specs=[whole] * (4 + len(sides)),
        out_specs=(pl.BlockSpec((FINISH, cols, chans), lambda g: (g, 0, 0)), whole),
        input_output_aliases={0: 1},
        scratch_shapes=[
            pltpu.VMEM((8 * wide, 3 * chans), BF),
            pltpu.VMEM((4, sides[0].shape[1], chans), F32),
        ],
        compiler_params=params(26),
    )(hid, first, *sides, one, two)
    return out


def row_pairs(lat_count, lon_count):
    half = lon_count // 2
    inner, outer = [], []
    for lon in range(lon_count):
        for lat in range(0, lat_count, 2):
            inner += [((lat, lon), (lat + 1, lon)), ((lat + 1, lon), (lat, lon))]
        for lat in range(1, lat_count - 1, 2):
            outer += [((lat, lon), (lat + 1, lon)), ((lat + 1, lon), (lat, lon))]
        outer += [((lat, lon), (lat, lon + half)) for lat in (0, lat_count - 1)]
    return inner, outer


def shards(
    obs_features,
    obs_dest,
    obs_cells,
    obs_gauss,
    row_counts,
    background,
    w_in,
    w_bg,
    w_dens,
    conv_one,
    conv_two,
):
    nrows, nfeat = obs_features.shape
    lat_rows, cols, chans = background.shape
    axes = ("lat", "lon")
    devices = lax.axis_size(axes)
    lat_count, lon_count = lax.axis_size("lat"), lax.axis_size("lon")
    cap = 2 * nrows // devices
    wide = -(-(cols + 4) // 16) * 16
    send = pack(
        row_counts, obs_dest.reshape(1, nrows), obs_cells.T, obs_gauss.T, obs_features, devices, cap, cols,
        lat_rows // BAND,
    )
    recv = lax.all_to_all(send, axes, split_axis=0, concat_axis=0, tiled=True)
    back, w_in, w_dens = projected(background, w_in, w_bg, w_dens.reshape(1, chans), wide)
    first, own_west, own_east, inner_row, outer_row, corners = gridded(
        recv, back, w_in, w_dens, cap, wide, lat_rows, cols
    )
    inner, outer = row_pairs(lat_count, lon_count)

    def moved(value, pairs, turn):
        flat = [
            (source[0] * lon_count + source[1], to[0] * lon_count + (to[1] + turn) % lon_count)
            for source, to in pairs
        ]
        return lax.ppermute(value, axes, flat)

    here = [((lat, lon), (lat, lon)) for lat in range(lat_count) for lon in range(lon_count)]
    sides = (
        own_west,
        own_east,
        moved(own_east, here, 1),
        moved(own_west, here, -1),
        moved(inner_row, inner, 0),
        moved(outer_row, outer, 0),
        moved(corners[1], inner, 1),
        moved(corners[0], inner, -1),
        moved(corners[3], outer, 1),
        moved(corners[2], outer, -1),
    )
    one = conv_one.reshape(3, 3 * chans, chans)
    two = conv_two.reshape(3, 3 * chans, chans)
    hid = inside(first, one)
    return finished(hid, first, sides, one, two, cols, lat_count)


def solution(mesh):
    rows = P(("lat", "lon"), None)
    in_specs = (rows, rows, rows, rows, P(("lat", "lon")), P("lat", "lon", None), P(), P(), P(), P(), P())
    return jax.shard_map(
        shards, mesh=mesh, in_specs=in_specs, out_specs=P("lat", "lon", None), check_vma=False
    )
```

```python
import functools

import jax
import jax.numpy as jnp
from jax import lax
from jax.experimental import pallas as pl
from jax.experimental.pallas import tpu as pltpu
from jax.sharding import PartitionSpec as P

KCELL = 4
GBINS = 32
META = 16
GROUP = 6
BAND = 18
CHUNK = 256
FINISH = 15
BF = jnp.bfloat16
F32 = jnp.float32


def params(mib):
    return pltpu.CompilerParams(vmem_limit_bytes=mib * 1024 * 1024)


def dot(a, b):
    return jnp.dot(a, b, preferred_element_type=F32)


def pack_kernel(
    devices, cap, cols, bands, count_ref, dest_ref, cells_ref, gauss_ref, feat_ref, send_ref,
    ext_ref, hot_ref, sorted_ref, place_ref, place_smem, sem,
):
    nrows, nfeat = feat_ref.shape
    step = 256
    classes = 2 * bands
    kinds = devices * classes
    dest = dest_ref[...]
    row_id = lax.broadcasted_iota(jnp.int32, (1, nrows), 1)
    base = cells_ref[0:1, :].astype(F32)
    lat = jnp.floor((base + 0.5) * (1.0 / cols))
    lon = base - lat * cols
    band = jnp.floor((lat + 0.5) * (1.0 / BAND))
    kind = 2.0 * band + (lat == band * BAND + (BAND - 1)).astype(F32)
    kind = dest * classes + kind.astype(jnp.int32)
    kind = jnp.where(row_id < count_ref[0], kind, kinds)
    ratio = gauss_ref[...].astype(F32) * (1.0 / GBINS)
    weight = jnp.exp(-3.0 * ratio * ratio)
    meta = jnp.concatenate([lat, lon, weight, jnp.zeros((nfeat - 2 - KCELL, nrows), F32)], axis=0)
    ext_ref[:, :nfeat] = feat_ref[...]
    ext_ref[:, nfeat:] = meta.T.astype(BF)
    hot_ref[...] = (lax.broadcasted_iota(jnp.int32, (kinds, nrows), 0) == kind).astype(F32).astype(BF)
    counts = dot(hot_ref[...], jnp.ones((nrows, nfeat), BF))
    ka = lax.broadcasted_iota(jnp.int32, (kinds, kinds), 0)
    kb = lax.broadcasted_iota(jnp.int32, (kinds, kinds), 1)
    da, db = ka // classes, kb // classes
    within = ((da == db) & (kb < ka)).astype(F32).astype(BF)
    together = (da == db).astype(F32).astype(BF)
    ahead = ((db < da) & (kb % classes == 0)).astype(F32).astype(BF)
    loads = dot(together, counts.astype(BF))
    padded = jnp.floor((loads + 7.0) * 0.125) * 8.0
    begins = dot(ahead, padded.astype(BF))
    mine = begins + dot(within, counts.astype(BF))
    kind_id = lax.broadcasted_iota(jnp.int32, (kinds, nfeat), 0)
    lane_id = lax.broadcasted_iota(jnp.int32, (kinds, nfeat), 1)
    lead = kind_id == lane_id * classes
    place_ref[0:1, :] = jnp.sum(jnp.where(lead, begins, 0.0), axis=0, keepdims=True).astype(jnp.int32)
    place_ref[1:2, :] = jnp.sum(jnp.where(lead, loads, 0.0), axis=0, keepdims=True).astype(jnp.int32)
    copy = pltpu.make_async_copy(place_ref, place_smem, sem)
    copy.start()
    earlier = (
        lax.broadcasted_iota(jnp.int32, (step, step), 0) < lax.broadcasted_iota(jnp.int32, (step, step), 1)
    ).astype(F32).astype(BF)
    carry = mine[:, 0:1]
    places = []
    for begin in range(0, nrows, step):
        hot = hot_ref[:, begin : begin + step]
        before = dot(hot, earlier) + carry
        hot = hot.astype(F32)
        places.append(
            jnp.sum(before * hot, axis=0, keepdims=True) + jnp.sum(hot, axis=0, keepdims=True) - 1.0
        )
        carry = carry + jnp.sum(hot, axis=1, keepdims=True)
    place = jnp.concatenate(places, axis=1)
    live = row_id < count_ref[0]
    place = jnp.where(live, place, -1.0)
    slot = lax.broadcasted_iota(jnp.int32, (step, nrows), 0).astype(F32)
    span = sorted_ref.shape[0]
    for k in range(-(-(nrows + 8 * devices) // step)):
        pick = (slot == place - k * step).astype(F32).astype(BF)
        sorted_ref[k * step : (k + 1) * step, :] = dot(pick, ext_ref[...])
    tail = -(-(nrows + 8 * devices) // step) * step
    sorted_ref[tail:span, :] = jnp.zeros((span - tail, 2 * nfeat), F32)
    copy.wait()
    side_lane = lax.broadcasted_iota(jnp.int32, (META, nfeat), 1)

    def one(d, _):
        begin = pl.multiple_of(place_smem[0, d], 8)
        got = sorted_ref[pl.ds(begin, cap), :]
        send_ref[d, 0:cap, :] = got[:, :nfeat].astype(BF)
        side = got[:, nfeat:]
        if cap < nfeat:
            side = jnp.concatenate([side, jnp.zeros((nfeat - cap, nfeat), F32)], axis=0)
        side = jnp.where(side_lane < place_smem[1, d], side.T[0:META], 0.0)
        send_ref[d, cap : cap + META, :] = side.astype(BF)
        return 0

    lax.fori_loop(0, devices, one, 0, unroll=4)


def pack(count, dest, cells, gauss, feats, devices, cap, cols, bands):
    nrows, nfeat = feats.shape
    span = -(-(nrows + 8 * devices) // 256) * 256 + cap
    kinds = devices * 2 * bands
    return pl.pallas_call(
        functools.partial(pack_kernel, devices, cap, cols, bands),
        out_shape=jax.ShapeDtypeStruct((devices, cap + META, nfeat), BF),
        in_specs=[pl.BlockSpec(memory_space=pltpu.SMEM)] + [pl.BlockSpec(memory_space=pltpu.VMEM)] * 4,
        out_specs=pl.BlockSpec(memory_space=pltpu.VMEM),
        scratch_shapes=[
            pltpu.VMEM((nrows, 2 * nfeat), BF),
            pltpu.VMEM((kinds, nrows), BF),
            pltpu.VMEM((span, 2 * nfeat), F32),
            pltpu.VMEM((8, nfeat), jnp.int32),
            pltpu.SMEM((8, nfeat), jnp.int32),
            pltpu.SemaphoreType.DMA,
        ],
        compiler_params=params(56),
    )(count, dest, cells, gauss, feats)


def back_kernel(wide, back_ref, w_bg_ref, out_ref, scr):
    rows, cols, chans = back_ref.shape
    for i in range(rows):
        scr[i * wide : i * wide + cols, :] = back_ref[i]
    out_ref[...] = pltpu.roll(dot(scr[...], w_bg_ref[...]), 2, axis=0)


def projected(background, w_bg, wide):
    lat_rows, cols, chans = background.shape
    length = max(lat_rows * wide, 1 << 16) + 16
    return pl.pallas_call(
        functools.partial(back_kernel, wide),
        grid=(lat_rows // BAND,),
        out_shape=pltpu.HBM((length, chans), F32),
        in_specs=[
            pl.BlockSpec((BAND, cols, chans), lambda g: (g, 0, 0)),
            pl.BlockSpec(memory_space=pltpu.VMEM),
        ],
        out_specs=pl.BlockSpec((BAND * wide, chans), lambda g: (g, 0)),
        scratch_shapes=[pltpu.VMEM((BAND * wide, chans), BF)],
        compiler_params=params(24),
    )(background, w_bg)


def grid_kernel(
    devices, cap, wide, cols, lat_bands, recv_ref, back_hbm, w_in_hbm, w_dens_hbm,
    first_ref, west_ref, east_ref, inner_ref, outer_ref,
    rows_ref, lats_ref, feat_ref, meta_ref, acc_ref, edge_scr, ends_ref, ends_smem, sem,
    back_ref, w_in_ref, w_dens_ref, sems,
):
    band = pl.program_id(0)
    bands = pl.num_programs(0)
    nfeat = recv_ref.shape[2]
    lat_rows, _, chans = first_ref.shape
    rows = lat_rows // lat_bands
    slots = devices * cap
    span = rows * wide
    fetch = pltpu.make_async_copy(
        back_hbm.at[pl.ds(pl.multiple_of(band * span, 16), span), :], back_ref, sems.at[0]
    )
    fetch.start()
    loads = [
        pltpu.make_async_copy(w_in_hbm, w_in_ref, sems.at[1]),
        pltpu.make_async_copy(w_dens_hbm, w_dens_ref, sems.at[2]),
    ]

    @pl.when(band == 0)
    def _():
        for load in loads:
            load.start()
        feat_ref[...] = jnp.zeros(feat_ref.shape, F32)
        rows_ref[slots:, :] = jnp.zeros((rows_ref.shape[0] - slots, nfeat), F32)

        def widen(s, _):
            rows_ref[pl.ds(pl.multiple_of(s * cap, cap), cap), :] = recv_ref[s, 0:cap, :].astype(F32)
            side = recv_ref[s, cap : cap + META, :].astype(F32)
            lats_ref[pl.ds(s, 1), :] = jnp.where(side[2:3] > 0, side[0:1], 1e6)
            return 0

        lax.fori_loop(0, devices, widen, 0, unroll=4)
        lats = lats_ref[...]
        lane = lax.broadcasted_iota(jnp.int32, (devices, nfeat), 1)
        ends = jnp.zeros((devices, nfeat), F32)
        for b in range(lat_bands):
            low = jnp.sum((lats < b * rows - 1.0).astype(F32), axis=1, keepdims=True)
            high = jnp.sum((lats < (b + 1.0) * rows).astype(F32), axis=1, keepdims=True)
            ends = jnp.where(lane == 2 * b, low, jnp.where(lane == 2 * b + 1, high, ends))
        ends_ref[...] = ends.astype(jnp.int32)
        copy = pltpu.make_async_copy(ends_ref, ends_smem, sem)
        copy.start()
        copy.wait()

    meta_ref[...] = jnp.zeros(meta_ref.shape, F32)
    lane = lax.broadcasted_iota(jnp.int32, (8, nfeat), 1)

    def compact(s, out):
        out = pl.multiple_of(out, 8)
        low, high = ends_smem[s, 2 * band], ends_smem[s, 2 * band + 1]
        source = pl.multiple_of(low // 8 * 8, 8)
        feat_ref[pl.ds(out, cap), :] = rows_ref[pl.ds(pl.multiple_of(s * cap + source, 8), cap), :]
        side = recv_ref[s, cap : cap + META, :].astype(F32)[0:8]
        side = jnp.where((lane >= low) & (lane < high), side, 0.0)
        shift = out - source + nfeat
        tile, shift = shift // nfeat, shift % nfeat
        moved = pltpu.roll(side, shift, axis=1)
        meta_ref[tile] += jnp.where(lane >= shift, moved, 0.0)
        meta_ref[tile + 1] += jnp.where(lane < shift, moved, 0.0)
        return out + (high - source + 7) // 8 * 8

    total = lax.fori_loop(0, devices, compact, 0, unroll=4)
    acc_ref[...] = jnp.zeros(acc_ref.shape, F32)
    col_id = lax.broadcasted_iota(jnp.int32, (wide, CHUNK), 0).astype(F32)

    def chunk(k, _):
        side = jnp.concatenate(
            [meta_ref[1 + k * (CHUNK // nfeat) + q] for q in range(CHUNK // nfeat)], axis=1
        )
        lat, lon = side[0:1], side[1:2]
        here = (col_id == lon + 2.0).astype(F32).astype(BF)
        after = (col_id == lon + 3.0).astype(F32).astype(BF)
        parts = []
        for i in range(rows):
            row = (band * rows + i).astype(F32)
            same, above = lat == row, lat == row - 1.0
            left = jnp.where(same, side[2:3], jnp.where(above, side[4:5], 0.0)).astype(BF)
            right = jnp.where(same, side[3:4], jnp.where(above, side[5:6], 0.0)).astype(BF)
            parts.append(here * left + after * right)
        spread = jnp.concatenate(parts, axis=0)
        begin = pl.multiple_of(k * CHUNK, CHUNK)
        values = jnp.concatenate(
            [feat_ref[pl.ds(begin, CHUNK), :].astype(BF), jnp.ones((CHUNK, nfeat), BF)], axis=1
        )
        acc_ref[...] += dot(spread, values)
        return 0

    lax.fori_loop(0, (total + CHUNK - 1) // CHUNK, chunk, 0)
    fetch.wait()

    @pl.when(band == 0)
    def _():
        for load in loads:
            load.wait()

    for g in range(0, rows, GROUP):
        sums = acc_ref[g * wide : (g + GROUP) * wide, :]
        start = back_ref[g * wide : (g + GROUP) * wide, :]
        density = sums[:, nfeat:]
        normalized = (sums[:, :nfeat] / (density + 1.0)).astype(BF)
        start = start + dot(normalized, w_in_ref[...])
        start = start + jnp.concatenate([density] * (chans // nfeat), axis=1) * w_dens_ref[...]
        first = start.astype(BF)
        for i in range(GROUP):
            first_ref[band * rows + g + i] = first[i * wide : (i + 1) * wide]
            for k, col in enumerate((2, 3, cols, cols + 1)):
                edge_scr[k, pl.ds(band * rows + g + i, 1), :] = start[i * wide + col : i * wide + col + 1]

    @pl.when(band == bands - 1)
    def _():
        west_ref[...] = edge_scr[0:2].astype(BF)
        east_ref[...] = edge_scr[2:4].astype(BF)
        even = lax.axis_index("lat") % 2 == 0
        for k in range(2):
            top, bottom = first_ref[k].astype(F32), first_ref[lat_rows - 1 - k].astype(F32)
            inner = jnp.where(even, bottom, top).astype(BF)
            outer = jnp.where(even, top, bottom).astype(BF)
            inner_ref[k] = inner
            outer_ref[k] = outer


def gridded(recv, back, w_in, w_dens, cap, wide, lat_rows, cols):
    devices, _, nfeat = recv.shape
    chans = back.shape[1]
    slots = devices * cap
    tall = -(-lat_rows // 16) * 16
    whole = pl.BlockSpec(memory_space=pltpu.VMEM)
    return pl.pallas_call(
        functools.partial(grid_kernel, devices, cap, wide, cols, lat_rows // BAND),
        grid=(lat_rows // BAND,),
        out_shape=(
            jax.ShapeDtypeStruct((lat_rows, wide, chans), BF),
            jax.ShapeDtypeStruct((2, tall, chans), BF),
            jax.ShapeDtypeStruct((2, tall, chans), BF),
            jax.ShapeDtypeStruct((2, wide, chans), BF),
            jax.ShapeDtypeStruct((2, wide, chans), BF),
        ),
        in_specs=[whole] + [pl.BlockSpec(memory_space=pltpu.HBM)] * 3,
        out_specs=(whole,) * 5,
        scratch_shapes=[
            pltpu.VMEM((slots + cap, nfeat), F32),
            pltpu.VMEM((devices, nfeat), F32),
            pltpu.VMEM((slots + cap + CHUNK, nfeat), F32),
            pltpu.VMEM((slots // nfeat + 6, 8, nfeat), F32),
            pltpu.VMEM((BAND * wide, 2 * nfeat), F32),
            pltpu.VMEM((4, tall, chans), F32),
            pltpu.VMEM((devices, nfeat), jnp.int32),
            pltpu.SMEM((devices, nfeat), jnp.int32),
            pltpu.SemaphoreType.DMA,
            pltpu.VMEM((BAND * wide, chans), F32),
            pltpu.VMEM(w_in.shape, BF),
            pltpu.VMEM(w_dens.shape, F32),
            pltpu.SemaphoreType.DMA((3,)),
        ],
        compiler_params=params(32),
    )(recv, back, w_in, w_dens)


def put(ref, begin, value):
    size, chans = value.shape
    for b in range(3):
        part = value if b == 0 else pltpu.roll(value, size - b, axis=0)
        ref[pl.ds(begin, size), b * chans : (b + 1) * chans] = part.astype(BF)


def taps(ref, begin, size, wide, w_ref):
    field = jnp.concatenate([ref[pl.ds(begin + a * wide, size), :] for a in range(3)], axis=1)
    return dot(field, w_ref[...].reshape(field.shape[1], w_ref.shape[2]))


def border_kernel(lat_rows, cols, inner_ref, outer_ref, west_ref, east_ref, inner_out, outer_out):
    _, wide, chans = inner_ref.shape
    even = lax.axis_index("lat") % 2 == 0
    row_id = lax.broadcasted_iota(jnp.int32, (wide, chans), 0)
    sides = [west_ref[0], west_ref[1], east_ref[0], east_ref[1]]
    sides = [side.astype(F32) for side in sides]
    for k in range(2):
        inner, outer = inner_ref[k].astype(F32), outer_ref[k].astype(F32)
        for side, col in zip(sides, (0, 1, cols + 2, cols + 3)):
            top = side[k : k + 1]
            bottom = side[lat_rows - 1 - k : lat_rows - k]
            inner = jnp.where(row_id == col, jnp.where(even, bottom, top), inner)
            outer = jnp.where(row_id == col, jnp.where(even, top, bottom), outer)
        inner_out[k] = inner.astype(BF)
        outer_out[k] = outer.astype(BF)


def bordered(inner, outer, west, east, lat_rows, cols):
    whole = pl.BlockSpec(memory_space=pltpu.VMEM)
    shape = jax.ShapeDtypeStruct(inner.shape, BF)
    return pl.pallas_call(
        functools.partial(border_kernel, lat_rows, cols),
        out_shape=(shape, shape),
        in_specs=[whole] * 4,
        out_specs=(whole, whole),
        compiler_params=params(24),
    )(inner, outer, west, east)


def inside_kernel(split, first_ref, one_ref, after_ref, hid_ref, field):
    lat_rows, wide, chans = first_ref.shape

    def load(r, _):
        put(field, pl.multiple_of(r * wide, 16), first_ref[r].astype(F32))
        return 0

    lax.fori_loop(0, lat_rows, load, 0, unroll=6)
    size = (lat_rows - 2) // split * wide

    def hidden(g, _):
        begin = pl.multiple_of(g * size, 16)
        total = taps(field, begin, size, wide, one_ref)
        put(hid_ref, pl.multiple_of(begin + 2 * wide, 16), jax.nn.gelu(total))
        return 0

    lax.fori_loop(0, split, hidden, 0)


def inside(first, one, after):
    lat_rows, wide, chans = first.shape
    whole = pl.BlockSpec(memory_space=pltpu.VMEM)
    split = next(n for n in (4, 2, 1) if (lat_rows - 2) % n == 0)
    return pl.pallas_call(
        functools.partial(inside_kernel, split),
        out_shape=jax.ShapeDtypeStruct(((lat_rows + 2) * wide, 3 * chans), BF),
        in_specs=[whole, whole, pl.BlockSpec(memory_space=pl.ANY)],
        out_specs=whole,
        scratch_shapes=[pltpu.VMEM((lat_rows * wide, 3 * chans), BF)],
        compiler_params=params(30),
    )(first, one, after)


def finish_kernel(
    lat_count, hid_in, first_ref, own_west, own_east, west_ref, east_ref, inner_ref, outer_ref,
    one_ref, two_ref, out_ref, hid_ref, rim, cols_scr,
):
    group = pl.program_id(0)
    lat_rows, wide, chans = first_ref.shape
    rows, cols, _ = out_ref.shape
    block = rows * wide

    @pl.when(group == 0)
    def _():
        lat_index = lax.axis_index("lat")
        even = lat_index % 2 == 0
        row_id = lax.broadcasted_iota(jnp.int32, (wide, chans), 0)
        short_id = lax.broadcasted_iota(jnp.int32, (16, chans), 0)

        def edge_row(north, k):
            return jnp.where(even == north, outer_ref[k].astype(F32), inner_ref[k].astype(F32))

        def own_row(r):
            value = first_ref[r].astype(F32)
            sides = [west_ref[0], west_ref[1], east_ref[0], east_ref[1]]
            for side, col in zip(sides, (0, 1, cols + 2, cols + 3)):
                value = jnp.where(row_id == col, side.astype(F32)[r : r + 1], value)
            return value

        lines = [edge_row(True, 1), edge_row(True, 0), own_row(0), own_row(1)]
        lines += [own_row(lat_rows - 2), own_row(lat_rows - 1), edge_row(False, 0), edge_row(False, 1)]
        for n, line in enumerate(lines):
            put(rim, n * wide, line)
        for begin, index, pole in ((0, 0, lat_index == 0), (5, lat_rows + 1, lat_index == lat_count - 1)):
            total = jnp.zeros((wide, chans), F32)
            for a in range(3):
                tap = jnp.where(pole, 2 - a, a)
                total = total + dot(rim[(begin + a) * wide : (begin + a + 1) * wide, :], one_ref[tap])
            put(hid_ref, index * wide, jax.nn.gelu(total))
        total = jnp.zeros((2 * wide, chans), F32)
        for a in range(3):
            pair = [rim[(n + a) * wide : (n + a + 1) * wide, :] for n in (1, 4)]
            total = total + dot(jnp.concatenate(pair, axis=0), one_ref[a])
        total = jax.nn.gelu(total)
        put(hid_ref, wide, total[:wide])
        put(hid_ref, lat_rows * wide, total[wide:])

        lines = [west_ref[0], west_ref[1], own_west[0], own_west[1]]
        lines += [own_east[0], own_east[1], east_ref[0], east_ref[1]]
        windows = [jnp.concatenate(lines[n : n + 3], axis=1) for n in (0, 1, 4, 5)]
        windows = jnp.concatenate(windows, axis=0)
        size = windows.shape[0]
        total = pltpu.roll(dot(windows, one_ref[0]), 1, axis=0) + dot(windows, one_ref[1])
        total = total + pltpu.roll(dot(windows, one_ref[2]), size - 1, axis=0)
        total = jax.nn.gelu(total)
        tall = size // 4
        for n in range(4):
            cols_scr[n] = total[n * tall : (n + 1) * tall]
        last = wide - 16

        def patch(r, _):
            fixes = [cols_scr[n, pl.ds(r, 1), :] for n in range(4)]
            begin = pl.multiple_of((r + 1) * wide, 16)
            for b in range(3):
                lanes = slice(b * chans, (b + 1) * chans)
                for start in (0, last):
                    edits = [
                        (col - b - start, fix)
                        for col, fix in zip((0, 1, cols, cols + 1), fixes)
                        if 0 <= col - b - start < 16
                    ]
                    if edits:
                        value = hid_ref[pl.ds(begin + start, 16), lanes].astype(F32)
                        for at, fix in edits:
                            value = jnp.where(short_id == at, fix, value)
                        hid_ref[pl.ds(begin + start, 16), lanes] = value.astype(BF)
            return 0

        lax.fori_loop(1, lat_rows - 1, patch, 0, unroll=8)

    begin = pl.multiple_of(group * block, 16)
    total = taps(hid_ref, begin, block, wide, two_ref)
    own = first_ref[pl.ds(group * rows, rows)].reshape(block, chans).astype(F32)
    total = total + pltpu.roll(own, block - 2, axis=0)
    result = total.astype(BF)
    for i in range(rows):
        out_ref[i] = result[i * wide : i * wide + cols]


def finished(hid, first, sides, one, two, cols, lat_count):
    lat_rows, wide, chans = first.shape
    whole = pl.BlockSpec(memory_space=pltpu.VMEM)
    out, _ = pl.pallas_call(
        functools.partial(finish_kernel, lat_count),
        grid=(lat_rows // FINISH,),
        out_shape=(
            jax.ShapeDtypeStruct((lat_rows, cols, chans), BF),
            jax.ShapeDtypeStruct(hid.shape, BF),
        ),
        in_specs=[whole] * (4 + len(sides)),
        out_specs=(pl.BlockSpec((FINISH, cols, chans), lambda g: (g, 0, 0)), whole),
        input_output_aliases={0: 1},
        scratch_shapes=[
            pltpu.VMEM((8 * wide, 3 * chans), BF),
            pltpu.VMEM((4, sides[0].shape[1], chans), F32),
        ],
        compiler_params=params(26),
    )(hid, first, *sides, one, two)
    return out


def row_pairs(lat_count, lon_count):
    half = lon_count // 2

    def flat(lat, lon):
        return lat * lon_count + lon % lon_count

    inner, outer = [], []
    for lon in range(lon_count):
        for lat in range(0, lat_count, 2):
            inner += [(flat(lat, lon), flat(lat + 1, lon)), (flat(lat + 1, lon), flat(lat, lon))]
        for lat in range(1, lat_count - 1, 2):
            outer += [(flat(lat, lon), flat(lat + 1, lon)), (flat(lat + 1, lon), flat(lat, lon))]
        outer += [(flat(lat, lon), flat(lat, lon + half)) for lat in (0, lat_count - 1)]
    return inner, outer


def shards(
    obs_features,
    obs_dest,
    obs_cells,
    obs_gauss,
    row_counts,
    background,
    w_in,
    w_bg,
    w_dens,
    conv_one,
    conv_two,
):
    nrows, nfeat = obs_features.shape
    lat_rows, cols, chans = background.shape
    axes = ("lat", "lon")
    devices = lax.axis_size(axes)
    lat_count, lon_count = lax.axis_size("lat"), lax.axis_size("lon")
    cap = 2 * nrows // devices
    wide = -(-(cols + 4) // 16) * 16
    send = pack(
        row_counts, obs_dest.reshape(1, nrows), obs_cells.T, obs_gauss.T, obs_features, devices, cap, cols,
        lat_rows // BAND,
    )
    recv = lax.all_to_all(send, axes, split_axis=0, concat_axis=0, tiled=True)
    back = projected(background, w_bg, wide)
    first, own_west, own_east, inner_row, outer_row = gridded(
        recv, back, w_in, w_dens.reshape(1, chans), cap, wide, lat_rows, cols
    )
    west = lax.ppermute(own_east, "lon", [(i, (i + 1) % lon_count) for i in range(lon_count)])
    east = lax.ppermute(own_west, "lon", [((i + 1) % lon_count, i) for i in range(lon_count)])
    one = conv_one.reshape(3, 3 * chans, chans)
    two = conv_two.reshape(3, 3 * chans, chans)
    inner_row, outer_row = bordered(inner_row, outer_row, west, east, lat_rows, cols)
    inner, outer = row_pairs(lat_count, lon_count)
    hid = inside(first, one, inner_row)
    inner_row = lax.ppermute(inner_row, axes, inner)
    outer_row = lax.ppermute(outer_row, axes, outer)
    sides = (own_west, own_east, west, east, inner_row, outer_row)
    return finished(hid, first, sides, one, two, cols, lat_count)


def solution(mesh):
    rows = P(("lat", "lon"), None)
    in_specs = (rows, rows, rows, rows, P(("lat", "lon")), P("lat", "lon", None), P(), P(), P(), P(), P())
    return jax.shard_map(
        shards, mesh=mesh, in_specs=in_specs, out_specs=P("lat", "lon", None), check_vma=False
    )
```

```python
import functools

import jax
import jax.numpy as jnp
from jax import lax
from jax.experimental import pallas as pl
from jax.experimental.pallas import tpu as pltpu
from jax.sharding import PartitionSpec as P

KCELL = 4
GBINS = 32
META = 8
GROUP = 6
BAND = 18
CHUNK = 256
HEAD = 768
FINISH = 15
BF = jnp.bfloat16
F32 = jnp.float32


def params(mib):
    return pltpu.CompilerParams(vmem_limit_bytes=mib * 1024 * 1024)


def gelu(x):
    scale = 0.7978845608028654
    half = 0.5 * x
    return half + half * jnp.tanh(x * (scale + (scale * 0.044715) * (x * x)))


def dot(a, b):
    return jnp.dot(a, b, preferred_element_type=F32)


def pack_kernel(
    devices, lon_count, cap, cols, bands, count_ref, dest_ref, cells_ref, gauss_ref, feat_ref, send_ref,
    ext_ref, hot_ref, sorted_ref, place_ref, place_smem, sem,
):
    nrows, nfeat = feat_ref.shape
    step = 256
    classes = 2 * bands
    kinds = devices * classes
    dest = dest_ref[...]
    row_id = lax.broadcasted_iota(jnp.int32, (1, nrows), 1)
    base = cells_ref[0:1, :].astype(F32)
    lat = jnp.floor((base + 0.5) * (1.0 / cols))
    lon = base - lat * cols
    band = jnp.floor((lat + 0.5) * (1.0 / BAND))
    kind = 2.0 * band + (lat == band * BAND + (BAND - 1)).astype(F32)
    kind = dest * classes + kind.astype(jnp.int32)
    kind = jnp.where(row_id < count_ref[0], kind, kinds)
    ratio = gauss_ref[...].astype(F32) * (1.0 / GBINS)
    weight = jnp.exp(-3.0 * ratio * ratio)
    meta = jnp.concatenate([lat, lon, weight, jnp.zeros((nfeat - 2 - KCELL, nrows), F32)], axis=0)
    ext_ref[:, :nfeat] = feat_ref[...]
    ext_ref[:, nfeat:] = meta.T.astype(BF)
    hot_ref[...] = (lax.broadcasted_iota(jnp.int32, (kinds, nrows), 0) == kind).astype(F32).astype(BF)
    counts = dot(hot_ref[...], jnp.ones((nrows, nfeat), BF))
    ka = lax.broadcasted_iota(jnp.int32, (kinds, kinds), 0)
    kb = lax.broadcasted_iota(jnp.int32, (kinds, kinds), 1)
    da, db = ka // classes, kb // classes
    within = ((da == db) & (kb < ka)).astype(F32).astype(BF)
    together = (da == db).astype(F32).astype(BF)
    ahead = ((db < da) & (kb % classes == 0)).astype(F32).astype(BF)
    loads = dot(together, counts.astype(BF))
    padded = jnp.floor((loads + 7.0) * 0.125) * 8.0
    begins = dot(ahead, padded.astype(BF))
    mine = begins + dot(within, counts.astype(BF))
    kind_id = lax.broadcasted_iota(jnp.int32, (kinds, nfeat), 0)
    lane_id = lax.broadcasted_iota(jnp.int32, (kinds, nfeat), 1)
    lead = kind_id == lane_id * classes
    place_ref[0:1, :] = jnp.sum(jnp.where(lead, begins, 0.0), axis=0, keepdims=True).astype(jnp.int32)
    place_ref[1:2, :] = jnp.sum(jnp.where(lead, loads, 0.0), axis=0, keepdims=True).astype(jnp.int32)
    copy = pltpu.make_async_copy(place_ref, place_smem, sem)
    copy.start()
    earlier = (
        lax.broadcasted_iota(jnp.int32, (step, step), 0) < lax.broadcasted_iota(jnp.int32, (step, step), 1)
    ).astype(F32).astype(BF)
    carry = mine[:, 0:1]
    places = []
    for begin in range(0, nrows, step):
        hot = hot_ref[:, begin : begin + step]
        before = dot(hot, earlier) + carry
        hot = hot.astype(F32)
        places.append(
            jnp.sum(before * hot, axis=0, keepdims=True) + jnp.sum(hot, axis=0, keepdims=True) - 1.0
        )
        carry = carry + jnp.sum(hot, axis=1, keepdims=True)
    place = jnp.concatenate(places, axis=1)
    live = row_id < count_ref[0]
    place = jnp.where(live, place, -1.0)
    slot = lax.broadcasted_iota(jnp.int32, (step, nrows), 0).astype(F32)
    span = sorted_ref.shape[0]
    for k in range(-(-(nrows + 8 * devices) // step)):
        pick = (slot == place - k * step).astype(F32).astype(BF)
        sorted_ref[k * step : (k + 1) * step, :] = dot(pick, ext_ref[...])
    tail = -(-(nrows + 8 * devices) // step) * step
    sorted_ref[tail:span, :] = jnp.zeros((span - tail, 2 * nfeat), F32)
    copy.wait()
    side_lane = lax.broadcasted_iota(jnp.int32, (META, nfeat), 1)
    odd = (lax.axis_index("lat") * lon_count + lax.axis_index("lon")) % 2 == 1

    def one(d):
        begin = pl.multiple_of(place_smem[0, d], 8)
        got = sorted_ref[pl.ds(begin, cap), :]
        side = got[:, nfeat:]
        if cap < nfeat:
            side = jnp.concatenate([side, jnp.zeros((nfeat - cap, nfeat), F32)], axis=0)
        return got[:, :nfeat], jnp.where(side_lane < place_smem[1, d], side.T[0:META], 0.0)

    def pair(p, _):
        (rows_a, side_a), (rows_b, side_b) = one(2 * p), one(2 * p + 1)
        plain = jnp.concatenate([rows_a, side_a, rows_b, side_b], axis=0)
        turned = jnp.concatenate([side_a, rows_a, side_b, rows_b], axis=0)
        send_ref[p] = jnp.where(odd, turned, plain).astype(BF)
        return 0

    lax.fori_loop(0, devices // 2, pair, 0, unroll=2)


def pack(count, dest, cells, gauss, feats, devices, lon_count, cap, cols, bands):
    nrows, nfeat = feats.shape
    span = -(-(nrows + 8 * devices) // 256) * 256 + cap
    kinds = devices * 2 * bands
    return pl.pallas_call(
        functools.partial(pack_kernel, devices, lon_count, cap, cols, bands),
        out_shape=jax.ShapeDtypeStruct((devices // 2, 2 * (cap + META), nfeat), BF),
        in_specs=[pl.BlockSpec(memory_space=pltpu.SMEM)] + [pl.BlockSpec(memory_space=pltpu.VMEM)] * 4,
        out_specs=pl.BlockSpec(memory_space=pltpu.VMEM),
        scratch_shapes=[
            pltpu.VMEM((nrows, 2 * nfeat), BF),
            pltpu.VMEM((kinds, nrows), BF),
            pltpu.VMEM((span, 2 * nfeat), F32),
            pltpu.VMEM((8, nfeat), jnp.int32),
            pltpu.SMEM((8, nfeat), jnp.int32),
            pltpu.SemaphoreType.DMA,
        ],
        compiler_params=params(56),
    )(count, dest, cells, gauss, feats)


def back_kernel(wide, back_ref, w_bg_ref, out_ref, scr):
    rows, cols, chans = back_ref.shape
    for i in range(rows):
        scr[i * wide : i * wide + cols, :] = back_ref[i]
    out_ref[...] = pltpu.roll(dot(scr[...], w_bg_ref[...]), 2, axis=0)


def projected(background, w_bg, wide):
    lat_rows, cols, chans = background.shape
    length = max(lat_rows * wide, 1 << 16) + 16
    return pl.pallas_call(
        functools.partial(back_kernel, wide),
        grid=(lat_rows // BAND,),
        out_shape=pltpu.HBM((length, chans), F32),
        in_specs=[
            pl.BlockSpec((BAND, cols, chans), lambda g: (g, 0, 0)),
            pl.BlockSpec(memory_space=pltpu.VMEM),
        ],
        out_specs=pl.BlockSpec((BAND * wide, chans), lambda g: (g, 0)),
        scratch_shapes=[pltpu.VMEM((BAND * wide, chans), BF)],
        compiler_params=params(24),
    )(background, w_bg)


def grid_kernel(
    devices, cap, wide, cols, lat_bands, recv_ref, back_hbm, w_in_hbm, w_dens_hbm,
    first_ref, west_ref, east_ref, inner_ref, outer_ref,
    rows_ref, sides_ref, lats_ref, feat_ref, meta_ref, acc_ref, edge_scr, ends_ref, ends_smem, sem,
    back_ref, w_in_ref, w_dens_ref, sems,
):
    band = pl.program_id(0)
    bands = pl.num_programs(0)
    nfeat = recv_ref.shape[2]
    lat_rows, _, chans = first_ref.shape
    rows = lat_rows // lat_bands
    slots = devices * cap
    span = rows * wide
    fetch = pltpu.make_async_copy(
        back_hbm.at[pl.ds(pl.multiple_of(band * span, 16), span), :], back_ref, sems.at[0]
    )
    fetch.start()
    loads = [
        pltpu.make_async_copy(w_in_hbm, w_in_ref, sems.at[1]),
        pltpu.make_async_copy(w_dens_hbm, w_dens_ref, sems.at[2]),
    ]

    @pl.when(band == 0)
    def _():
        for load in loads:
            load.start()

        def read(p, _):
            both = recv_ref[p, cap : cap + 2 * META, :].astype(F32)
            for s, side in ((2 * p, both[:META]), (2 * p + 1, both[META:])):
                sides_ref[s] = side
                lats_ref[pl.ds(s, 1), :] = jnp.where(side[2:3] > 0, side[0:1], 1e6)
            return 0

        lax.fori_loop(0, devices // 2, read, 0, unroll=8)
        lats = lats_ref[...]
        lane = lax.broadcasted_iota(jnp.int32, (devices, nfeat), 1)
        ends = jnp.zeros((devices, nfeat), F32)
        for b in range(lat_bands):
            low = jnp.sum((lats < b * rows - 1.0).astype(F32), axis=1, keepdims=True)
            high = jnp.sum((lats < (b + 1.0) * rows).astype(F32), axis=1, keepdims=True)
            ends = jnp.where(lane == 2 * b, low, jnp.where(lane == 2 * b + 1, high, ends))
        ends_ref[...] = ends.astype(jnp.int32)
        copy = pltpu.make_async_copy(ends_ref, ends_smem, sem)
        copy.start()
        feat_ref[...] = jnp.zeros(feat_ref.shape, F32)
        rows_ref[slots:, :] = jnp.zeros((rows_ref.shape[0] - slots, nfeat), F32)

        def widen(p, _):
            begin = pl.multiple_of(2 * p * cap, cap)
            rows_ref[pl.ds(begin, cap), :] = recv_ref[p, 0:cap, :].astype(F32)
            rows_ref[pl.ds(begin + cap, cap), :] = recv_ref[p, cap + 2 * META :, :].astype(F32)
            return 0

        lax.fori_loop(0, devices // 2, widen, 0, unroll=2)
        copy.wait()

    meta_ref[...] = jnp.zeros(meta_ref.shape, F32)
    lane = lax.broadcasted_iota(jnp.int32, (META, nfeat), 1)

    def compact(s, out):
        out = pl.multiple_of(out, 8)
        low, high = ends_smem[s, 2 * band], ends_smem[s, 2 * band + 1]
        source = pl.multiple_of(low // 8 * 8, 8)
        feat_ref[pl.ds(out, cap), :] = rows_ref[pl.ds(pl.multiple_of(s * cap + source, 8), cap), :]
        side = sides_ref[s]
        side = jnp.where((lane >= low) & (lane < high), side, 0.0)
        shift = out - source + nfeat
        tile, shift = shift // nfeat, shift % nfeat
        moved = pltpu.roll(side, shift, axis=1)
        meta_ref[tile] += jnp.where(lane >= shift, moved, 0.0)
        meta_ref[tile + 1] += jnp.where(lane < shift, moved, 0.0)
        return out + (high - source + 7) // 8 * 8

    total = lax.fori_loop(0, devices, compact, 0, unroll=16)

    def piece(begin, size):
        begin = pl.multiple_of(begin, CHUNK)
        col_id = lax.broadcasted_iota(jnp.int32, (wide, size), 0).astype(F32)
        side = jnp.concatenate([meta_ref[1 + begin // nfeat + q] for q in range(size // nfeat)], axis=1)
        lat, lon = side[0:1], side[1:2]
        here = (col_id == lon + 2.0).astype(F32).astype(BF)
        after = (col_id == lon + 3.0).astype(F32).astype(BF)
        parts = []
        for i in range(rows):
            row = (band * rows + i).astype(F32)
            same, above = lat == row, lat == row - 1.0
            left = jnp.where(same, side[2:3], jnp.where(above, side[4:5], 0.0)).astype(BF)
            right = jnp.where(same, side[3:4], jnp.where(above, side[5:6], 0.0)).astype(BF)
            parts.append(here * left + after * right)
        spread = jnp.concatenate(parts, axis=0)
        values = jnp.concatenate(
            [feat_ref[pl.ds(begin, size), :].astype(BF), jnp.ones((size, nfeat), BF)], axis=1
        )
        return dot(spread, values)

    def more(k, _):
        acc_ref[...] += piece(k * CHUNK, CHUNK)
        return 0

    acc_ref[...] = piece(0, HEAD)
    lax.fori_loop(HEAD // CHUNK, (total + CHUNK - 1) // CHUNK, more, 0)
    fetch.wait()

    @pl.when(band == 0)
    def _():
        for load in loads:
            load.wait()

    for g in range(0, rows, GROUP):
        sums = acc_ref[g * wide : (g + GROUP) * wide, :]
        start = back_ref[g * wide : (g + GROUP) * wide, :]
        density = sums[:, nfeat:]
        normalized = (sums[:, :nfeat] / (density + 1.0)).astype(BF)
        start = start + dot(normalized, w_in_ref[...])
        start = start + jnp.concatenate([density] * (chans // nfeat), axis=1) * w_dens_ref[...]
        first = start.astype(BF)
        for i in range(GROUP):
            first_ref[band * rows + g + i] = first[i * wide : (i + 1) * wide]
            for k, col in enumerate((2, 3, cols, cols + 1)):
                edge_scr[k, pl.ds(band * rows + g + i, 1), :] = start[i * wide + col : i * wide + col + 1]

    @pl.when(band == bands - 1)
    def _():
        west_ref[...] = edge_scr[0:2].astype(BF)
        east_ref[...] = edge_scr[2:4].astype(BF)
        even = lax.axis_index("lat") % 2 == 0
        for k in range(2):
            top, bottom = first_ref[k].astype(F32), first_ref[lat_rows - 1 - k].astype(F32)
            inner = jnp.where(even, bottom, top).astype(BF)
            outer = jnp.where(even, top, bottom).astype(BF)
            inner_ref[k] = inner
            outer_ref[k] = outer


def gridded(recv, back, w_in, w_dens, cap, wide, lat_rows, cols):
    devices, nfeat = 2 * recv.shape[0], recv.shape[2]
    chans = back.shape[1]
    slots = devices * cap
    tall = -(-lat_rows // 16) * 16
    whole = pl.BlockSpec(memory_space=pltpu.VMEM)
    return pl.pallas_call(
        functools.partial(grid_kernel, devices, cap, wide, cols, lat_rows // BAND),
        grid=(lat_rows // BAND,),
        out_shape=(
            jax.ShapeDtypeStruct((lat_rows, wide, chans), BF),
            jax.ShapeDtypeStruct((2, tall, chans), BF),
            jax.ShapeDtypeStruct((2, tall, chans), BF),
            jax.ShapeDtypeStruct((2, wide, chans), BF),
            jax.ShapeDtypeStruct((2, wide, chans), BF),
        ),
        in_specs=[whole] + [pl.BlockSpec(memory_space=pltpu.HBM)] * 3,
        out_specs=(whole,) * 5,
        scratch_shapes=[
            pltpu.VMEM((slots + cap, nfeat), F32),
            pltpu.VMEM((devices, META, nfeat), F32),
            pltpu.VMEM((devices, nfeat), F32),
            pltpu.VMEM((slots + cap + HEAD, nfeat), F32),
            pltpu.VMEM((slots // nfeat + 8, META, nfeat), F32),
            pltpu.VMEM((BAND * wide, 2 * nfeat), F32),
            pltpu.VMEM((4, tall, chans), F32),
            pltpu.VMEM((devices, nfeat), jnp.int32),
            pltpu.SMEM((devices, nfeat), jnp.int32),
            pltpu.SemaphoreType.DMA,
            pltpu.VMEM((BAND * wide, chans), F32),
            pltpu.VMEM(w_in.shape, BF),
            pltpu.VMEM(w_dens.shape, F32),
            pltpu.SemaphoreType.DMA((3,)),
        ],
        compiler_params=params(32),
    )(recv, back, w_in, w_dens)


def put(ref, begin, value):
    size, chans = value.shape
    for b in range(3):
        part = value if b == 0 else pltpu.roll(value, size - b, axis=0)
        ref[pl.ds(begin, size), b * chans : (b + 1) * chans] = part.astype(BF)


def taps(ref, begin, size, wide, w_ref):
    field = jnp.concatenate([ref[pl.ds(begin + a * wide, size), :] for a in range(3)], axis=1)
    return dot(field, w_ref[...].reshape(field.shape[1], w_ref.shape[2]))


def border_kernel(lat_rows, cols, inner_ref, outer_ref, west_ref, east_ref, inner_out, outer_out):
    _, wide, chans = inner_ref.shape
    even = lax.axis_index("lat") % 2 == 0
    row_id = lax.broadcasted_iota(jnp.int32, (wide, chans), 0)
    sides = [west_ref[0], west_ref[1], east_ref[0], east_ref[1]]
    sides = [side.astype(F32) for side in sides]
    for k in range(2):
        inner, outer = inner_ref[k].astype(F32), outer_ref[k].astype(F32)
        for side, col in zip(sides, (0, 1, cols + 2, cols + 3)):
            top = side[k : k + 1]
            bottom = side[lat_rows - 1 - k : lat_rows - k]
            inner = jnp.where(row_id == col, jnp.where(even, bottom, top), inner)
            outer = jnp.where(row_id == col, jnp.where(even, top, bottom), outer)
        inner_out[k] = inner.astype(BF)
        outer_out[k] = outer.astype(BF)


def bordered(inner, outer, west, east, lat_rows, cols):
    whole = pl.BlockSpec(memory_space=pltpu.VMEM)
    shape = jax.ShapeDtypeStruct(inner.shape, BF)
    return pl.pallas_call(
        functools.partial(border_kernel, lat_rows, cols),
        out_shape=(shape, shape),
        in_specs=[whole] * 4,
        out_specs=(whole, whole),
        compiler_params=params(24),
    )(inner, outer, west, east)


def inside_kernel(split, first_ref, one_ref, after_ref, hid_ref, field):
    lat_rows, wide, chans = first_ref.shape

    def load(r, _):
        put(field, pl.multiple_of(r * wide, 16), first_ref[r].astype(F32))
        return 0

    lax.fori_loop(0, lat_rows, load, 0, unroll=6)
    size = (lat_rows - 2) // split * wide

    def hidden(g, _):
        begin = pl.multiple_of(g * size, 16)
        total = taps(field, begin, size, wide, one_ref)
        put(hid_ref, pl.multiple_of(begin + 2 * wide, 16), gelu(total))
        return 0

    lax.fori_loop(0, split, hidden, 0)


def inside(first, one, after):
    lat_rows, wide, chans = first.shape
    whole = pl.BlockSpec(memory_space=pltpu.VMEM)
    split = next(n for n in (4, 2, 1) if (lat_rows - 2) % n == 0)
    return pl.pallas_call(
        functools.partial(inside_kernel, split),
        out_shape=jax.ShapeDtypeStruct(((lat_rows + 2) * wide, 3 * chans), BF),
        in_specs=[whole, whole, pl.BlockSpec(memory_space=pl.ANY)],
        out_specs=whole,
        scratch_shapes=[pltpu.VMEM((lat_rows * wide, 3 * chans), BF)],
        compiler_params=params(30),
    )(first, one, after)


def finish_kernel(
    lat_count, hid_in, first_ref, own_west, own_east, west_ref, east_ref, inner_ref, outer_ref,
    one_ref, two_ref, out_ref, hid_ref, rim, cols_scr,
):
    group = pl.program_id(0)
    lat_rows, wide, chans = first_ref.shape
    rows, cols, _ = out_ref.shape
    block = rows * wide

    @pl.when(group == 0)
    def _():
        lat_index = lax.axis_index("lat")
        even = lat_index % 2 == 0
        row_id = lax.broadcasted_iota(jnp.int32, (wide, chans), 0)
        short_id = lax.broadcasted_iota(jnp.int32, (16, chans), 0)

        def edge_row(north, k):
            return jnp.where(even == north, outer_ref[k].astype(F32), inner_ref[k].astype(F32))

        def own_row(r):
            value = first_ref[r].astype(F32)
            sides = [west_ref[0], west_ref[1], east_ref[0], east_ref[1]]
            for side, col in zip(sides, (0, 1, cols + 2, cols + 3)):
                value = jnp.where(row_id == col, side.astype(F32)[r : r + 1], value)
            return value

        lines = [edge_row(True, 1), edge_row(True, 0), own_row(0), own_row(1)]
        lines += [own_row(lat_rows - 2), own_row(lat_rows - 1), edge_row(False, 0), edge_row(False, 1)]
        for n, line in enumerate(lines):
            put(rim, n * wide, line)
        for begin, index, pole in ((0, 0, lat_index == 0), (5, lat_rows + 1, lat_index == lat_count - 1)):
            total = jnp.zeros((wide, chans), F32)
            for a in range(3):
                tap = jnp.where(pole, 2 - a, a)
                total = total + dot(rim[(begin + a) * wide : (begin + a + 1) * wide, :], one_ref[tap])
            put(hid_ref, index * wide, gelu(total))
        total = jnp.zeros((2 * wide, chans), F32)
        for a in range(3):
            pair = [rim[(n + a) * wide : (n + a + 1) * wide, :] for n in (1, 4)]
            total = total + dot(jnp.concatenate(pair, axis=0), one_ref[a])
        total = gelu(total)
        put(hid_ref, wide, total[:wide])
        put(hid_ref, lat_rows * wide, total[wide:])

        lines = [west_ref[0], west_ref[1], own_west[0], own_west[1]]
        lines += [own_east[0], own_east[1], east_ref[0], east_ref[1]]
        windows = [jnp.concatenate(lines[n : n + 3], axis=1) for n in (0, 1, 4, 5)]
        windows = jnp.concatenate(windows, axis=0)
        size = windows.shape[0]
        total = pltpu.roll(dot(windows, one_ref[0]), 1, axis=0) + dot(windows, one_ref[1])
        total = total + pltpu.roll(dot(windows, one_ref[2]), size - 1, axis=0)
        total = gelu(total)
        tall = size // 4
        for n in range(4):
            cols_scr[n] = total[n * tall : (n + 1) * tall]
        last = wide - 16

        def patch(r, _):
            fixes = [cols_scr[n, pl.ds(r, 1), :] for n in range(4)]
            begin = pl.multiple_of((r + 1) * wide, 16)
            for b in range(3):
                lanes = slice(b * chans, (b + 1) * chans)
                for start in (0, last):
                    edits = [
                        (col - b - start, fix)
                        for col, fix in zip((0, 1, cols, cols + 1), fixes)
                        if 0 <= col - b - start < 16
                    ]
                    if edits:
                        value = hid_ref[pl.ds(begin + start, 16), lanes].astype(F32)
                        for at, fix in edits:
                            value = jnp.where(short_id == at, fix, value)
                        hid_ref[pl.ds(begin + start, 16), lanes] = value.astype(BF)
            return 0

        lax.fori_loop(1, lat_rows - 1, patch, 0, unroll=8)

    begin = pl.multiple_of(group * block, 16)
    total = taps(hid_ref, begin, block, wide, two_ref)
    own = first_ref[pl.ds(group * rows, rows)].reshape(block, chans).astype(F32)
    total = total + pltpu.roll(own, block - 2, axis=0)
    result = total.astype(BF)
    for i in range(rows):
        out_ref[i] = result[i * wide : i * wide + cols]


def finished(hid, first, sides, one, two, cols, lat_count):
    lat_rows, wide, chans = first.shape
    whole = pl.BlockSpec(memory_space=pltpu.VMEM)
    out, _ = pl.pallas_call(
        functools.partial(finish_kernel, lat_count),
        grid=(lat_rows // FINISH,),
        out_shape=(
            jax.ShapeDtypeStruct((lat_rows, cols, chans), BF),
            jax.ShapeDtypeStruct(hid.shape, BF),
        ),
        in_specs=[whole] * (4 + len(sides)),
        out_specs=(pl.BlockSpec((FINISH, cols, chans), lambda g: (g, 0, 0)), whole),
        input_output_aliases={0: 1},
        scratch_shapes=[
            pltpu.VMEM((8 * wide, 3 * chans), BF),
            pltpu.VMEM((4, sides[0].shape[1], chans), F32),
        ],
        compiler_params=params(26),
    )(hid, first, *sides, one, two)
    return out


def row_pairs(lat_count, lon_count):
    half = lon_count // 2

    def flat(lat, lon):
        return lat * lon_count + lon % lon_count

    inner, outer = [], []
    for lon in range(lon_count):
        for lat in range(0, lat_count, 2):
            inner += [(flat(lat, lon), flat(lat + 1, lon)), (flat(lat + 1, lon), flat(lat, lon))]
        for lat in range(1, lat_count - 1, 2):
            outer += [(flat(lat, lon), flat(lat + 1, lon)), (flat(lat + 1, lon), flat(lat, lon))]
        outer += [(flat(lat, lon), flat(lat, lon + half)) for lat in (0, lat_count - 1)]
    return inner, outer


def shards(
    obs_features,
    obs_dest,
    obs_cells,
    obs_gauss,
    row_counts,
    background,
    w_in,
    w_bg,
    w_dens,
    conv_one,
    conv_two,
):
    nrows, nfeat = obs_features.shape
    lat_rows, cols, chans = background.shape
    axes = ("lat", "lon")
    devices = lax.axis_size(axes)
    lat_count, lon_count = lax.axis_size("lat"), lax.axis_size("lon")
    cap = 2 * nrows // devices
    wide = -(-(cols + 4) // 16) * 16
    send = pack(
        row_counts, obs_dest.reshape(1, nrows), obs_cells.T, obs_gauss.T, obs_features, devices, lon_count, cap, cols,
        lat_rows // BAND,
    )
    paired = send.shape
    send = send.reshape(devices, cap + META, nfeat)
    recv = lax.all_to_all(send, axes, split_axis=0, concat_axis=0, tiled=True).reshape(paired)
    back = projected(background, w_bg, wide)
    first, own_west, own_east, inner_row, outer_row = gridded(
        recv, back, w_in, w_dens.reshape(1, chans), cap, wide, lat_rows, cols
    )
    west = lax.ppermute(own_east, "lon", [(i, (i + 1) % lon_count) for i in range(lon_count)])
    east = lax.ppermute(own_west, "lon", [((i + 1) % lon_count, i) for i in range(lon_count)])
    one = conv_one.reshape(3, 3 * chans, chans)
    two = conv_two.reshape(3, 3 * chans, chans)
    inner_row, outer_row = bordered(inner_row, outer_row, west, east, lat_rows, cols)
    inner, outer = row_pairs(lat_count, lon_count)
    hid = inside(first, one, inner_row)
    inner_row = lax.ppermute(inner_row, axes, inner)
    outer_row = lax.ppermute(outer_row, axes, outer)
    sides = (own_west, own_east, west, east, inner_row, outer_row)
    return finished(hid, first, sides, one, two, cols, lat_count)


def solution(mesh):
    rows = P(("lat", "lon"), None)
    in_specs = (rows, rows, rows, rows, P(("lat", "lon")), P("lat", "lon", None), P(), P(), P(), P(), P())
    return jax.shard_map(
        shards, mesh=mesh, in_specs=in_specs, out_specs=P("lat", "lon", None), check_vma=False
    )
```

```python
import functools

import jax
import jax.numpy as jnp
from jax import lax
from jax.experimental import pallas as pl
from jax.experimental.pallas import tpu as pltpu
from jax.sharding import PartitionSpec as P

KCELL = 4
GBINS = 32
META = 8
GROUP = 6
BAND = 18
CHUNK = 256
HEAD = 768
FINISH = 15
BF = jnp.bfloat16
F32 = jnp.float32


def params(mib):
    return pltpu.CompilerParams(vmem_limit_bytes=mib * 1024 * 1024)


def gelu(x):
    scale = 0.7978845608028654
    half = 0.5 * x
    return half + half * jnp.tanh(x * (scale + (scale * 0.044715) * (x * x)))


def dot(a, b):
    return jnp.dot(a, b, preferred_element_type=F32)


def pack_kernel(
    devices, lon_count, cap, cols, bands, count_ref, dest_ref, cells_ref, gauss_ref, feat_ref, send_ref,
    ext_ref, hot_ref, sorted_ref, place_ref, place_smem, sem,
):
    nrows, nfeat = feat_ref.shape
    step = 256
    classes = 2 * bands
    kinds = devices * classes
    dest = dest_ref[...]
    row_id = lax.broadcasted_iota(jnp.int32, (1, nrows), 1)
    base = cells_ref[0:1, :].astype(F32)
    lat = jnp.floor((base + 0.5) * (1.0 / cols))
    lon = base - lat * cols
    band = jnp.floor((lat + 0.5) * (1.0 / BAND))
    kind = 2.0 * band + (lat == band * BAND + (BAND - 1)).astype(F32)
    kind = dest * classes + kind.astype(jnp.int32)
    kind = jnp.where(row_id < count_ref[0], kind, kinds)
    ratio = gauss_ref[...].astype(F32) * (1.0 / GBINS)
    weight = jnp.exp(-3.0 * ratio * ratio)
    meta = jnp.concatenate([lat, lon, weight, jnp.zeros((nfeat - 2 - KCELL, nrows), F32)], axis=0)
    ext_ref[:, :nfeat] = feat_ref[...]
    ext_ref[:, nfeat:] = meta.T.astype(BF)
    hot_ref[...] = (lax.broadcasted_iota(jnp.int32, (kinds, nrows), 0) == kind).astype(F32).astype(BF)
    counts = dot(hot_ref[...], jnp.ones((nrows, nfeat), BF))
    ka = lax.broadcasted_iota(jnp.int32, (kinds, kinds), 0)
    kb = lax.broadcasted_iota(jnp.int32, (kinds, kinds), 1)
    da, db = ka // classes, kb // classes
    within = ((da == db) & (kb < ka)).astype(F32).astype(BF)
    together = (da == db).astype(F32).astype(BF)
    ahead = ((db < da) & (kb % classes == 0)).astype(F32).astype(BF)
    loads = dot(together, counts.astype(BF))
    padded = jnp.floor((loads + 7.0) * 0.125) * 8.0
    begins = dot(ahead, padded.astype(BF))
    mine = begins + dot(within, counts.astype(BF))
    kind_id = lax.broadcasted_iota(jnp.int32, (kinds, nfeat), 0)
    lane_id = lax.broadcasted_iota(jnp.int32, (kinds, nfeat), 1)
    lead = kind_id == lane_id * classes
    place_ref[0:1, :] = jnp.sum(jnp.where(lead, begins, 0.0), axis=0, keepdims=True).astype(jnp.int32)
    place_ref[1:2, :] = jnp.sum(jnp.where(lead, loads, 0.0), axis=0, keepdims=True).astype(jnp.int32)
    copy = pltpu.make_async_copy(place_ref, place_smem, sem)
    copy.start()
    earlier = (
        lax.broadcasted_iota(jnp.int32, (step, step), 0) < lax.broadcasted_iota(jnp.int32, (step, step), 1)
    ).astype(F32).astype(BF)
    carry = mine[:, 0:1]
    places = []
    for begin in range(0, nrows, step):
        hot = hot_ref[:, begin : begin + step]
        before = dot(hot, earlier) + carry
        hot = hot.astype(F32)
        places.append(
            jnp.sum(before * hot, axis=0, keepdims=True) + jnp.sum(hot, axis=0, keepdims=True) - 1.0
        )
        carry = carry + jnp.sum(hot, axis=1, keepdims=True)
    place = jnp.concatenate(places, axis=1)
    live = row_id < count_ref[0]
    place = jnp.where(live, place, -1.0)
    slot = lax.broadcasted_iota(jnp.int32, (step, nrows), 0).astype(F32)
    span = sorted_ref.shape[0]
    for k in range(-(-(nrows + 8 * devices) // step)):
        pick = (slot == place - k * step).astype(F32).astype(BF)
        sorted_ref[k * step : (k + 1) * step, :] = dot(pick, ext_ref[...])
    tail = -(-(nrows + 8 * devices) // step) * step
    sorted_ref[tail:span, :] = jnp.zeros((span - tail, 2 * nfeat), F32)
    copy.wait()
    side_lane = lax.broadcasted_iota(jnp.int32, (META, nfeat), 1)
    odd = (lax.axis_index("lat") * lon_count + lax.axis_index("lon")) % 2 == 1

    def one(d):
        begin = pl.multiple_of(place_smem[0, d], 8)
        got = sorted_ref[pl.ds(begin, cap), :]
        side = got[:, nfeat:]
        if cap < nfeat:
            side = jnp.concatenate([side, jnp.zeros((nfeat - cap, nfeat), F32)], axis=0)
        return got[:, :nfeat], jnp.where(side_lane < place_smem[1, d], side.T[0:META], 0.0)

    def pair(p, _):
        (rows_a, side_a), (rows_b, side_b) = one(2 * p), one(2 * p + 1)
        plain = jnp.concatenate([rows_a, side_a, rows_b, side_b], axis=0)
        turned = jnp.concatenate([side_a, rows_a, side_b, rows_b], axis=0)
        send_ref[p] = jnp.where(odd, turned, plain).astype(BF)
        return 0

    lax.fori_loop(0, devices // 2, pair, 0, unroll=2)


def pack(count, dest, cells, gauss, feats, devices, lon_count, cap, cols, bands):
    nrows, nfeat = feats.shape
    span = -(-(nrows + 8 * devices) // 256) * 256 + cap
    kinds = devices * 2 * bands
    return pl.pallas_call(
        functools.partial(pack_kernel, devices, lon_count, cap, cols, bands),
        out_shape=jax.ShapeDtypeStruct((devices // 2, 2 * (cap + META), nfeat), BF),
        in_specs=[pl.BlockSpec(memory_space=pltpu.SMEM)] + [pl.BlockSpec(memory_space=pltpu.VMEM)] * 4,
        out_specs=pl.BlockSpec(memory_space=pltpu.VMEM),
        scratch_shapes=[
            pltpu.VMEM((nrows, 2 * nfeat), BF),
            pltpu.VMEM((kinds, nrows), BF),
            pltpu.VMEM((span, 2 * nfeat), F32),
            pltpu.VMEM((8, nfeat), jnp.int32),
            pltpu.SMEM((8, nfeat), jnp.int32),
            pltpu.SemaphoreType.DMA,
        ],
        compiler_params=params(56),
    )(count, dest, cells, gauss, feats)


def back_kernel(wide, back_ref, w_bg_ref, out_ref, scr):
    rows, cols, chans = back_ref.shape
    for i in range(rows):
        scr[i * wide : i * wide + cols, :] = back_ref[i]
    out_ref[...] = pltpu.roll(dot(scr[...], w_bg_ref[...]), 2, axis=0)


def projected(background, w_bg, wide):
    lat_rows, cols, chans = background.shape
    length = max(lat_rows * wide, 1 << 16) + 16
    return pl.pallas_call(
        functools.partial(back_kernel, wide),
        grid=(lat_rows // BAND,),
        out_shape=pltpu.HBM((length, chans), F32),
        in_specs=[
            pl.BlockSpec((BAND, cols, chans), lambda g: (g, 0, 0)),
            pl.BlockSpec(memory_space=pltpu.VMEM),
        ],
        out_specs=pl.BlockSpec((BAND * wide, chans), lambda g: (g, 0)),
        scratch_shapes=[pltpu.VMEM((BAND * wide, chans), BF)],
        compiler_params=params(24),
    )(background, w_bg)


def grid_kernel(
    devices, cap, wide, cols, lat_bands, recv_ref, back_hbm, w_in_hbm, w_dens_hbm,
    first_ref, west_ref, east_ref, inner_ref, outer_ref,
    rows_ref, sides_ref, lats_ref, feat_ref, meta_ref, acc_ref, edge_scr, ends_ref, ends_smem, sem,
    back_ref, w_in_ref, w_dens_ref, sems,
):
    band = pl.program_id(0)
    bands = pl.num_programs(0)
    nfeat = recv_ref.shape[2]
    lat_rows, _, chans = first_ref.shape
    rows = lat_rows // lat_bands
    slots = devices * cap
    span = rows * wide
    fetch = pltpu.make_async_copy(
        back_hbm.at[pl.ds(pl.multiple_of(band * span, 16), span), :], back_ref, sems.at[0]
    )
    fetch.start()
    loads = [
        pltpu.make_async_copy(w_in_hbm, w_in_ref, sems.at[1]),
        pltpu.make_async_copy(w_dens_hbm, w_dens_ref, sems.at[2]),
    ]

    @pl.when(band == 0)
    def _():
        for load in loads:
            load.start()

        def read(p, _):
            both = recv_ref[p, cap : cap + 2 * META, :].astype(F32)
            for s, side in ((2 * p, both[:META]), (2 * p + 1, both[META:])):
                sides_ref[s] = side
                lats_ref[pl.ds(s, 1), :] = jnp.where(side[2:3] > 0, side[0:1], 1e6)
            return 0

        lax.fori_loop(0, devices // 2, read, 0, unroll=8)
        lats = lats_ref[...]
        lane = lax.broadcasted_iota(jnp.int32, (devices, nfeat), 1)
        ends = jnp.zeros((devices, nfeat), F32)
        for b in range(lat_bands):
            low = jnp.sum((lats < b * rows - 1.0).astype(F32), axis=1, keepdims=True)
            high = jnp.sum((lats < (b + 1.0) * rows).astype(F32), axis=1, keepdims=True)
            ends = jnp.where(lane == 2 * b, low, jnp.where(lane == 2 * b + 1, high, ends))
        ends_ref[...] = ends.astype(jnp.int32)
        copy = pltpu.make_async_copy(ends_ref, ends_smem, sem)
        copy.start()
        feat_ref[...] = jnp.zeros(feat_ref.shape, F32)
        rows_ref[slots:, :] = jnp.zeros((rows_ref.shape[0] - slots, nfeat), F32)

        def widen(p, _):
            begin = pl.multiple_of(2 * p * cap, cap)
            rows_ref[pl.ds(begin, cap), :] = recv_ref[p, 0:cap, :].astype(F32)
            rows_ref[pl.ds(begin + cap, cap), :] = recv_ref[p, cap + 2 * META :, :].astype(F32)
            return 0

        lax.fori_loop(0, devices // 2, widen, 0, unroll=2)
        copy.wait()

    meta_ref[...] = jnp.zeros(meta_ref.shape, F32)
    lane = lax.broadcasted_iota(jnp.int32, (META, nfeat), 1)

    def compact(s, out):
        out = pl.multiple_of(out, 8)
        low, high = ends_smem[s, 2 * band], ends_smem[s, 2 * band + 1]
        source = pl.multiple_of(low // 8 * 8, 8)
        feat_ref[pl.ds(out, cap), :] = rows_ref[pl.ds(pl.multiple_of(s * cap + source, 8), cap), :]
        side = sides_ref[s]
        side = jnp.where((lane >= low) & (lane < high), side, 0.0)
        shift = out - source + nfeat
        tile, shift = shift // nfeat, shift % nfeat
        moved = pltpu.roll(side, shift, axis=1)
        meta_ref[tile] += jnp.where(lane >= shift, moved, 0.0)
        meta_ref[tile + 1] += jnp.where(lane < shift, moved, 0.0)
        return out + (high - source + 7) // 8 * 8

    total = lax.fori_loop(0, devices, compact, 0, unroll=16)

    def piece(begin, size):
        begin = pl.multiple_of(begin, CHUNK)
        col_id = lax.broadcasted_iota(jnp.int32, (wide, size), 0).astype(F32)
        side = jnp.concatenate([meta_ref[1 + begin // nfeat + q] for q in range(size // nfeat)], axis=1)
        lat, lon = side[0:1], side[1:2]
        here = (col_id == lon + 2.0).astype(F32).astype(BF)
        after = (col_id == lon + 3.0).astype(F32).astype(BF)
        parts = []
        for i in range(rows):
            row = (band * rows + i).astype(F32)
            same, above = lat == row, lat == row - 1.0
            left = jnp.where(same, side[2:3], jnp.where(above, side[4:5], 0.0)).astype(BF)
            right = jnp.where(same, side[3:4], jnp.where(above, side[5:6], 0.0)).astype(BF)
            parts.append(here * left + after * right)
        spread = jnp.concatenate(parts, axis=0)
        values = jnp.concatenate(
            [feat_ref[pl.ds(begin, size), :].astype(BF), jnp.ones((size, nfeat), BF)], axis=1
        )
        return dot(spread, values)

    def more(k, _):
        acc_ref[...] += piece(k * CHUNK, CHUNK)
        return 0

    acc_ref[...] = piece(0, HEAD)
    lax.fori_loop(HEAD // CHUNK, (total + CHUNK - 1) // CHUNK, more, 0)
    fetch.wait()

    @pl.when(band == 0)
    def _():
        for load in loads:
            load.wait()

    for g in range(0, rows, GROUP):
        sums = acc_ref[g * wide : (g + GROUP) * wide, :]
        start = back_ref[g * wide : (g + GROUP) * wide, :]
        density = sums[:, nfeat:]
        normalized = (sums[:, :nfeat] / (density + 1.0)).astype(BF)
        start = start + dot(normalized, w_in_ref[...])
        start = start + jnp.concatenate([density] * (chans // nfeat), axis=1) * w_dens_ref[...]
        first = start.astype(BF)
        for i in range(GROUP):
            first_ref[band * rows + g + i] = first[i * wide : (i + 1) * wide]
            for k, col in enumerate((2, 3, cols, cols + 1)):
                edge_scr[k, pl.ds(band * rows + g + i, 1), :] = start[i * wide + col : i * wide + col + 1]

    @pl.when(band == bands - 1)
    def _():
        west_ref[...] = edge_scr[0:2].astype(BF)
        east_ref[...] = edge_scr[2:4].astype(BF)
        even = lax.axis_index("lat") % 2 == 0
        for k in range(2):
            top, bottom = first_ref[k].astype(F32), first_ref[lat_rows - 1 - k].astype(F32)
            inner = jnp.where(even, bottom, top).astype(BF)
            outer = jnp.where(even, top, bottom).astype(BF)
            inner_ref[k] = inner
            outer_ref[k] = outer


def gridded(recv, back, w_in, w_dens, cap, wide, lat_rows, cols):
    devices, nfeat = 2 * recv.shape[0], recv.shape[2]
    chans = back.shape[1]
    slots = devices * cap
    tall = -(-lat_rows // 16) * 16
    whole = pl.BlockSpec(memory_space=pltpu.VMEM)
    return pl.pallas_call(
        functools.partial(grid_kernel, devices, cap, wide, cols, lat_rows // BAND),
        grid=(lat_rows // BAND,),
        out_shape=(
            jax.ShapeDtypeStruct((lat_rows, wide, chans), BF),
            jax.ShapeDtypeStruct((2, tall, chans), BF),
            jax.ShapeDtypeStruct((2, tall, chans), BF),
            jax.ShapeDtypeStruct((2, wide, chans), BF),
            jax.ShapeDtypeStruct((2, wide, chans), BF),
        ),
        in_specs=[whole] + [pl.BlockSpec(memory_space=pltpu.HBM)] * 3,
        out_specs=(whole,) * 5,
        scratch_shapes=[
            pltpu.VMEM((slots + cap, nfeat), F32),
            pltpu.VMEM((devices, META, nfeat), F32),
            pltpu.VMEM((devices, nfeat), F32),
            pltpu.VMEM((slots + cap + HEAD, nfeat), F32),
            pltpu.VMEM((slots // nfeat + 8, META, nfeat), F32),
            pltpu.VMEM((BAND * wide, 2 * nfeat), F32),
            pltpu.VMEM((4, tall, chans), F32),
            pltpu.VMEM((devices, nfeat), jnp.int32),
            pltpu.SMEM((devices, nfeat), jnp.int32),
            pltpu.SemaphoreType.DMA,
            pltpu.VMEM((BAND * wide, chans), F32),
            pltpu.VMEM(w_in.shape, BF),
            pltpu.VMEM(w_dens.shape, F32),
            pltpu.SemaphoreType.DMA((3,)),
        ],
        compiler_params=params(32),
    )(recv, back, w_in, w_dens)


def put(ref, begin, value):
    size, chans = value.shape
    for b in range(3):
        part = value if b == 0 else pltpu.roll(value, size - b, axis=0)
        ref[pl.ds(begin, size), b * chans : (b + 1) * chans] = part.astype(BF)


def taps(ref, begin, size, wide, w_ref):
    field = jnp.concatenate([ref[pl.ds(begin + a * wide, size), :] for a in range(3)], axis=1)
    return dot(field, w_ref[...].reshape(field.shape[1], w_ref.shape[2]))


def border_kernel(lat_rows, cols, inner_ref, outer_ref, west_ref, east_ref, after_ref, inner_out, outer_out):
    _, wide, chans = inner_ref.shape
    even = lax.axis_index("lat") % 2 == 0
    row_id = lax.broadcasted_iota(jnp.int32, (wide, chans), 0)
    sides = [west_ref[0], west_ref[1], east_ref[0], east_ref[1]]
    sides = [side.astype(F32) for side in sides]
    for k in range(2):
        inner, outer = inner_ref[k].astype(F32), outer_ref[k].astype(F32)
        for side, col in zip(sides, (0, 1, cols + 2, cols + 3)):
            top = side[k : k + 1]
            bottom = side[lat_rows - 1 - k : lat_rows - k]
            inner = jnp.where(row_id == col, jnp.where(even, bottom, top), inner)
            outer = jnp.where(row_id == col, jnp.where(even, top, bottom), outer)
        inner_out[k] = inner.astype(BF)
        outer_out[k] = outer.astype(BF)


def bordered(inner, outer, west, east, after, lat_rows, cols):
    whole = pl.BlockSpec(memory_space=pltpu.VMEM)
    shape = jax.ShapeDtypeStruct(inner.shape, BF)
    return pl.pallas_call(
        functools.partial(border_kernel, lat_rows, cols),
        out_shape=(shape, shape),
        in_specs=[whole] * 4 + [pl.BlockSpec(memory_space=pl.ANY)],
        out_specs=(whole, whole),
        compiler_params=params(24),
    )(inner, outer, west, east, after)


def inside_kernel(lead, place, first_ref, one_ref, after_ref, hid_ref, field):
    lat_rows, wide, chans = first_ref.shape
    half = lat_rows // 2

    def load(r, _):
        put(field, pl.multiple_of(r * wide, 16), first_ref[lead + r].astype(F32))
        return 0

    lax.fori_loop(0, half + 2, load, 0)
    size = FINISH * wide

    def hidden(g, _):
        begin = pl.multiple_of(g * size, 16)
        total = taps(field, begin, size, wide, one_ref)
        put(hid_ref, pl.multiple_of(begin + place * wide, 16), gelu(total))
        return 0

    lax.fori_loop(0, half // FINISH, hidden, 0)


def inside(first, one, after, lead, place):
    lat_rows, wide, chans = first.shape
    size = (lat_rows // 2 + 2) * wide
    whole = pl.BlockSpec(memory_space=pltpu.VMEM)
    return pl.pallas_call(
        functools.partial(inside_kernel, lead, place),
        out_shape=jax.ShapeDtypeStruct((size, 3 * chans), BF),
        in_specs=[whole, whole, pl.BlockSpec(memory_space=pl.ANY)],
        out_specs=whole,
        scratch_shapes=[pltpu.VMEM((size, 3 * chans), BF)],
        compiler_params=params(24),
    )(first, one, after)


def finish_kernel(
    lat_count, upper_in, lower_in, first_ref, own_west, own_east, west_ref, east_ref, inner_ref, outer_ref,
    one_ref, two_ref, out_ref, upper_ref, lower_ref, rim, cols_scr,
):
    group = pl.program_id(0)
    lat_rows, wide, chans = first_ref.shape
    rows, cols, _ = out_ref.shape
    block = rows * wide
    half = lat_rows // 2

    @pl.when(group == 0)
    def _():
        lat_index = lax.axis_index("lat")
        even = lat_index % 2 == 0
        row_id = lax.broadcasted_iota(jnp.int32, (wide, chans), 0)
        short_id = lax.broadcasted_iota(jnp.int32, (16, chans), 0)

        def edge_row(north, k):
            return jnp.where(even == north, outer_ref[k].astype(F32), inner_ref[k].astype(F32))

        def own_row(r):
            value = first_ref[r].astype(F32)
            sides = [west_ref[0], west_ref[1], east_ref[0], east_ref[1]]
            for side, col in zip(sides, (0, 1, cols + 2, cols + 3)):
                value = jnp.where(row_id == col, side.astype(F32)[r : r + 1], value)
            return value

        lines = [edge_row(True, 1), edge_row(True, 0), own_row(0), own_row(1)]
        lines += [own_row(lat_rows - 2), own_row(lat_rows - 1), edge_row(False, 0), edge_row(False, 1)]
        for n, line in enumerate(lines):
            put(rim, n * wide, line)
        ends = (
            (0, upper_ref, 0, lat_index == 0),
            (5, lower_ref, half + 1, lat_index == lat_count - 1),
        )
        for begin, ref, index, pole in ends:
            total = jnp.zeros((wide, chans), F32)
            for a in range(3):
                tap = jnp.where(pole, 2 - a, a)
                total = total + dot(rim[(begin + a) * wide : (begin + a + 1) * wide, :], one_ref[tap])
            put(ref, index * wide, gelu(total))
        total = jnp.zeros((2 * wide, chans), F32)
        for a in range(3):
            pair = [rim[(n + a) * wide : (n + a + 1) * wide, :] for n in (1, 4)]
            total = total + dot(jnp.concatenate(pair, axis=0), one_ref[a])
        total = gelu(total)
        put(upper_ref, wide, total[:wide])
        put(lower_ref, half * wide, total[wide:])

        lines = [west_ref[0], west_ref[1], own_west[0], own_west[1]]
        lines += [own_east[0], own_east[1], east_ref[0], east_ref[1]]
        windows = [jnp.concatenate(lines[n : n + 3], axis=1) for n in (0, 1, 4, 5)]
        windows = jnp.concatenate(windows, axis=0)
        size = windows.shape[0]
        total = pltpu.roll(dot(windows, one_ref[0]), 1, axis=0) + dot(windows, one_ref[1])
        total = total + pltpu.roll(dot(windows, one_ref[2]), size - 1, axis=0)
        total = gelu(total)
        tall = size // 4
        for n in range(4):
            cols_scr[n] = total[n * tall : (n + 1) * tall]
        last = wide - 16

        def patch(ref, shift, r, _):
            fixes = [cols_scr[n, pl.ds(r, 1), :] for n in range(4)]
            begin = pl.multiple_of((r - shift) * wide, 16)
            for b in range(3):
                lanes = slice(b * chans, (b + 1) * chans)
                for start in (0, last):
                    edits = [
                        (col - b - start, fix)
                        for col, fix in zip((0, 1, cols, cols + 1), fixes)
                        if 0 <= col - b - start < 16
                    ]
                    if edits:
                        value = ref[pl.ds(begin + start, 16), lanes].astype(F32)
                        for at, fix in edits:
                            value = jnp.where(short_id == at, fix, value)
                        ref[pl.ds(begin + start, 16), lanes] = value.astype(BF)
            return 0

        lax.fori_loop(1, half + 1, functools.partial(patch, upper_ref, -1), 0, unroll=9)
        lax.fori_loop(half - 1, lat_rows - 1, functools.partial(patch, lower_ref, half - 1), 0, unroll=9)

    def second(ref, first_group):
        begin = pl.multiple_of((group - first_group) * block, 16)
        total = taps(ref, begin, block, wide, two_ref)
        own = first_ref[pl.ds(group * rows, rows)].reshape(block, chans).astype(F32)
        total = total + pltpu.roll(own, block - 2, axis=0)
        result = total.astype(BF)
        for i in range(rows):
            out_ref[i] = result[i * wide : i * wide + cols]

    pl.when(group < half // rows)(lambda: second(upper_ref, 0))
    pl.when(group >= half // rows)(lambda: second(lower_ref, half // rows))


def finished(upper, lower, first, sides, one, two, cols, lat_count):
    lat_rows, wide, chans = first.shape
    whole = pl.BlockSpec(memory_space=pltpu.VMEM)
    out, _, _ = pl.pallas_call(
        functools.partial(finish_kernel, lat_count),
        grid=(lat_rows // FINISH,),
        out_shape=(
            jax.ShapeDtypeStruct((lat_rows, cols, chans), BF),
            jax.ShapeDtypeStruct(upper.shape, BF),
            jax.ShapeDtypeStruct(lower.shape, BF),
        ),
        in_specs=[whole] * (5 + len(sides)),
        out_specs=(pl.BlockSpec((FINISH, cols, chans), lambda g: (g, 0, 0)), whole, whole),
        input_output_aliases={0: 1, 1: 2},
        scratch_shapes=[
            pltpu.VMEM((8 * wide, 3 * chans), BF),
            pltpu.VMEM((4, sides[0].shape[1], chans), F32),
        ],
        compiler_params=params(26),
    )(upper, lower, first, *sides, one, two)
    return out


def row_pairs(lat_count, lon_count):
    half = lon_count // 2

    def flat(lat, lon):
        return lat * lon_count + lon % lon_count

    inner, outer = [], []
    for lon in range(lon_count):
        for lat in range(0, lat_count, 2):
            inner += [(flat(lat, lon), flat(lat + 1, lon)), (flat(lat + 1, lon), flat(lat, lon))]
        for lat in range(1, lat_count - 1, 2):
            outer += [(flat(lat, lon), flat(lat + 1, lon)), (flat(lat + 1, lon), flat(lat, lon))]
        outer += [(flat(lat, lon), flat(lat, lon + half)) for lat in (0, lat_count - 1)]
    return inner, outer


def shards(
    obs_features,
    obs_dest,
    obs_cells,
    obs_gauss,
    row_counts,
    background,
    w_in,
    w_bg,
    w_dens,
    conv_one,
    conv_two,
):
    nrows, nfeat = obs_features.shape
    lat_rows, cols, chans = background.shape
    axes = ("lat", "lon")
    devices = lax.axis_size(axes)
    lat_count, lon_count = lax.axis_size("lat"), lax.axis_size("lon")
    cap = 2 * nrows // devices
    wide = -(-(cols + 4) // 16) * 16
    send = pack(
        row_counts, obs_dest.reshape(1, nrows), obs_cells.T, obs_gauss.T, obs_features, devices, lon_count, cap, cols,
        lat_rows // BAND,
    )
    paired = send.shape
    send = send.reshape(devices, cap + META, nfeat)
    recv = lax.all_to_all(send, axes, split_axis=0, concat_axis=0, tiled=True).reshape(paired)
    back = projected(background, w_bg, wide)
    first, own_west, own_east, inner_row, outer_row = gridded(
        recv, back, w_in, w_dens.reshape(1, chans), cap, wide, lat_rows, cols
    )
    west = lax.ppermute(own_east, "lon", [(i, (i + 1) % lon_count) for i in range(lon_count)])
    east = lax.ppermute(own_west, "lon", [((i + 1) % lon_count, i) for i in range(lon_count)])
    one = conv_one.reshape(3, 3 * chans, chans)
    two = conv_two.reshape(3, 3 * chans, chans)
    half = lat_rows // 2
    upper = inside(first, one, own_west, 0, 2)
    inner_row, outer_row = bordered(inner_row, outer_row, west, east, upper, lat_rows, cols)
    inner, outer = row_pairs(lat_count, lon_count)
    lower = inside(first, one, inner_row, half - 2, 0)
    inner_row = lax.ppermute(inner_row, axes, inner)
    outer_row = lax.ppermute(outer_row, axes, outer)
    sides = (own_west, own_east, west, east, inner_row, outer_row)
    return finished(upper, lower, first, sides, one, two, cols, lat_count)


def solution(mesh):
    rows = P(("lat", "lon"), None)
    in_specs = (rows, rows, rows, rows, P(("lat", "lon")), P("lat", "lon", None), P(), P(), P(), P(), P())
    return jax.shard_map(
        shards, mesh=mesh, in_specs=in_specs, out_specs=P("lat", "lon", None), check_vma=False
    )
```

```python
import functools

import jax
import jax.numpy as jnp
from jax import lax
from jax.experimental import pallas as pl
from jax.experimental.pallas import tpu as pltpu
from jax.sharding import PartitionSpec as P

KCELL = 4
GBINS = 32
META = 8
GROUP = 6
BAND = 18
CHUNK = 256
HEAD = 768
FINISH = 15
UPPER = 30
BF = jnp.bfloat16
F32 = jnp.float32


def params(mib):
    return pltpu.CompilerParams(vmem_limit_bytes=mib * 1024 * 1024)


def gelu(x):
    scale = 0.7978845608028654
    half = 0.5 * x
    return half + half * jnp.tanh(x * (scale + (scale * 0.044715) * (x * x)))


def dot(a, b):
    return jnp.dot(a, b, preferred_element_type=F32)


def pack_kernel(
    devices, lon_count, cap, cols, bands, count_ref, dest_ref, cells_ref, gauss_ref, feat_ref, send_ref,
    ext_ref, hot_ref, sorted_ref, place_ref, place_smem, sem,
):
    nrows, nfeat = feat_ref.shape
    step = 256
    classes = 2 * bands
    kinds = devices * classes
    dest = dest_ref[...]
    row_id = lax.broadcasted_iota(jnp.int32, (1, nrows), 1)
    base = cells_ref[0:1, :].astype(F32)
    lat = jnp.floor((base + 0.5) * (1.0 / cols))
    lon = base - lat * cols
    band = jnp.floor((lat + 0.5) * (1.0 / BAND))
    kind = 2.0 * band + (lat == band * BAND + (BAND - 1)).astype(F32)
    kind = dest * classes + kind.astype(jnp.int32)
    kind = jnp.where(row_id < count_ref[0], kind, kinds)
    ratio = gauss_ref[...].astype(F32) * (1.0 / GBINS)
    weight = jnp.exp(-3.0 * ratio * ratio)
    meta = jnp.concatenate([lat, lon, weight, jnp.zeros((nfeat - 2 - KCELL, nrows), F32)], axis=0)
    ext_ref[:, :nfeat] = feat_ref[...]
    ext_ref[:, nfeat:] = meta.T.astype(BF)
    hot_ref[...] = (lax.broadcasted_iota(jnp.int32, (kinds, nrows), 0) == kind).astype(F32).astype(BF)
    counts = dot(hot_ref[...], jnp.ones((nrows, nfeat), BF))
    ka = lax.broadcasted_iota(jnp.int32, (kinds, kinds), 0)
    kb = lax.broadcasted_iota(jnp.int32, (kinds, kinds), 1)
    da, db = ka // classes, kb // classes
    within = ((da == db) & (kb < ka)).astype(F32).astype(BF)
    together = (da == db).astype(F32).astype(BF)
    ahead = ((db < da) & (kb % classes == 0)).astype(F32).astype(BF)
    loads = dot(together, counts.astype(BF))
    padded = jnp.floor((loads + 7.0) * 0.125) * 8.0
    begins = dot(ahead, padded.astype(BF))
    mine = begins + dot(within, counts.astype(BF))
    kind_id = lax.broadcasted_iota(jnp.int32, (kinds, nfeat), 0)
    lane_id = lax.broadcasted_iota(jnp.int32, (kinds, nfeat), 1)
    lead = kind_id == lane_id * classes
    place_ref[0:1, :] = jnp.sum(jnp.where(lead, begins, 0.0), axis=0, keepdims=True).astype(jnp.int32)
    place_ref[1:2, :] = jnp.sum(jnp.where(lead, loads, 0.0), axis=0, keepdims=True).astype(jnp.int32)
    copy = pltpu.make_async_copy(place_ref, place_smem, sem)
    copy.start()
    earlier = (
        lax.broadcasted_iota(jnp.int32, (step, step), 0) < lax.broadcasted_iota(jnp.int32, (step, step), 1)
    ).astype(F32).astype(BF)
    carry = mine[:, 0:1]
    places = []
    for begin in range(0, nrows, step):
        hot = hot_ref[:, begin : begin + step]
        before = dot(hot, earlier) + carry
        hot = hot.astype(F32)
        places.append(
            jnp.sum(before * hot, axis=0, keepdims=True) + jnp.sum(hot, axis=0, keepdims=True) - 1.0
        )
        carry = carry + jnp.sum(hot, axis=1, keepdims=True)
    place = jnp.concatenate(places, axis=1)
    live = row_id < count_ref[0]
    place = jnp.where(live, place, -1.0)
    slot = lax.broadcasted_iota(jnp.int32, (step, nrows), 0).astype(F32)
    span = sorted_ref.shape[0]
    for k in range(-(-(nrows + 8 * devices) // step)):
        pick = (slot == place - k * step).astype(F32).astype(BF)
        sorted_ref[k * step : (k + 1) * step, :] = dot(pick, ext_ref[...])
    tail = -(-(nrows + 8 * devices) // step) * step
    sorted_ref[tail:span, :] = jnp.zeros((span - tail, 2 * nfeat), F32)
    copy.wait()
    side_lane = lax.broadcasted_iota(jnp.int32, (META, nfeat), 1)
    odd = (lax.axis_index("lat") * lon_count + lax.axis_index("lon")) % 2 == 1

    def one(d):
        begin = pl.multiple_of(place_smem[0, d], 8)
        got = sorted_ref[pl.ds(begin, cap), :]
        side = got[:, nfeat:]
        if cap < nfeat:
            side = jnp.concatenate([side, jnp.zeros((nfeat - cap, nfeat), F32)], axis=0)
        return got[:, :nfeat], jnp.where(side_lane < place_smem[1, d], side.T[0:META], 0.0)

    def pair(p, _):
        (rows_a, side_a), (rows_b, side_b) = one(2 * p), one(2 * p + 1)
        plain = jnp.concatenate([rows_a, side_a, rows_b, side_b], axis=0)
        turned = jnp.concatenate([side_a, rows_a, side_b, rows_b], axis=0)
        send_ref[p] = jnp.where(odd, turned, plain).astype(BF)
        return 0

    lax.fori_loop(0, devices // 2, pair, 0, unroll=2)


def pack(count, dest, cells, gauss, feats, devices, lon_count, cap, cols, bands):
    nrows, nfeat = feats.shape
    span = -(-(nrows + 8 * devices) // 256) * 256 + cap
    kinds = devices * 2 * bands
    return pl.pallas_call(
        functools.partial(pack_kernel, devices, lon_count, cap, cols, bands),
        out_shape=jax.ShapeDtypeStruct((devices // 2, 2 * (cap + META), nfeat), BF),
        in_specs=[pl.BlockSpec(memory_space=pltpu.SMEM)] + [pl.BlockSpec(memory_space=pltpu.VMEM)] * 4,
        out_specs=pl.BlockSpec(memory_space=pltpu.VMEM),
        scratch_shapes=[
            pltpu.VMEM((nrows, 2 * nfeat), BF),
            pltpu.VMEM((kinds, nrows), BF),
            pltpu.VMEM((span, 2 * nfeat), F32),
            pltpu.VMEM((8, nfeat), jnp.int32),
            pltpu.SMEM((8, nfeat), jnp.int32),
            pltpu.SemaphoreType.DMA,
        ],
        compiler_params=params(56),
    )(count, dest, cells, gauss, feats)


def back_kernel(wide, back_ref, w_bg_ref, out_ref, scr):
    rows, cols, chans = back_ref.shape
    for i in range(rows):
        scr[i * wide : i * wide + cols, :] = back_ref[i]
    out_ref[...] = pltpu.roll(dot(scr[...], w_bg_ref[...]), 2, axis=0)


def projected(background, w_bg, wide):
    lat_rows, cols, chans = background.shape
    length = max(lat_rows * wide, 1 << 16) + 16
    return pl.pallas_call(
        functools.partial(back_kernel, wide),
        grid=(lat_rows // BAND,),
        out_shape=pltpu.HBM((length, chans), F32),
        in_specs=[
            pl.BlockSpec((BAND, cols, chans), lambda g: (g, 0, 0)),
            pl.BlockSpec(memory_space=pltpu.VMEM),
        ],
        out_specs=pl.BlockSpec((BAND * wide, chans), lambda g: (g, 0)),
        scratch_shapes=[pltpu.VMEM((BAND * wide, chans), BF)],
        compiler_params=params(24),
    )(background, w_bg)


def grid_kernel(
    devices, cap, wide, cols, lat_bands, recv_ref, back_hbm, w_in_hbm, w_dens_hbm,
    first_ref, west_ref, east_ref, inner_ref, outer_ref,
    rows_ref, sides_ref, lats_ref, feat_ref, meta_ref, acc_ref, edge_scr, ends_ref, ends_smem, sem,
    back_ref, w_in_ref, w_dens_ref, sems,
):
    band = pl.program_id(0)
    bands = pl.num_programs(0)
    nfeat = recv_ref.shape[2]
    lat_rows, _, chans = first_ref.shape
    rows = lat_rows // lat_bands
    slots = devices * cap
    span = rows * wide
    fetch = pltpu.make_async_copy(
        back_hbm.at[pl.ds(pl.multiple_of(band * span, 16), span), :], back_ref, sems.at[0]
    )
    fetch.start()
    loads = [
        pltpu.make_async_copy(w_in_hbm, w_in_ref, sems.at[1]),
        pltpu.make_async_copy(w_dens_hbm, w_dens_ref, sems.at[2]),
    ]

    @pl.when(band == 0)
    def _():
        for load in loads:
            load.start()

        def read(p, _):
            both = recv_ref[p, cap : cap + 2 * META, :].astype(F32)
            for s, side in ((2 * p, both[:META]), (2 * p + 1, both[META:])):
                sides_ref[s] = side
                lats_ref[pl.ds(s, 1), :] = jnp.where(side[2:3] > 0, side[0:1], 1e6)
            return 0

        lax.fori_loop(0, devices // 2, read, 0, unroll=8)
        lats = lats_ref[...]
        lane = lax.broadcasted_iota(jnp.int32, (devices, nfeat), 1)
        ends = jnp.zeros((devices, nfeat), F32)
        for b in range(lat_bands):
            low = jnp.sum((lats < b * rows - 1.0).astype(F32), axis=1, keepdims=True)
            high = jnp.sum((lats < (b + 1.0) * rows).astype(F32), axis=1, keepdims=True)
            ends = jnp.where(lane == 2 * b, low, jnp.where(lane == 2 * b + 1, high, ends))
        ends_ref[...] = ends.astype(jnp.int32)
        copy = pltpu.make_async_copy(ends_ref, ends_smem, sem)
        copy.start()
        feat_ref[...] = jnp.zeros(feat_ref.shape, F32)
        rows_ref[slots:, :] = jnp.zeros((rows_ref.shape[0] - slots, nfeat), F32)

        def widen(p, _):
            begin = pl.multiple_of(2 * p * cap, cap)
            rows_ref[pl.ds(begin, cap), :] = recv_ref[p, 0:cap, :].astype(F32)
            rows_ref[pl.ds(begin + cap, cap), :] = recv_ref[p, cap + 2 * META :, :].astype(F32)
            return 0

        lax.fori_loop(0, devices // 2, widen, 0, unroll=2)
        copy.wait()

    meta_ref[...] = jnp.zeros(meta_ref.shape, F32)
    lane = lax.broadcasted_iota(jnp.int32, (META, nfeat), 1)

    def compact(s, out):
        out = pl.multiple_of(out, 8)
        low, high = ends_smem[s, 2 * band], ends_smem[s, 2 * band + 1]
        source = pl.multiple_of(low // 8 * 8, 8)
        feat_ref[pl.ds(out, cap), :] = rows_ref[pl.ds(pl.multiple_of(s * cap + source, 8), cap), :]
        side = sides_ref[s]
        side = jnp.where((lane >= low) & (lane < high), side, 0.0)
        shift = out - source + nfeat
        tile, shift = shift // nfeat, shift % nfeat
        moved = pltpu.roll(side, shift, axis=1)
        meta_ref[tile] += jnp.where(lane >= shift, moved, 0.0)
        meta_ref[tile + 1] += jnp.where(lane < shift, moved, 0.0)
        return out + (high - source + 7) // 8 * 8

    total = lax.fori_loop(0, devices, compact, 0, unroll=16)

    def piece(begin, size):
        begin = pl.multiple_of(begin, CHUNK)
        col_id = lax.broadcasted_iota(jnp.int32, (wide, size), 0).astype(F32)
        side = jnp.concatenate([meta_ref[1 + begin // nfeat + q] for q in range(size // nfeat)], axis=1)
        lat, lon = side[0:1], side[1:2]
        here = (col_id == lon + 2.0).astype(F32).astype(BF)
        after = (col_id == lon + 3.0).astype(F32).astype(BF)
        parts = []
        for i in range(rows):
            row = (band * rows + i).astype(F32)
            same, above = lat == row, lat == row - 1.0
            left = jnp.where(same, side[2:3], jnp.where(above, side[4:5], 0.0)).astype(BF)
            right = jnp.where(same, side[3:4], jnp.where(above, side[5:6], 0.0)).astype(BF)
            parts.append(here * left + after * right)
        spread = jnp.concatenate(parts, axis=0)
        values = jnp.concatenate(
            [feat_ref[pl.ds(begin, size), :].astype(BF), jnp.ones((size, nfeat), BF)], axis=1
        )
        return dot(spread, values)

    def more(k, _):
        acc_ref[...] += piece(k * CHUNK, CHUNK)
        return 0

    acc_ref[...] = piece(0, HEAD)
    lax.fori_loop(HEAD // CHUNK, (total + CHUNK - 1) // CHUNK, more, 0)
    fetch.wait()

    @pl.when(band == 0)
    def _():
        for load in loads:
            load.wait()

    for g in range(0, rows, GROUP):
        sums = acc_ref[g * wide : (g + GROUP) * wide, :]
        start = back_ref[g * wide : (g + GROUP) * wide, :]
        density = sums[:, nfeat:]
        normalized = (sums[:, :nfeat] / (density + 1.0)).astype(BF)
        start = start + dot(normalized, w_in_ref[...])
        start = start + jnp.concatenate([density] * (chans // nfeat), axis=1) * w_dens_ref[...]
        first = start.astype(BF)
        for i in range(GROUP):
            first_ref[band * rows + g + i] = first[i * wide : (i + 1) * wide]
            for k, col in enumerate((2, 3, cols, cols + 1)):
                edge_scr[k, pl.ds(band * rows + g + i, 1), :] = start[i * wide + col : i * wide + col + 1]

    @pl.when(band == bands - 1)
    def _():
        west_ref[...] = edge_scr[0:2].astype(BF)
        east_ref[...] = edge_scr[2:4].astype(BF)
        even = lax.axis_index("lat") % 2 == 0
        for k in range(2):
            top, bottom = first_ref[k].astype(F32), first_ref[lat_rows - 1 - k].astype(F32)
            inner = jnp.where(even, bottom, top).astype(BF)
            outer = jnp.where(even, top, bottom).astype(BF)
            inner_ref[k] = inner
            outer_ref[k] = outer


def gridded(recv, back, w_in, w_dens, cap, wide, lat_rows, cols):
    devices, nfeat = 2 * recv.shape[0], recv.shape[2]
    chans = back.shape[1]
    slots = devices * cap
    tall = -(-lat_rows // 16) * 16
    whole = pl.BlockSpec(memory_space=pltpu.VMEM)
    return pl.pallas_call(
        functools.partial(grid_kernel, devices, cap, wide, cols, lat_rows // BAND),
        grid=(lat_rows // BAND,),
        out_shape=(
            jax.ShapeDtypeStruct((lat_rows, wide, chans), BF),
            jax.ShapeDtypeStruct((2, tall, chans), BF),
            jax.ShapeDtypeStruct((2, tall, chans), BF),
            jax.ShapeDtypeStruct((2, wide, chans), BF),
            jax.ShapeDtypeStruct((2, wide, chans), BF),
        ),
        in_specs=[whole] + [pl.BlockSpec(memory_space=pltpu.HBM)] * 3,
        out_specs=(whole,) * 5,
        scratch_shapes=[
            pltpu.VMEM((slots + cap, nfeat), F32),
            pltpu.VMEM((devices, META, nfeat), F32),
            pltpu.VMEM((devices, nfeat), F32),
            pltpu.VMEM((slots + cap + HEAD, nfeat), F32),
            pltpu.VMEM((slots // nfeat + 8, META, nfeat), F32),
            pltpu.VMEM((BAND * wide, 2 * nfeat), F32),
            pltpu.VMEM((4, tall, chans), F32),
            pltpu.VMEM((devices, nfeat), jnp.int32),
            pltpu.SMEM((devices, nfeat), jnp.int32),
            pltpu.SemaphoreType.DMA,
            pltpu.VMEM((BAND * wide, chans), F32),
            pltpu.VMEM(w_in.shape, BF),
            pltpu.VMEM(w_dens.shape, F32),
            pltpu.SemaphoreType.DMA((3,)),
        ],
        compiler_params=params(32),
    )(recv, back, w_in, w_dens)


def put(ref, begin, value):
    size, chans = value.shape
    for b in range(3):
        part = value if b == 0 else pltpu.roll(value, size - b, axis=0)
        ref[pl.ds(begin, size), b * chans : (b + 1) * chans] = part.astype(BF)


def taps(ref, begin, size, wide, w_ref):
    field = jnp.concatenate([ref[pl.ds(begin + a * wide, size), :] for a in range(3)], axis=1)
    return dot(field, w_ref[...].reshape(field.shape[1], w_ref.shape[2]))


def border_kernel(lat_rows, cols, inner_ref, outer_ref, west_ref, east_ref, after_ref, inner_out, outer_out):
    _, wide, chans = inner_ref.shape
    even = lax.axis_index("lat") % 2 == 0
    row_id = lax.broadcasted_iota(jnp.int32, (wide, chans), 0)
    sides = [west_ref[0], west_ref[1], east_ref[0], east_ref[1]]
    sides = [side.astype(F32) for side in sides]
    for k in range(2):
        inner, outer = inner_ref[k].astype(F32), outer_ref[k].astype(F32)
        for side, col in zip(sides, (0, 1, cols + 2, cols + 3)):
            top = side[k : k + 1]
            bottom = side[lat_rows - 1 - k : lat_rows - k]
            inner = jnp.where(row_id == col, jnp.where(even, bottom, top), inner)
            outer = jnp.where(row_id == col, jnp.where(even, top, bottom), outer)
        inner_out[k] = inner.astype(BF)
        outer_out[k] = outer.astype(BF)


def bordered(inner, outer, west, east, after, lat_rows, cols):
    whole = pl.BlockSpec(memory_space=pltpu.VMEM)
    shape = jax.ShapeDtypeStruct(inner.shape, BF)
    return pl.pallas_call(
        functools.partial(border_kernel, lat_rows, cols),
        out_shape=(shape, shape),
        in_specs=[whole] * 4 + [pl.BlockSpec(memory_space=pl.ANY)],
        out_specs=(whole, whole),
        compiler_params=params(24),
    )(inner, outer, west, east, after)


def with_sides(value, sides, cols):
    wide, chans = value.shape
    last = wide - 16
    row_id = lax.broadcasted_iota(jnp.int32, (16, chans), 0)
    head, tail = value[:16], value[last:]
    for k in range(2):
        head = jnp.where(row_id == k, sides[k], head)
        tail = jnp.where(row_id == cols + 2 + k - last, sides[2 + k], tail)
    return jnp.concatenate([head, value[16:last], tail], axis=0)


def convolve_rows(field, one_ref, hid_ref, place, count, wide):
    size = FINISH * wide

    def hidden(g, _):
        begin = pl.multiple_of(g * size, 16)
        total = taps(field, begin, size, wide, one_ref)
        put(hid_ref, pl.multiple_of(begin + place * wide, 16), gelu(total))
        return 0

    lax.fori_loop(0, count // FINISH, hidden, 0)


def upper_kernel(first_ref, one_ref, after_ref, hid_ref, field):
    wide = first_ref.shape[1]
    count = field.shape[0] // wide

    def load(r, _):
        put(field, pl.multiple_of(r * wide, 16), first_ref[r].astype(F32))
        return 0

    lax.fori_loop(0, count, load, 0, unroll=4)
    convolve_rows(field, one_ref, hid_ref, 2, count - 2, wide)


def lower_kernel(cols, first_ref, one_ref, west_ref, east_ref, after_ref, hid_ref, field, side_scr):
    lat_rows, wide, _ = first_ref.shape
    count = field.shape[0] // wide
    lead = lat_rows - count
    side_scr[0:2] = west_ref[...].astype(F32)
    side_scr[2:4] = east_ref[...].astype(F32)

    def load(r, _):
        sides = [side_scr[k, pl.ds(lead + r, 1), :] for k in range(4)]
        value = with_sides(first_ref[lead + r].astype(F32), sides, cols)
        put(field, pl.multiple_of(r * wide, 16), value)
        return 0

    lax.fori_loop(0, count, load, 0, unroll=2)
    convolve_rows(field, one_ref, hid_ref, 0, count - 2, wide)


def upper_part(first, one, after, rows):
    _, wide, chans = first.shape
    whole = pl.BlockSpec(memory_space=pltpu.VMEM)
    shape = ((rows + 2) * wide, 3 * chans)
    return pl.pallas_call(
        upper_kernel,
        out_shape=jax.ShapeDtypeStruct(shape, BF),
        in_specs=[whole, whole, pl.BlockSpec(memory_space=pl.ANY)],
        out_specs=whole,
        scratch_shapes=[pltpu.VMEM(shape, BF)],
        compiler_params=params(24),
    )(first, one, after)


def lower_part(first, one, west, east, after, rows, cols):
    _, wide, chans = first.shape
    whole = pl.BlockSpec(memory_space=pltpu.VMEM)
    shape = ((rows + 2) * wide, 3 * chans)
    return pl.pallas_call(
        functools.partial(lower_kernel, cols),
        out_shape=jax.ShapeDtypeStruct(shape, BF),
        in_specs=[whole] * 4 + [pl.BlockSpec(memory_space=pl.ANY)],
        out_specs=whole,
        scratch_shapes=[pltpu.VMEM(shape, BF), pltpu.VMEM((4, west.shape[1], chans), F32)],
        compiler_params=params(24),
    )(first, one, west, east, after)


def finish_kernel(
    lat_count, upper_in, lower_in, first_ref, own_west, own_east, west_ref, east_ref, inner_ref, outer_ref,
    one_ref, two_ref, out_ref, upper_ref, lower_ref, rim, cols_scr,
):
    group = pl.program_id(0)
    lat_rows, wide, chans = first_ref.shape
    rows, cols, _ = out_ref.shape
    block = rows * wide
    above = upper_ref.shape[0] // wide - 2
    below = lat_rows - above

    @pl.when(group == 0)
    def _():
        lat_index = lax.axis_index("lat")
        even = lat_index % 2 == 0
        short_id = lax.broadcasted_iota(jnp.int32, (16, chans), 0)
        lines = [west_ref[0], west_ref[1], own_west[0], own_west[1]]
        lines += [own_east[0], own_east[1], east_ref[0], east_ref[1]]
        lines = [line.astype(F32) for line in lines]

        def edge_row(north, k):
            return jnp.where(even == north, outer_ref[k].astype(F32), inner_ref[k].astype(F32))

        def own_row(r):
            sides = [lines[n][r : r + 1] for n in (0, 1, 6, 7)]
            return with_sides(first_ref[r].astype(F32), sides, cols)

        rims = [edge_row(True, 1), edge_row(True, 0), own_row(0), own_row(1)]
        rims += [own_row(lat_rows - 2), own_row(lat_rows - 1), edge_row(False, 0), edge_row(False, 1)]
        for n, line in enumerate(rims):
            put(rim, n * wide, line)
        size = cols_scr.shape[1]
        fields = []
        for a in range(3):
            top = jnp.where(lat_index == 0, 2 - a, a)
            bottom = jnp.where(lat_index == lat_count - 1, 7 - a, 5 + a)
            parts = [
                rim[pl.ds(pl.multiple_of(n * wide, 16), wide), :] for n in (top, 1 + a, 4 + a, bottom)
            ]
            for n in (0, 1, 4, 5):
                window = [lines[n + b][a : a + size].astype(BF) for b in range(3)]
                parts.append(jnp.concatenate(window, axis=1))
            fields.append(jnp.concatenate(parts, axis=0))
        total = jnp.zeros((4 * wide + 4 * size, chans), F32)
        for a in range(3):
            total = total + dot(fields[a], one_ref[a])
        total = gelu(total)
        put(upper_ref, 0, total[:wide])
        put(upper_ref, wide, total[wide : 2 * wide])
        put(lower_ref, below * wide, total[2 * wide : 3 * wide])
        put(lower_ref, (below + 1) * wide, total[3 * wide : 4 * wide])
        for n in range(4):
            cols_scr[n] = total[4 * wide + n * size : 4 * wide + (n + 1) * size]
        last = wide - 16

        def patch(r, _):
            fixes = [cols_scr[n, pl.ds(r, 1), :] for n in range(4)]
            begin = pl.multiple_of((r + 2) * wide, 16)
            for b in range(3):
                lanes = slice(b * chans, (b + 1) * chans)
                for start in (0, last):
                    edits = [
                        (col - b - start, fix)
                        for col, fix in zip((0, 1, cols, cols + 1), fixes)
                        if 0 <= col - b - start < 16
                    ]
                    if edits:
                        value = upper_ref[pl.ds(begin + start, 16), lanes].astype(F32)
                        for at, fix in edits:
                            value = jnp.where(short_id == at, fix, value)
                        upper_ref[pl.ds(begin + start, 16), lanes] = value.astype(BF)
            return 0

        lax.fori_loop(0, above, patch, 0, unroll=10)

    def second(ref, first_group):
        begin = pl.multiple_of((group - first_group) * block, 16)
        total = taps(ref, begin, block, wide, two_ref)
        own = first_ref[pl.ds(group * rows, rows)].reshape(block, chans).astype(F32)
        total = total + pltpu.roll(own, block - 2, axis=0)
        result = total.astype(BF)
        for i in range(rows):
            out_ref[i] = result[i * wide : i * wide + cols]

    pl.when(group < above // rows)(lambda: second(upper_ref, 0))
    pl.when(group >= above // rows)(lambda: second(lower_ref, above // rows))


def finished(upper, lower, first, sides, one, two, cols, lat_count):
    lat_rows, wide, chans = first.shape
    whole = pl.BlockSpec(memory_space=pltpu.VMEM)
    out, _, _ = pl.pallas_call(
        functools.partial(finish_kernel, lat_count),
        grid=(lat_rows // FINISH,),
        out_shape=(
            jax.ShapeDtypeStruct((lat_rows, cols, chans), BF),
            jax.ShapeDtypeStruct(upper.shape, BF),
            jax.ShapeDtypeStruct(lower.shape, BF),
        ),
        in_specs=[whole] * (5 + len(sides)),
        out_specs=(pl.BlockSpec((FINISH, cols, chans), lambda g: (g, 0, 0)), whole, whole),
        input_output_aliases={0: 1, 1: 2},
        scratch_shapes=[
            pltpu.VMEM((8 * wide, 3 * chans), BF),
            pltpu.VMEM((4, -(-UPPER // 16) * 16, chans), F32),
        ],
        compiler_params=params(26),
    )(upper, lower, first, *sides, one, two)
    return out


def row_pairs(lat_count, lon_count):
    half = lon_count // 2

    def flat(lat, lon):
        return lat * lon_count + lon % lon_count

    inner, outer = [], []
    for lon in range(lon_count):
        for lat in range(0, lat_count, 2):
            inner += [(flat(lat, lon), flat(lat + 1, lon)), (flat(lat + 1, lon), flat(lat, lon))]
        for lat in range(1, lat_count - 1, 2):
            outer += [(flat(lat, lon), flat(lat + 1, lon)), (flat(lat + 1, lon), flat(lat, lon))]
        outer += [(flat(lat, lon), flat(lat, lon + half)) for lat in (0, lat_count - 1)]
    return inner, outer


def shards(
    obs_features,
    obs_dest,
    obs_cells,
    obs_gauss,
    row_counts,
    background,
    w_in,
    w_bg,
    w_dens,
    conv_one,
    conv_two,
):
    nrows, nfeat = obs_features.shape
    lat_rows, cols, chans = background.shape
    axes = ("lat", "lon")
    devices = lax.axis_size(axes)
    lat_count, lon_count = lax.axis_size("lat"), lax.axis_size("lon")
    cap = 2 * nrows // devices
    wide = -(-(cols + 4) // 16) * 16
    send = pack(
        row_counts, obs_dest.reshape(1, nrows), obs_cells.T, obs_gauss.T, obs_features, devices, lon_count, cap, cols,
        lat_rows // BAND,
    )
    paired = send.shape
    send = send.reshape(devices, cap + META, nfeat)
    recv = lax.all_to_all(send, axes, split_axis=0, concat_axis=0, tiled=True).reshape(paired)
    back = projected(background, w_bg, wide)
    first, own_west, own_east, inner_row, outer_row = gridded(
        recv, back, w_in, w_dens.reshape(1, chans), cap, wide, lat_rows, cols
    )
    west = lax.ppermute(own_east, "lon", [(i, (i + 1) % lon_count) for i in range(lon_count)])
    east = lax.ppermute(own_west, "lon", [((i + 1) % lon_count, i) for i in range(lon_count)])
    one = conv_one.reshape(3, 3 * chans, chans)
    two = conv_two.reshape(3, 3 * chans, chans)
    upper = upper_part(first, one, own_west, UPPER)
    inner_row, outer_row = bordered(inner_row, outer_row, west, east, upper, lat_rows, cols)
    inner, outer = row_pairs(lat_count, lon_count)
    lower = lower_part(first, one, west, east, inner_row, lat_rows - UPPER, cols)
    inner_row = lax.ppermute(inner_row, axes, inner)
    outer_row = lax.ppermute(outer_row, axes, outer)
    sides = (own_west, own_east, west, east, inner_row, outer_row)
    return finished(upper, lower, first, sides, one, two, cols, lat_count)


def solution(mesh):
    rows = P(("lat", "lon"), None)
    in_specs = (rows, rows, rows, rows, P(("lat", "lon")), P("lat", "lon", None), P(), P(), P(), P(), P())
    return jax.shard_map(
        shards, mesh=mesh, in_specs=in_specs, out_specs=P("lat", "lon", None), check_vma=False
    )
```

```python
import functools

import jax
import jax.numpy as jnp
from jax import lax
from jax.experimental import pallas as pl
from jax.experimental.pallas import tpu as pltpu
from jax.sharding import PartitionSpec as P

KCELL = 4
GBINS = 32
META = 8
GROUP = 6
BAND = 18
CHUNK = 256
HEAD = 768
FINISH = 15
UPPER = 30
BF = jnp.bfloat16
F32 = jnp.float32


def params(mib):
    return pltpu.CompilerParams(vmem_limit_bytes=mib * 1024 * 1024)


def gelu(x):
    scale = 0.7978845608028654
    half = 0.5 * x
    return half + half * jnp.tanh(x * (scale + (scale * 0.044715) * (x * x)))


def dot(a, b):
    return jnp.dot(a, b, preferred_element_type=F32)


def pack_kernel(
    devices, lon_count, cap, cols, bands, count_ref, dest_ref, cells_ref, gauss_ref, feat_hbm, send_hbm,
    ext_ref, hot_ref, sorted_ref, place_ref, place_smem, send_ref, sem, feat_sem, send_sems,
):
    nrows, nfeat = feat_hbm.shape
    fetch = pltpu.make_async_copy(feat_hbm, ext_ref.at[:, pl.ds(0, nfeat)], feat_sem)
    fetch.start()
    step = 256
    classes = 2 * bands
    kinds = devices * classes
    dest = dest_ref[...]
    row_id = lax.broadcasted_iota(jnp.int32, (1, nrows), 1)
    base = cells_ref[0:1, :].astype(F32)
    lat = jnp.floor((base + 0.5) * (1.0 / cols))
    lon = base - lat * cols
    band = jnp.floor((lat + 0.5) * (1.0 / BAND))
    kind = 2.0 * band + (lat == band * BAND + (BAND - 1)).astype(F32)
    kind = dest * classes + kind.astype(jnp.int32)
    kind = jnp.where(row_id < count_ref[0], kind, kinds)
    ratio = gauss_ref[...].astype(F32) * (1.0 / GBINS)
    weight = jnp.exp(-3.0 * ratio * ratio)
    meta = jnp.concatenate([lat, lon, weight, jnp.zeros((nfeat - 2 - KCELL, nrows), F32)], axis=0)
    ext_ref[:, nfeat:] = meta.T.astype(BF)
    hot_ref[...] = (lax.broadcasted_iota(jnp.int32, (kinds, nrows), 0) == kind).astype(F32).astype(BF)
    counts = dot(hot_ref[...], jnp.ones((nrows, nfeat), BF))
    ka = lax.broadcasted_iota(jnp.int32, (kinds, kinds), 0)
    kb = lax.broadcasted_iota(jnp.int32, (kinds, kinds), 1)
    da, db = ka // classes, kb // classes
    within = ((da == db) & (kb < ka)).astype(F32).astype(BF)
    together = (da == db).astype(F32).astype(BF)
    ahead = ((db < da) & (kb % classes == 0)).astype(F32).astype(BF)
    loads = dot(together, counts.astype(BF))
    padded = jnp.floor((loads + 7.0) * 0.125) * 8.0
    begins = dot(ahead, padded.astype(BF))
    mine = begins + dot(within, counts.astype(BF))
    kind_id = lax.broadcasted_iota(jnp.int32, (kinds, nfeat), 0)
    lane_id = lax.broadcasted_iota(jnp.int32, (kinds, nfeat), 1)
    lead = kind_id == lane_id * classes
    place_ref[0:1, :] = jnp.sum(jnp.where(lead, begins, 0.0), axis=0, keepdims=True).astype(jnp.int32)
    place_ref[1:2, :] = jnp.sum(jnp.where(lead, loads, 0.0), axis=0, keepdims=True).astype(jnp.int32)
    copy = pltpu.make_async_copy(place_ref, place_smem, sem)
    copy.start()
    earlier = (
        lax.broadcasted_iota(jnp.int32, (step, step), 0) < lax.broadcasted_iota(jnp.int32, (step, step), 1)
    ).astype(F32).astype(BF)
    carry = mine[:, 0:1]
    places = []
    for begin in range(0, nrows, step):
        hot = hot_ref[:, begin : begin + step]
        before = dot(hot, earlier) + carry
        hot = hot.astype(F32)
        places.append(
            jnp.sum(before * hot, axis=0, keepdims=True) + jnp.sum(hot, axis=0, keepdims=True) - 1.0
        )
        carry = carry + jnp.sum(hot, axis=1, keepdims=True)
    place = jnp.concatenate(places, axis=1)
    live = row_id < count_ref[0]
    place = jnp.where(live, place, -1.0)
    slot = lax.broadcasted_iota(jnp.int32, (step, nrows), 0).astype(F32)
    span = sorted_ref.shape[0]
    fetch.wait()
    for k in range(-(-(nrows + 8 * devices) // step)):
        pick = (slot == place - k * step).astype(F32).astype(BF)
        sorted_ref[k * step : (k + 1) * step, :] = dot(pick, ext_ref[...])
    tail = -(-(nrows + 8 * devices) // step) * step
    sorted_ref[tail:span, :] = jnp.zeros((span - tail, 2 * nfeat), F32)
    copy.wait()
    side_lane = lax.broadcasted_iota(jnp.int32, (META, nfeat), 1)
    odd = (lax.axis_index("lat") * lon_count + lax.axis_index("lon")) % 2 == 1

    def one(d):
        begin = pl.multiple_of(place_smem[0, d], 8)
        got = sorted_ref[pl.ds(begin, cap), :]
        side = got[:, nfeat:]
        if cap < nfeat:
            side = jnp.concatenate([side, jnp.zeros((nfeat - cap, nfeat), F32)], axis=0)
        return got[:, :nfeat], jnp.where(side_lane < place_smem[1, d], side.T[0:META], 0.0)

    def pair(p, _):
        (rows_a, side_a), (rows_b, side_b) = one(2 * p), one(2 * p + 1)
        plain = jnp.concatenate([rows_a, side_a, rows_b, side_b], axis=0)
        turned = jnp.concatenate([side_a, rows_a, side_b, rows_b], axis=0)
        send_ref[p] = jnp.where(odd, turned, plain).astype(BF)
        pltpu.make_async_copy(send_ref.at[p], send_hbm.at[p], send_sems.at[p]).start()
        return 0

    def sent(p, _):
        pltpu.make_async_copy(send_ref.at[p], send_hbm.at[p], send_sems.at[p]).wait()
        return 0

    lax.fori_loop(0, devices // 2, pair, 0, unroll=2)
    lax.fori_loop(0, devices // 2, sent, 0)


def pack(count, dest, cells, gauss, feats, devices, lon_count, cap, cols, bands):
    nrows, nfeat = feats.shape
    span = -(-(nrows + 8 * devices) // 256) * 256 + cap
    kinds = devices * 2 * bands
    return pl.pallas_call(
        functools.partial(pack_kernel, devices, lon_count, cap, cols, bands),
        out_shape=jax.ShapeDtypeStruct((devices // 2, 2 * (cap + META), nfeat), BF),
        in_specs=[pl.BlockSpec(memory_space=pltpu.SMEM)] + [pl.BlockSpec(memory_space=pltpu.VMEM)] * 3
        + [pl.BlockSpec(memory_space=pl.ANY)],
        out_specs=pl.BlockSpec(memory_space=pl.ANY),
        scratch_shapes=[
            pltpu.VMEM((nrows, 2 * nfeat), BF),
            pltpu.VMEM((kinds, nrows), BF),
            pltpu.VMEM((span, 2 * nfeat), F32),
            pltpu.VMEM((8, nfeat), jnp.int32),
            pltpu.SMEM((8, nfeat), jnp.int32),
            pltpu.VMEM((devices // 2, 2 * (cap + META), nfeat), BF),
            pltpu.SemaphoreType.DMA,
            pltpu.SemaphoreType.DMA,
            pltpu.SemaphoreType.DMA((devices // 2,)),
        ],
        compiler_params=params(56),
    )(count, dest, cells, gauss, feats)


def back_kernel(wide, back_ref, w_bg_ref, out_ref, scr):
    rows, cols, chans = back_ref.shape
    for i in range(rows):
        scr[i * wide : i * wide + cols, :] = back_ref[i]
    out_ref[...] = pltpu.roll(dot(scr[...], w_bg_ref[...]), 2, axis=0)


def projected(background, w_bg, wide):
    lat_rows, cols, chans = background.shape
    length = max(lat_rows * wide, 1 << 16) + 16
    return pl.pallas_call(
        functools.partial(back_kernel, wide),
        grid=(lat_rows // BAND,),
        out_shape=pltpu.HBM((length, chans), F32),
        in_specs=[
            pl.BlockSpec((BAND, cols, chans), lambda g: (g, 0, 0)),
            pl.BlockSpec(memory_space=pltpu.VMEM),
        ],
        out_specs=pl.BlockSpec((BAND * wide, chans), lambda g: (g, 0)),
        scratch_shapes=[pltpu.VMEM((BAND * wide, chans), BF)],
        compiler_params=params(24),
    )(background, w_bg)


def grid_kernel(
    devices, cap, wide, cols, lat_bands, recv_ref, back_hbm, w_in_hbm, w_dens_hbm,
    first_ref, west_ref, east_ref, inner_ref, outer_ref,
    rows_ref, sides_ref, lats_ref, feat_ref, meta_ref, acc_ref, edge_scr, ends_ref, ends_smem, sem,
    back_ref, w_in_ref, w_dens_ref, sems,
):
    band = pl.program_id(0)
    bands = pl.num_programs(0)
    nfeat = recv_ref.shape[2]
    lat_rows, _, chans = first_ref.shape
    rows = lat_rows // lat_bands
    slots = devices * cap
    span = rows * wide

    def fetch(b):
        begin = pl.multiple_of(b * span, 16)
        return pltpu.make_async_copy(back_hbm.at[pl.ds(begin, span), :], back_ref.at[b], sems.at[b])

    loads = [
        pltpu.make_async_copy(w_in_hbm, w_in_ref, sems.at[lat_bands]),
        pltpu.make_async_copy(w_dens_hbm, w_dens_ref, sems.at[lat_bands + 1]),
    ]

    @pl.when(band == 0)
    def _():
        for b in range(lat_bands):
            fetch(b).start()
        for load in loads:
            load.start()

        def read(p, _):
            both = recv_ref[p, cap : cap + 2 * META, :].astype(F32)
            for s, side in ((2 * p, both[:META]), (2 * p + 1, both[META:])):
                sides_ref[s] = side
                lats_ref[pl.ds(s, 1), :] = jnp.where(side[2:3] > 0, side[0:1], 1e6)
            return 0

        lax.fori_loop(0, devices // 2, read, 0, unroll=8)
        lats = lats_ref[...]
        lane = lax.broadcasted_iota(jnp.int32, (devices, nfeat), 1)
        ends = jnp.zeros((devices, nfeat), F32)
        for b in range(lat_bands):
            low = jnp.sum((lats < b * rows - 1.0).astype(F32), axis=1, keepdims=True)
            high = jnp.sum((lats < (b + 1.0) * rows).astype(F32), axis=1, keepdims=True)
            ends = jnp.where(lane == 2 * b, low, jnp.where(lane == 2 * b + 1, high, ends))
        ends_ref[...] = ends.astype(jnp.int32)
        copy = pltpu.make_async_copy(ends_ref, ends_smem, sem)
        copy.start()
        feat_ref[...] = jnp.zeros(feat_ref.shape, F32)
        rows_ref[slots:, :] = jnp.zeros((rows_ref.shape[0] - slots, nfeat), F32)

        def widen(p, _):
            begin = pl.multiple_of(2 * p * cap, cap)
            rows_ref[pl.ds(begin, cap), :] = recv_ref[p, 0:cap, :].astype(F32)
            rows_ref[pl.ds(begin + cap, cap), :] = recv_ref[p, cap + 2 * META :, :].astype(F32)
            return 0

        lax.fori_loop(0, devices // 2, widen, 0, unroll=2)
        copy.wait()

    meta_ref[...] = jnp.zeros(meta_ref.shape, F32)
    lane = lax.broadcasted_iota(jnp.int32, (META, nfeat), 1)

    def compact(s, out):
        out = pl.multiple_of(out, 8)
        low, high = ends_smem[s, 2 * band], ends_smem[s, 2 * band + 1]
        source = pl.multiple_of(low // 8 * 8, 8)
        feat_ref[pl.ds(out, cap), :] = rows_ref[pl.ds(pl.multiple_of(s * cap + source, 8), cap), :]
        side = sides_ref[s]
        side = jnp.where((lane >= low) & (lane < high), side, 0.0)
        shift = out - source + nfeat
        tile, shift = shift // nfeat, shift % nfeat
        moved = pltpu.roll(side, shift, axis=1)
        meta_ref[tile] += jnp.where(lane >= shift, moved, 0.0)
        meta_ref[tile + 1] += jnp.where(lane < shift, moved, 0.0)
        return out + (high - source + 7) // 8 * 8

    total = lax.fori_loop(0, devices, compact, 0, unroll=16)

    def piece(begin, size):
        begin = pl.multiple_of(begin, CHUNK)
        col_id = lax.broadcasted_iota(jnp.int32, (wide, size), 0).astype(F32)
        side = jnp.concatenate([meta_ref[1 + begin // nfeat + q] for q in range(size // nfeat)], axis=1)
        lat, lon = side[0:1], side[1:2]
        here = (col_id == lon + 2.0).astype(F32).astype(BF)
        after = (col_id == lon + 3.0).astype(F32).astype(BF)
        parts = []
        for i in range(rows):
            row = (band * rows + i).astype(F32)
            same, above = lat == row, lat == row - 1.0
            left = jnp.where(same, side[2:3], jnp.where(above, side[4:5], 0.0)).astype(BF)
            right = jnp.where(same, side[3:4], jnp.where(above, side[5:6], 0.0)).astype(BF)
            parts.append(here * left + after * right)
        spread = jnp.concatenate(parts, axis=0)
        values = jnp.concatenate(
            [feat_ref[pl.ds(begin, size), :].astype(BF), jnp.ones((size, nfeat), BF)], axis=1
        )
        return dot(spread, values)

    def more(k, _):
        acc_ref[...] += piece(k * CHUNK, CHUNK)
        return 0

    acc_ref[...] = piece(0, HEAD)
    lax.fori_loop(HEAD // CHUNK, (total + CHUNK - 1) // CHUNK, more, 0)
    fetch(band).wait()

    @pl.when(band == 0)
    def _():
        for load in loads:
            load.wait()

    for g in range(0, rows, GROUP):
        sums = acc_ref[g * wide : (g + GROUP) * wide, :]
        start = back_ref[band, g * wide : (g + GROUP) * wide, :]
        density = sums[:, nfeat:]
        normalized = (sums[:, :nfeat] / (density + 1.0)).astype(BF)
        start = start + dot(normalized, w_in_ref[...])
        start = start + jnp.concatenate([density] * (chans // nfeat), axis=1) * w_dens_ref[...]
        first = start.astype(BF)
        for i in range(GROUP):
            first_ref[band * rows + g + i] = first[i * wide : (i + 1) * wide]
            for k, col in enumerate((2, 3, cols, cols + 1)):
                edge_scr[k, pl.ds(band * rows + g + i, 1), :] = start[i * wide + col : i * wide + col + 1]

    @pl.when(band == bands - 1)
    def _():
        west_ref[...] = edge_scr[0:2].astype(BF)
        east_ref[...] = edge_scr[2:4].astype(BF)
        even = lax.axis_index("lat") % 2 == 0
        for k in range(2):
            top, bottom = first_ref[k].astype(F32), first_ref[lat_rows - 1 - k].astype(F32)
            inner = jnp.where(even, bottom, top).astype(BF)
            outer = jnp.where(even, top, bottom).astype(BF)
            inner_ref[k] = inner
            outer_ref[k] = outer


def gridded(recv, back, w_in, w_dens, cap, wide, lat_rows, cols):
    devices, nfeat = 2 * recv.shape[0], recv.shape[2]
    chans = back.shape[1]
    slots = devices * cap
    tall = -(-lat_rows // 16) * 16
    whole = pl.BlockSpec(memory_space=pltpu.VMEM)
    return pl.pallas_call(
        functools.partial(grid_kernel, devices, cap, wide, cols, lat_rows // BAND),
        grid=(lat_rows // BAND,),
        out_shape=(
            jax.ShapeDtypeStruct((lat_rows, wide, chans), BF),
            jax.ShapeDtypeStruct((2, tall, chans), BF),
            jax.ShapeDtypeStruct((2, tall, chans), BF),
            jax.ShapeDtypeStruct((2, wide, chans), BF),
            jax.ShapeDtypeStruct((2, wide, chans), BF),
        ),
        in_specs=[whole] + [pl.BlockSpec(memory_space=pltpu.HBM)] * 3,
        out_specs=(whole,) * 5,
        scratch_shapes=[
            pltpu.VMEM((slots + cap, nfeat), F32),
            pltpu.VMEM((devices, META, nfeat), F32),
            pltpu.VMEM((devices, nfeat), F32),
            pltpu.VMEM((slots + cap + HEAD, nfeat), F32),
            pltpu.VMEM((slots // nfeat + 8, META, nfeat), F32),
            pltpu.VMEM((BAND * wide, 2 * nfeat), F32),
            pltpu.VMEM((4, tall, chans), F32),
            pltpu.VMEM((devices, nfeat), jnp.int32),
            pltpu.SMEM((devices, nfeat), jnp.int32),
            pltpu.SemaphoreType.DMA,
            pltpu.VMEM((lat_rows // BAND, BAND * wide, chans), F32),
            pltpu.VMEM(w_in.shape, BF),
            pltpu.VMEM(w_dens.shape, F32),
            pltpu.SemaphoreType.DMA((lat_rows // BAND + 2,)),
        ],
        compiler_params=params(42),
    )(recv, back, w_in, w_dens)


def put(ref, begin, value):
    size, chans = value.shape
    for b in range(3):
        part = value if b == 0 else pltpu.roll(value, size - b, axis=0)
        ref[pl.ds(begin, size), b * chans : (b + 1) * chans] = part.astype(BF)


def taps(ref, begin, size, wide, w_ref):
    field = jnp.concatenate([ref[pl.ds(begin + a * wide, size), :] for a in range(3)], axis=1)
    return dot(field, w_ref[...].reshape(field.shape[1], w_ref.shape[2]))


def border_kernel(lat_rows, cols, inner_ref, outer_ref, west_ref, east_ref, after_ref, inner_out, outer_out):
    _, wide, chans = inner_ref.shape
    even = lax.axis_index("lat") % 2 == 0
    row_id = lax.broadcasted_iota(jnp.int32, (wide, chans), 0)
    sides = [west_ref[0], west_ref[1], east_ref[0], east_ref[1]]
    sides = [side.astype(F32) for side in sides]
    for k in range(2):
        inner, outer = inner_ref[k].astype(F32), outer_ref[k].astype(F32)
        for side, col in zip(sides, (0, 1, cols + 2, cols + 3)):
            top = side[k : k + 1]
            bottom = side[lat_rows - 1 - k : lat_rows - k]
            inner = jnp.where(row_id == col, jnp.where(even, bottom, top), inner)
            outer = jnp.where(row_id == col, jnp.where(even, top, bottom), outer)
        inner_out[k] = inner.astype(BF)
        outer_out[k] = outer.astype(BF)


def bordered(inner, outer, west, east, after, lat_rows, cols):
    whole = pl.BlockSpec(memory_space=pltpu.VMEM)
    shape = jax.ShapeDtypeStruct(inner.shape, BF)
    return pl.pallas_call(
        functools.partial(border_kernel, lat_rows, cols),
        out_shape=(shape, shape),
        in_specs=[whole] * 4 + [pl.BlockSpec(memory_space=pl.ANY)],
        out_specs=(whole, whole),
        compiler_params=params(24),
    )(inner, outer, west, east, after)


def with_sides(value, sides, cols):
    wide, chans = value.shape
    last = wide - 16
    row_id = lax.broadcasted_iota(jnp.int32, (16, chans), 0)
    head, tail = value[:16], value[last:]
    for k in range(2):
        head = jnp.where(row_id == k, sides[k], head)
        tail = jnp.where(row_id == cols + 2 + k - last, sides[2 + k], tail)
    return jnp.concatenate([head, value[16:last], tail], axis=0)


def convolve_rows(field, one_ref, hid_ref, place, count, wide):
    size = FINISH * wide

    def hidden(g, _):
        begin = pl.multiple_of(g * size, 16)
        total = taps(field, begin, size, wide, one_ref)
        put(hid_ref, pl.multiple_of(begin + place * wide, 16), gelu(total))
        return 0

    lax.fori_loop(0, count // FINISH, hidden, 0)


def upper_kernel(first_ref, one_ref, after_ref, hid_ref, field):
    wide = first_ref.shape[1]
    count = field.shape[0] // wide

    def load(r, _):
        put(field, pl.multiple_of(r * wide, 16), first_ref[r].astype(F32))
        return 0

    lax.fori_loop(0, count, load, 0, unroll=4)
    convolve_rows(field, one_ref, hid_ref, 2, count - 2, wide)


def lower_kernel(cols, first_ref, one_ref, west_ref, east_ref, after_ref, hid_ref, field, side_scr):
    lat_rows, wide, _ = first_ref.shape
    count = field.shape[0] // wide
    lead = lat_rows - count
    side_scr[0:2] = west_ref[...].astype(F32)
    side_scr[2:4] = east_ref[...].astype(F32)

    def load(r, _):
        sides = [side_scr[k, pl.ds(lead + r, 1), :] for k in range(4)]
        value = with_sides(first_ref[lead + r].astype(F32), sides, cols)
        put(field, pl.multiple_of(r * wide, 16), value)
        return 0

    lax.fori_loop(0, count, load, 0, unroll=2)
    convolve_rows(field, one_ref, hid_ref, 0, count - 2, wide)


def upper_part(first, one, after, rows):
    _, wide, chans = first.shape
    whole = pl.BlockSpec(memory_space=pltpu.VMEM)
    shape = ((rows + 2) * wide, 3 * chans)
    return pl.pallas_call(
        upper_kernel,
        out_shape=jax.ShapeDtypeStruct(shape, BF),
        in_specs=[whole, whole, pl.BlockSpec(memory_space=pl.ANY)],
        out_specs=whole,
        scratch_shapes=[pltpu.VMEM(shape, BF)],
        compiler_params=params(24),
    )(first, one, after)


def lower_part(first, one, west, east, after, rows, cols):
    _, wide, chans = first.shape
    whole = pl.BlockSpec(memory_space=pltpu.VMEM)
    shape = ((rows + 2) * wide, 3 * chans)
    return pl.pallas_call(
        functools.partial(lower_kernel, cols),
        out_shape=jax.ShapeDtypeStruct(shape, BF),
        in_specs=[whole] * 4 + [pl.BlockSpec(memory_space=pl.ANY)],
        out_specs=whole,
        scratch_shapes=[pltpu.VMEM(shape, BF), pltpu.VMEM((4, west.shape[1], chans), F32)],
        compiler_params=params(24),
    )(first, one, west, east, after)


def finish_kernel(
    lat_count, upper_in, lower_in, first_ref, own_west, own_east, west_ref, east_ref, inner_ref, outer_ref,
    one_ref, two_ref, out_ref, upper_ref, lower_ref, rim, cols_scr,
):
    group = pl.program_id(0)
    lat_rows, wide, chans = first_ref.shape
    rows, cols, _ = out_ref.shape
    block = rows * wide
    above = upper_ref.shape[0] // wide - 2
    below = lat_rows - above

    @pl.when(group == 0)
    def _():
        lat_index = lax.axis_index("lat")
        even = lat_index % 2 == 0
        short_id = lax.broadcasted_iota(jnp.int32, (16, chans), 0)
        lines = [west_ref[0], west_ref[1], own_west[0], own_west[1]]
        lines += [own_east[0], own_east[1], east_ref[0], east_ref[1]]
        lines = [line.astype(F32) for line in lines]

        def edge_row(north, k):
            return jnp.where(even == north, outer_ref[k].astype(F32), inner_ref[k].astype(F32))

        def own_row(r):
            sides = [lines[n][r : r + 1] for n in (0, 1, 6, 7)]
            return with_sides(first_ref[r].astype(F32), sides, cols)

        rims = [edge_row(True, 1), edge_row(True, 0), own_row(0), own_row(1)]
        rims += [own_row(lat_rows - 2), own_row(lat_rows - 1), edge_row(False, 0), edge_row(False, 1)]
        for n, line in enumerate(rims):
            put(rim, n * wide, line)
        size = cols_scr.shape[1]
        fields = []
        for a in range(3):
            top = jnp.where(lat_index == 0, 2 - a, a)
            bottom = jnp.where(lat_index == lat_count - 1, 7 - a, 5 + a)
            parts = [
                rim[pl.ds(pl.multiple_of(n * wide, 16), wide), :] for n in (top, 1 + a, 4 + a, bottom)
            ]
            for n in (0, 1, 4, 5):
                window = [lines[n + b][a : a + size].astype(BF) for b in range(3)]
                parts.append(jnp.concatenate(window, axis=1))
            fields.append(jnp.concatenate(parts, axis=0))
        total = jnp.zeros((4 * wide + 4 * size, chans), F32)
        for a in range(3):
            total = total + dot(fields[a], one_ref[a])
        total = gelu(total)
        put(upper_ref, 0, total[:wide])
        put(upper_ref, wide, total[wide : 2 * wide])
        put(lower_ref, below * wide, total[2 * wide : 3 * wide])
        put(lower_ref, (below + 1) * wide, total[3 * wide : 4 * wide])
        for n in range(4):
            cols_scr[n] = total[4 * wide + n * size : 4 * wide + (n + 1) * size]
        last = wide - 16

        def patch(r, _):
            fixes = [cols_scr[n, pl.ds(r, 1), :] for n in range(4)]
            begin = pl.multiple_of((r + 2) * wide, 16)
            for b in range(3):
                lanes = slice(b * chans, (b + 1) * chans)
                for start in (0, last):
                    edits = [
                        (col - b - start, fix)
                        for col, fix in zip((0, 1, cols, cols + 1), fixes)
                        if 0 <= col - b - start < 16
                    ]
                    if edits:
                        value = upper_ref[pl.ds(begin + start, 16), lanes].astype(F32)
                        for at, fix in edits:
                            value = jnp.where(short_id == at, fix, value)
                        upper_ref[pl.ds(begin + start, 16), lanes] = value.astype(BF)
            return 0

        lax.fori_loop(0, above, patch, 0, unroll=10)

    def second(ref, first_group):
        begin = pl.multiple_of((group - first_group) * block, 16)
        total = taps(ref, begin, block, wide, two_ref)
        own = first_ref[pl.ds(group * rows, rows)].reshape(block, chans).astype(F32)
        total = total + pltpu.roll(own, block - 2, axis=0)
        result = total.astype(BF)
        for i in range(rows):
            out_ref[i] = result[i * wide : i * wide + cols]

    pl.when(group < above // rows)(lambda: second(upper_ref, 0))
    pl.when(group >= above // rows)(lambda: second(lower_ref, above // rows))


def finished(upper, lower, first, sides, one, two, cols, lat_count):
    lat_rows, wide, chans = first.shape
    whole = pl.BlockSpec(memory_space=pltpu.VMEM)
    out, _, _ = pl.pallas_call(
        functools.partial(finish_kernel, lat_count),
        grid=(lat_rows // FINISH,),
        out_shape=(
            jax.ShapeDtypeStruct((lat_rows, cols, chans), BF),
            jax.ShapeDtypeStruct(upper.shape, BF),
            jax.ShapeDtypeStruct(lower.shape, BF),
        ),
        in_specs=[whole] * (5 + len(sides)),
        out_specs=(pl.BlockSpec((FINISH, cols, chans), lambda g: (g, 0, 0)), whole, whole),
        input_output_aliases={0: 1, 1: 2},
        scratch_shapes=[
            pltpu.VMEM((8 * wide, 3 * chans), BF),
            pltpu.VMEM((4, -(-UPPER // 16) * 16, chans), F32),
        ],
        compiler_params=params(26),
    )(upper, lower, first, *sides, one, two)
    return out


def row_pairs(lat_count, lon_count):
    half = lon_count // 2

    def flat(lat, lon):
        return lat * lon_count + lon % lon_count

    inner, outer = [], []
    for lon in range(lon_count):
        for lat in range(0, lat_count, 2):
            inner += [(flat(lat, lon), flat(lat + 1, lon)), (flat(lat + 1, lon), flat(lat, lon))]
        for lat in range(1, lat_count - 1, 2):
            outer += [(flat(lat, lon), flat(lat + 1, lon)), (flat(lat + 1, lon), flat(lat, lon))]
        outer += [(flat(lat, lon), flat(lat, lon + half)) for lat in (0, lat_count - 1)]
    return inner, outer


def shards(
    obs_features,
    obs_dest,
    obs_cells,
    obs_gauss,
    row_counts,
    background,
    w_in,
    w_bg,
    w_dens,
    conv_one,
    conv_two,
):
    nrows, nfeat = obs_features.shape
    lat_rows, cols, chans = background.shape
    axes = ("lat", "lon")
    devices = lax.axis_size(axes)
    lat_count, lon_count = lax.axis_size("lat"), lax.axis_size("lon")
    cap = 2 * nrows // devices
    wide = -(-(cols + 4) // 16) * 16
    send = pack(
        row_counts, obs_dest.reshape(1, nrows), obs_cells.T, obs_gauss.T, obs_features, devices, lon_count, cap, cols,
        lat_rows // BAND,
    )
    paired = send.shape
    send = send.reshape(devices, cap + META, nfeat)
    recv = lax.all_to_all(send, axes, split_axis=0, concat_axis=0, tiled=True).reshape(paired)
    back = projected(background, w_bg, wide)
    first, own_west, own_east, inner_row, outer_row = gridded(
        recv, back, w_in, w_dens.reshape(1, chans), cap, wide, lat_rows, cols
    )
    west = lax.ppermute(own_east, "lon", [(i, (i + 1) % lon_count) for i in range(lon_count)])
    east = lax.ppermute(own_west, "lon", [((i + 1) % lon_count, i) for i in range(lon_count)])
    one = conv_one.reshape(3, 3 * chans, chans)
    two = conv_two.reshape(3, 3 * chans, chans)
    upper = upper_part(first, one, own_west, UPPER)
    inner_row, outer_row = bordered(inner_row, outer_row, west, east, upper, lat_rows, cols)
    inner, outer = row_pairs(lat_count, lon_count)
    lower = lower_part(first, one, west, east, inner_row, lat_rows - UPPER, cols)
    inner_row = lax.ppermute(inner_row, axes, inner)
    outer_row = lax.ppermute(outer_row, axes, outer)
    sides = (own_west, own_east, west, east, inner_row, outer_row)
    return finished(upper, lower, first, sides, one, two, cols, lat_count)


def solution(mesh):
    rows = P(("lat", "lon"), None)
    in_specs = (rows, rows, rows, rows, P(("lat", "lon")), P("lat", "lon", None), P(), P(), P(), P(), P())
    return jax.shard_map(
        shards, mesh=mesh, in_specs=in_specs, out_specs=P("lat", "lon", None), check_vma=False
    )
```

```python
import functools

import jax
import jax.numpy as jnp
from jax import lax
from jax.experimental import pallas as pl
from jax.experimental.pallas import tpu as pltpu
from jax.sharding import PartitionSpec as P

KCELL = 4
GBINS = 32
META = 8
GROUP = 6
BAND = 18
CHUNK = 256
HEAD = 768
FINISH = 15
UPPER = 30
BF = jnp.bfloat16
F32 = jnp.float32


def params(mib):
    return pltpu.CompilerParams(vmem_limit_bytes=mib * 1024 * 1024)


def gelu(x):
    scale = 0.7978845608028654
    half = 0.5 * x
    return half + half * jnp.tanh(x * (scale + (scale * 0.044715) * (x * x)))


def dot(a, b):
    return jnp.dot(a, b, preferred_element_type=F32)


def pack_kernel(
    devices, lon_count, cap, cols, bands, count_ref, dest_ref, cells_ref, gauss_ref, feat_hbm, send_hbm,
    ext_ref, hot_ref, sorted_ref, place_ref, place_smem, send_ref, sem, feat_sem, send_sems,
):
    nrows, nfeat = feat_hbm.shape
    fetch = pltpu.make_async_copy(feat_hbm, ext_ref.at[:, pl.ds(0, nfeat)], feat_sem)
    fetch.start()
    step = 256
    classes = 2 * bands
    kinds = devices * classes
    dest = dest_ref[...]
    row_id = lax.broadcasted_iota(jnp.int32, (1, nrows), 1)
    base = cells_ref[0:1, :].astype(F32)
    lat = jnp.floor((base + 0.5) * (1.0 / cols))
    lon = base - lat * cols
    band = jnp.floor((lat + 0.5) * (1.0 / BAND))
    kind = 2.0 * band + (lat == band * BAND + (BAND - 1)).astype(F32)
    kind = dest * classes + kind.astype(jnp.int32)
    kind = jnp.where(row_id < count_ref[0], kind, kinds)
    ratio = gauss_ref[...].astype(F32) * (1.0 / GBINS)
    weight = jnp.exp(-3.0 * ratio * ratio)
    meta = jnp.concatenate([lat, lon, weight, jnp.zeros((nfeat - 2 - KCELL, nrows), F32)], axis=0)
    ext_ref[:, nfeat:] = meta.T.astype(BF)
    hot_ref[...] = (lax.broadcasted_iota(jnp.int32, (kinds, nrows), 0) == kind).astype(F32).astype(BF)
    counts = dot(hot_ref[...], jnp.ones((nrows, nfeat), BF))
    ka = lax.broadcasted_iota(jnp.int32, (kinds, kinds), 0)
    kb = lax.broadcasted_iota(jnp.int32, (kinds, kinds), 1)
    da = lax.broadcasted_iota(jnp.int32, (kinds, 1), 0) // classes
    row = lax.broadcasted_iota(jnp.int32, (1, kinds), 1)
    db = row // classes
    within = ((da == db) & (kb < ka)).astype(F32).astype(BF)
    together = (da == db).astype(F32).astype(BF)
    ahead = ((db < da) & (row == db * classes)).astype(F32).astype(BF)
    loads = dot(together, counts.astype(BF))
    padded = jnp.floor((loads + 7.0) * 0.125) * 8.0
    begins = dot(ahead, padded.astype(BF))
    mine = begins + dot(within, counts.astype(BF))
    kind_id = lax.broadcasted_iota(jnp.int32, (kinds, nfeat), 0)
    lane_id = lax.broadcasted_iota(jnp.int32, (kinds, nfeat), 1)
    lead = kind_id == lane_id * classes
    place_ref[0:1, :] = jnp.sum(jnp.where(lead, begins, 0.0), axis=0, keepdims=True).astype(jnp.int32)
    place_ref[1:2, :] = jnp.sum(jnp.where(lead, loads, 0.0), axis=0, keepdims=True).astype(jnp.int32)
    copy = pltpu.make_async_copy(place_ref, place_smem, sem)
    copy.start()
    earlier = (
        lax.broadcasted_iota(jnp.int32, (step, step), 0) < lax.broadcasted_iota(jnp.int32, (step, step), 1)
    ).astype(F32).astype(BF)
    carry = mine[:, 0:1]
    places = []
    for begin in range(0, nrows, step):
        hot = hot_ref[:, begin : begin + step]
        before = dot(hot, earlier) + carry
        hot = hot.astype(F32)
        places.append(
            jnp.sum(before * hot, axis=0, keepdims=True) + jnp.sum(hot, axis=0, keepdims=True) - 1.0
        )
        carry = carry + jnp.sum(hot, axis=1, keepdims=True)
    place = jnp.concatenate(places, axis=1)
    live = row_id < count_ref[0]
    place = jnp.where(live, place, -1.0)
    slot = lax.broadcasted_iota(jnp.int32, (step, nrows), 0).astype(F32)
    span = sorted_ref.shape[0]
    fetch.wait()
    for k in range(-(-(nrows + 8 * devices) // step)):
        pick = (slot == place - k * step).astype(F32).astype(BF)
        sorted_ref[k * step : (k + 1) * step, :] = dot(pick, ext_ref[...])
    tail = -(-(nrows + 8 * devices) // step) * step
    sorted_ref[tail:span, :] = jnp.zeros((span - tail, 2 * nfeat), F32)
    copy.wait()
    side_lane = lax.broadcasted_iota(jnp.int32, (META, nfeat), 1)
    odd = (lax.axis_index("lat") * lon_count + lax.axis_index("lon")) % 2 == 1

    def one(d):
        begin = pl.multiple_of(place_smem[0, d], 8)
        got = sorted_ref[pl.ds(begin, cap), :]
        side = got[:, nfeat:]
        if cap < nfeat:
            side = jnp.concatenate([side, jnp.zeros((nfeat - cap, nfeat), F32)], axis=0)
        return got[:, :nfeat], jnp.where(side_lane < place_smem[1, d], side.T[0:META], 0.0)

    def pair(p, _):
        (rows_a, side_a), (rows_b, side_b) = one(2 * p), one(2 * p + 1)
        plain = jnp.concatenate([rows_a, side_a, rows_b, side_b], axis=0)
        turned = jnp.concatenate([side_a, rows_a, side_b, rows_b], axis=0)
        send_ref[p] = jnp.where(odd, turned, plain).astype(BF)
        pltpu.make_async_copy(send_ref.at[p], send_hbm.at[p], send_sems.at[p]).start()
        return 0

    def sent(p, _):
        pltpu.make_async_copy(send_ref.at[p], send_hbm.at[p], send_sems.at[p]).wait()
        return 0

    lax.fori_loop(0, devices // 2, pair, 0, unroll=2)
    lax.fori_loop(0, devices // 2, sent, 0)


def pack(count, dest, cells, gauss, feats, devices, lon_count, cap, cols, bands):
    nrows, nfeat = feats.shape
    span = -(-(nrows + 8 * devices) // 256) * 256 + cap
    kinds = devices * 2 * bands
    return pl.pallas_call(
        functools.partial(pack_kernel, devices, lon_count, cap, cols, bands),
        out_shape=jax.ShapeDtypeStruct((devices // 2, 2 * (cap + META), nfeat), BF),
        in_specs=[pl.BlockSpec(memory_space=pltpu.SMEM)] + [pl.BlockSpec(memory_space=pltpu.VMEM)] * 3
        + [pl.BlockSpec(memory_space=pl.ANY)],
        out_specs=pl.BlockSpec(memory_space=pl.ANY),
        scratch_shapes=[
            pltpu.VMEM((nrows, 2 * nfeat), BF),
            pltpu.VMEM((kinds, nrows), BF),
            pltpu.VMEM((span, 2 * nfeat), F32),
            pltpu.VMEM((8, nfeat), jnp.int32),
            pltpu.SMEM((8, nfeat), jnp.int32),
            pltpu.VMEM((devices // 2, 2 * (cap + META), nfeat), BF),
            pltpu.SemaphoreType.DMA,
            pltpu.SemaphoreType.DMA,
            pltpu.SemaphoreType.DMA((devices // 2,)),
        ],
        compiler_params=params(56),
    )(count, dest, cells, gauss, feats)


def back_kernel(wide, back_ref, w_bg_ref, out_ref, scr):
    rows, cols, chans = back_ref.shape
    for i in range(rows):
        scr[i * wide : i * wide + cols, :] = back_ref[i]
    out_ref[...] = pltpu.roll(dot(scr[...], w_bg_ref[...]), 2, axis=0)


def projected(background, w_bg, wide):
    lat_rows, cols, chans = background.shape
    length = max(lat_rows * wide, 1 << 16) + 16
    return pl.pallas_call(
        functools.partial(back_kernel, wide),
        grid=(lat_rows // BAND,),
        out_shape=pltpu.HBM((length, chans), F32),
        in_specs=[
            pl.BlockSpec((BAND, cols, chans), lambda g: (g, 0, 0)),
            pl.BlockSpec(memory_space=pltpu.VMEM),
        ],
        out_specs=pl.BlockSpec((BAND * wide, chans), lambda g: (g, 0)),
        scratch_shapes=[pltpu.VMEM((BAND * wide, chans), BF)],
        compiler_params=params(24),
    )(background, w_bg)


def grid_kernel(
    devices, cap, wide, cols, lat_bands, recv_ref, back_hbm, w_in_hbm, w_dens_hbm,
    first_ref, west_ref, east_ref, inner_ref, outer_ref,
    rows_ref, sides_ref, lats_ref, feat_ref, meta_ref, acc_ref, edge_scr, ends_ref, ends_smem, sem,
    back_ref, w_in_ref, w_dens_ref, sems,
):
    band = pl.program_id(0)
    bands = pl.num_programs(0)
    nfeat = recv_ref.shape[2]
    lat_rows, _, chans = first_ref.shape
    rows = lat_rows // lat_bands
    slots = devices * cap
    span = rows * wide

    def fetch(b):
        begin = pl.multiple_of(b * span, 16)
        return pltpu.make_async_copy(back_hbm.at[pl.ds(begin, span), :], back_ref.at[b], sems.at[b])

    loads = [
        pltpu.make_async_copy(w_in_hbm, w_in_ref, sems.at[lat_bands]),
        pltpu.make_async_copy(w_dens_hbm, w_dens_ref, sems.at[lat_bands + 1]),
    ]

    @pl.when(band == 0)
    def _():
        for b in range(lat_bands):
            fetch(b).start()
        for load in loads:
            load.start()

        def read(p, _):
            both = recv_ref[p, cap : cap + 2 * META, :].astype(F32)
            for s, side in ((2 * p, both[:META]), (2 * p + 1, both[META:])):
                sides_ref[s] = side
                lats_ref[pl.ds(s, 1), :] = jnp.where(side[2:3] > 0, side[0:1], 1e6)
            return 0

        lax.fori_loop(0, devices // 2, read, 0, unroll=8)
        lats = lats_ref[...]
        lane = lax.broadcasted_iota(jnp.int32, (devices, nfeat), 1)
        ends = jnp.zeros((devices, nfeat), F32)
        for b in range(lat_bands):
            low = jnp.sum((lats < b * rows - 1.0).astype(F32), axis=1, keepdims=True)
            high = jnp.sum((lats < (b + 1.0) * rows).astype(F32), axis=1, keepdims=True)
            ends = jnp.where(lane == 2 * b, low, jnp.where(lane == 2 * b + 1, high, ends))
        ends_ref[...] = ends.astype(jnp.int32)
        copy = pltpu.make_async_copy(ends_ref, ends_smem, sem)
        copy.start()
        feat_ref[...] = jnp.zeros(feat_ref.shape, F32)
        rows_ref[slots:, :] = jnp.zeros((rows_ref.shape[0] - slots, nfeat), F32)

        def widen(p, _):
            begin = pl.multiple_of(2 * p * cap, cap)
            rows_ref[pl.ds(begin, cap), :] = recv_ref[p, 0:cap, :].astype(F32)
            rows_ref[pl.ds(begin + cap, cap), :] = recv_ref[p, cap + 2 * META :, :].astype(F32)
            return 0

        lax.fori_loop(0, devices // 2, widen, 0, unroll=2)
        copy.wait()

    meta_ref[...] = jnp.zeros(meta_ref.shape, F32)
    lane = lax.broadcasted_iota(jnp.int32, (META, nfeat), 1)

    def compact(s, out):
        out = pl.multiple_of(out, 8)
        low, high = ends_smem[s, 2 * band], ends_smem[s, 2 * band + 1]
        source = pl.multiple_of(low & -8, 8)
        feat_ref[pl.ds(out, cap), :] = rows_ref[pl.ds(pl.multiple_of(s * cap + source, 8), cap), :]
        side = sides_ref[s]
        side = jnp.where((lane >= low) & (lane < high), side, 0.0)
        shift = out - source + nfeat
        tile, shift = shift >> (nfeat.bit_length() - 1), shift & (nfeat - 1)
        moved = pltpu.roll(side, shift, axis=1)
        near, far = meta_ref[tile], meta_ref[tile + 1]
        meta_ref[tile] = near + jnp.where(lane >= shift, moved, 0.0)
        meta_ref[tile + 1] = far + jnp.where(lane < shift, moved, 0.0)
        return out + ((high - source + 7) & -8)

    total = lax.fori_loop(0, devices, compact, 0, unroll=32)

    def piece(begin, size):
        begin = pl.multiple_of(begin, CHUNK)
        col_id = lax.broadcasted_iota(jnp.int32, (wide, size), 0).astype(F32)
        side = jnp.concatenate([meta_ref[1 + begin // nfeat + q] for q in range(size // nfeat)], axis=1)
        lat, lon = side[0:1], side[1:2]
        here = (col_id == lon + 2.0).astype(F32).astype(BF)
        after = (col_id == lon + 3.0).astype(F32).astype(BF)
        parts = []
        for i in range(rows):
            row = (band * rows + i).astype(F32)
            same, above = lat == row, lat == row - 1.0
            left = jnp.where(same, side[2:3], jnp.where(above, side[4:5], 0.0)).astype(BF)
            right = jnp.where(same, side[3:4], jnp.where(above, side[5:6], 0.0)).astype(BF)
            parts.append(here * left + after * right)
        spread = jnp.concatenate(parts, axis=0)
        values = jnp.concatenate(
            [feat_ref[pl.ds(begin, size), :].astype(BF), jnp.ones((size, nfeat), BF)], axis=1
        )
        return dot(spread, values)

    def more(k, _):
        acc_ref[...] += piece(k * CHUNK, CHUNK)
        return 0

    acc_ref[...] = piece(0, HEAD)
    lax.fori_loop(HEAD // CHUNK, (total + CHUNK - 1) // CHUNK, more, 0)
    fetch(band).wait()

    @pl.when(band == 0)
    def _():
        for load in loads:
            load.wait()

    for g in range(0, rows, GROUP):
        sums = acc_ref[g * wide : (g + GROUP) * wide, :]
        start = back_ref[band, g * wide : (g + GROUP) * wide, :]
        density = sums[:, nfeat:]
        normalized = (sums[:, :nfeat] / (density + 1.0)).astype(BF)
        start = start + dot(normalized, w_in_ref[...])
        start = start + jnp.concatenate([density] * (chans // nfeat), axis=1) * w_dens_ref[...]
        first = start.astype(BF)
        for i in range(GROUP):
            first_ref[band * rows + g + i] = first[i * wide : (i + 1) * wide]
            for k, col in enumerate((2, 3, cols, cols + 1)):
                edge_scr[k, pl.ds(band * rows + g + i, 1), :] = start[i * wide + col : i * wide + col + 1]

    @pl.when(band == bands - 1)
    def _():
        west_ref[...] = edge_scr[0:2].astype(BF)
        east_ref[...] = edge_scr[2:4].astype(BF)
        even = lax.axis_index("lat") % 2 == 0
        for k in range(2):
            top, bottom = first_ref[k].astype(F32), first_ref[lat_rows - 1 - k].astype(F32)
            inner = jnp.where(even, bottom, top).astype(BF)
            outer = jnp.where(even, top, bottom).astype(BF)
            inner_ref[k] = inner
            outer_ref[k] = outer


def gridded(recv, back, w_in, w_dens, cap, wide, lat_rows, cols):
    devices, nfeat = 2 * recv.shape[0], recv.shape[2]
    chans = back.shape[1]
    slots = devices * cap
    tall = -(-lat_rows // 16) * 16
    whole = pl.BlockSpec(memory_space=pltpu.VMEM)
    return pl.pallas_call(
        functools.partial(grid_kernel, devices, cap, wide, cols, lat_rows // BAND),
        grid=(lat_rows // BAND,),
        out_shape=(
            jax.ShapeDtypeStruct((lat_rows, wide, chans), BF),
            jax.ShapeDtypeStruct((2, tall, chans), BF),
            jax.ShapeDtypeStruct((2, tall, chans), BF),
            jax.ShapeDtypeStruct((2, wide, chans), BF),
            jax.ShapeDtypeStruct((2, wide, chans), BF),
        ),
        in_specs=[whole] + [pl.BlockSpec(memory_space=pltpu.HBM)] * 3,
        out_specs=(whole,) * 5,
        scratch_shapes=[
            pltpu.VMEM((slots + cap, nfeat), F32),
            pltpu.VMEM((devices, META, nfeat), F32),
            pltpu.VMEM((devices, nfeat), F32),
            pltpu.VMEM((slots + cap + HEAD, nfeat), F32),
            pltpu.VMEM((slots // nfeat + 8, META, nfeat), F32),
            pltpu.VMEM((BAND * wide, 2 * nfeat), F32),
            pltpu.VMEM((4, tall, chans), F32),
            pltpu.VMEM((devices, nfeat), jnp.int32),
            pltpu.SMEM((devices, nfeat), jnp.int32),
            pltpu.SemaphoreType.DMA,
            pltpu.VMEM((lat_rows // BAND, BAND * wide, chans), F32),
            pltpu.VMEM(w_in.shape, BF),
            pltpu.VMEM(w_dens.shape, F32),
            pltpu.SemaphoreType.DMA((lat_rows // BAND + 2,)),
        ],
        compiler_params=params(42),
    )(recv, back, w_in, w_dens)


def put(ref, begin, value):
    size, chans = value.shape
    for b in range(3):
        part = value if b == 0 else pltpu.roll(value, size - b, axis=0)
        ref[pl.ds(begin, size), b * chans : (b + 1) * chans] = part.astype(BF)


def taps(ref, begin, size, wide, w_ref):
    field = jnp.concatenate([ref[pl.ds(begin + a * wide, size), :] for a in range(3)], axis=1)
    return dot(field, w_ref[...].reshape(field.shape[1], w_ref.shape[2]))


def border_kernel(lat_rows, cols, inner_ref, outer_ref, west_ref, east_ref, after_ref, inner_out, outer_out):
    _, wide, chans = inner_ref.shape
    even = lax.axis_index("lat") % 2 == 0
    row_id = lax.broadcasted_iota(jnp.int32, (wide, chans), 0)
    sides = [west_ref[0], west_ref[1], east_ref[0], east_ref[1]]
    sides = [side.astype(F32) for side in sides]
    for k in range(2):
        inner, outer = inner_ref[k].astype(F32), outer_ref[k].astype(F32)
        for side, col in zip(sides, (0, 1, cols + 2, cols + 3)):
            top = side[k : k + 1]
            bottom = side[lat_rows - 1 - k : lat_rows - k]
            inner = jnp.where(row_id == col, jnp.where(even, bottom, top), inner)
            outer = jnp.where(row_id == col, jnp.where(even, top, bottom), outer)
        inner_out[k] = inner.astype(BF)
        outer_out[k] = outer.astype(BF)


def bordered(inner, outer, west, east, after, lat_rows, cols):
    whole = pl.BlockSpec(memory_space=pltpu.VMEM)
    shape = jax.ShapeDtypeStruct(inner.shape, BF)
    return pl.pallas_call(
        functools.partial(border_kernel, lat_rows, cols),
        out_shape=(shape, shape),
        in_specs=[whole] * 4 + [pl.BlockSpec(memory_space=pl.ANY)],
        out_specs=(whole, whole),
        compiler_params=params(24),
    )(inner, outer, west, east, after)


def with_sides(value, sides, cols):
    wide, chans = value.shape
    last = wide - 16
    row_id = lax.broadcasted_iota(jnp.int32, (16, chans), 0)
    head, tail = value[:16], value[last:]
    for k in range(2):
        head = jnp.where(row_id == k, sides[k], head)
        tail = jnp.where(row_id == cols + 2 + k - last, sides[2 + k], tail)
    return jnp.concatenate([head, value[16:last], tail], axis=0)


def convolve_rows(field, one_ref, hid_ref, place, count, wide):
    size = FINISH * wide

    def hidden(g, _):
        begin = pl.multiple_of(g * size, 16)
        total = taps(field, begin, size, wide, one_ref)
        put(hid_ref, pl.multiple_of(begin + place * wide, 16), gelu(total))
        return 0

    lax.fori_loop(0, count // FINISH, hidden, 0)


def upper_kernel(first_ref, one_ref, after_ref, hid_ref, field):
    wide = first_ref.shape[1]
    count = field.shape[0] // wide

    def load(r, _):
        put(field, pl.multiple_of(r * wide, 16), first_ref[r].astype(F32))
        return 0

    lax.fori_loop(0, count, load, 0, unroll=4)
    convolve_rows(field, one_ref, hid_ref, 2, count - 2, wide)


def lower_kernel(cols, first_ref, one_ref, west_ref, east_ref, after_ref, hid_ref, field, side_scr):
    lat_rows, wide, _ = first_ref.shape
    count = field.shape[0] // wide
    lead = lat_rows - count
    side_scr[0:2] = west_ref[...].astype(F32)
    side_scr[2:4] = east_ref[...].astype(F32)

    def load(r, _):
        sides = [side_scr[k, pl.ds(lead + r, 1), :] for k in range(4)]
        value = with_sides(first_ref[lead + r].astype(F32), sides, cols)
        put(field, pl.multiple_of(r * wide, 16), value)
        return 0

    lax.fori_loop(0, count, load, 0, unroll=2)
    convolve_rows(field, one_ref, hid_ref, 0, count - 2, wide)


def upper_part(first, one, after, rows):
    _, wide, chans = first.shape
    whole = pl.BlockSpec(memory_space=pltpu.VMEM)
    shape = ((rows + 2) * wide, 3 * chans)
    return pl.pallas_call(
        upper_kernel,
        out_shape=jax.ShapeDtypeStruct(shape, BF),
        in_specs=[whole, whole, pl.BlockSpec(memory_space=pl.ANY)],
        out_specs=whole,
        scratch_shapes=[pltpu.VMEM(shape, BF)],
        compiler_params=params(24),
    )(first, one, after)


def lower_part(first, one, west, east, after, rows, cols):
    _, wide, chans = first.shape
    whole = pl.BlockSpec(memory_space=pltpu.VMEM)
    shape = ((rows + 2) * wide, 3 * chans)
    return pl.pallas_call(
        functools.partial(lower_kernel, cols),
        out_shape=jax.ShapeDtypeStruct(shape, BF),
        in_specs=[whole] * 4 + [pl.BlockSpec(memory_space=pl.ANY)],
        out_specs=whole,
        scratch_shapes=[pltpu.VMEM(shape, BF), pltpu.VMEM((4, west.shape[1], chans), F32)],
        compiler_params=params(24),
    )(first, one, west, east, after)


def finish_kernel(
    lat_count, upper_in, lower_in, first_ref, own_west, own_east, west_ref, east_ref, inner_ref, outer_ref,
    one_ref, two_ref, out_ref, upper_ref, lower_ref, rim, cols_scr,
):
    group = pl.program_id(0)
    lat_rows, wide, chans = first_ref.shape
    rows, cols, _ = out_ref.shape
    block = rows * wide
    above = upper_ref.shape[0] // wide - 2
    below = lat_rows - above

    @pl.when(group == 0)
    def _():
        lat_index = lax.axis_index("lat")
        even = lat_index % 2 == 0
        short_id = lax.broadcasted_iota(jnp.int32, (16, chans), 0)
        lines = [west_ref[0], west_ref[1], own_west[0], own_west[1]]
        lines += [own_east[0], own_east[1], east_ref[0], east_ref[1]]
        lines = [line.astype(F32) for line in lines]

        def edge_row(north, k):
            return jnp.where(even == north, outer_ref[k].astype(F32), inner_ref[k].astype(F32))

        def own_row(r):
            sides = [lines[n][r : r + 1] for n in (0, 1, 6, 7)]
            return with_sides(first_ref[r].astype(F32), sides, cols)

        rims = [edge_row(True, 1), edge_row(True, 0), own_row(0), own_row(1)]
        rims += [own_row(lat_rows - 2), own_row(lat_rows - 1), edge_row(False, 0), edge_row(False, 1)]
        for n, line in enumerate(rims):
            put(rim, n * wide, line)
        size = cols_scr.shape[1]
        fields = []
        for a in range(3):
            top = jnp.where(lat_index == 0, 2 - a, a)
            bottom = jnp.where(lat_index == lat_count - 1, 7 - a, 5 + a)
            parts = [
                rim[pl.ds(pl.multiple_of(n * wide, 16), wide), :] for n in (top, 1 + a, 4 + a, bottom)
            ]
            for n in (0, 1, 4, 5):
                window = [lines[n + b][a : a + size].astype(BF) for b in range(3)]
                parts.append(jnp.concatenate(window, axis=1))
            fields.append(jnp.concatenate(parts, axis=0))
        total = jnp.zeros((4 * wide + 4 * size, chans), F32)
        for a in range(3):
            total = total + dot(fields[a], one_ref[a])
        total = gelu(total)
        put(upper_ref, 0, total[:wide])
        put(upper_ref, wide, total[wide : 2 * wide])
        put(lower_ref, below * wide, total[2 * wide : 3 * wide])
        put(lower_ref, (below + 1) * wide, total[3 * wide : 4 * wide])
        for n in range(4):
            cols_scr[n] = total[4 * wide + n * size : 4 * wide + (n + 1) * size]
        last = wide - 16

        def patch(r, _):
            fixes = [cols_scr[n, pl.ds(r, 1), :] for n in range(4)]
            begin = pl.multiple_of((r + 2) * wide, 16)
            for b in range(3):
                lanes = slice(b * chans, (b + 1) * chans)
                for start in (0, last):
                    edits = [
                        (col - b - start, fix)
                        for col, fix in zip((0, 1, cols, cols + 1), fixes)
                        if 0 <= col - b - start < 16
                    ]
                    if edits:
                        value = upper_ref[pl.ds(begin + start, 16), lanes].astype(F32)
                        for at, fix in edits:
                            value = jnp.where(short_id == at, fix, value)
                        upper_ref[pl.ds(begin + start, 16), lanes] = value.astype(BF)
            return 0

        lax.fori_loop(0, above, patch, 0, unroll=10)

    def second(ref, first_group):
        begin = pl.multiple_of((group - first_group) * block, 16)
        total = taps(ref, begin, block, wide, two_ref)
        own = first_ref[pl.ds(group * rows, rows)].reshape(block, chans).astype(F32)
        total = total + pltpu.roll(own, block - 2, axis=0)
        result = total.astype(BF)
        for i in range(rows):
            out_ref[i] = result[i * wide : i * wide + cols]

    pl.when(group < above // rows)(lambda: second(upper_ref, 0))
    pl.when(group >= above // rows)(lambda: second(lower_ref, above // rows))


def finished(upper, lower, first, sides, one, two, cols, lat_count):
    lat_rows, wide, chans = first.shape
    whole = pl.BlockSpec(memory_space=pltpu.VMEM)
    out, _, _ = pl.pallas_call(
        functools.partial(finish_kernel, lat_count),
        grid=(lat_rows // FINISH,),
        out_shape=(
            jax.ShapeDtypeStruct((lat_rows, cols, chans), BF),
            jax.ShapeDtypeStruct(upper.shape, BF),
            jax.ShapeDtypeStruct(lower.shape, BF),
        ),
        in_specs=[whole] * (5 + len(sides)),
        out_specs=(pl.BlockSpec((FINISH, cols, chans), lambda g: (g, 0, 0)), whole, whole),
        input_output_aliases={0: 1, 1: 2},
        scratch_shapes=[
            pltpu.VMEM((8 * wide, 3 * chans), BF),
            pltpu.VMEM((4, -(-UPPER // 16) * 16, chans), F32),
        ],
        compiler_params=params(26),
    )(upper, lower, first, *sides, one, two)
    return out


def row_pairs(lat_count, lon_count):
    half = lon_count // 2

    def flat(lat, lon):
        return lat * lon_count + lon % lon_count

    inner, outer = [], []
    for lon in range(lon_count):
        for lat in range(0, lat_count, 2):
            inner += [(flat(lat, lon), flat(lat + 1, lon)), (flat(lat + 1, lon), flat(lat, lon))]
        for lat in range(1, lat_count - 1, 2):
            outer += [(flat(lat, lon), flat(lat + 1, lon)), (flat(lat + 1, lon), flat(lat, lon))]
        outer += [(flat(lat, lon), flat(lat, lon + half)) for lat in (0, lat_count - 1)]
    return inner, outer


def shards(
    obs_features,
    obs_dest,
    obs_cells,
    obs_gauss,
    row_counts,
    background,
    w_in,
    w_bg,
    w_dens,
    conv_one,
    conv_two,
):
    nrows, nfeat = obs_features.shape
    lat_rows, cols, chans = background.shape
    axes = ("lat", "lon")
    devices = lax.axis_size(axes)
    lat_count, lon_count = lax.axis_size("lat"), lax.axis_size("lon")
    cap = 2 * nrows // devices
    wide = -(-(cols + 4) // 16) * 16
    send = pack(
        row_counts, obs_dest.reshape(1, nrows), obs_cells.T, obs_gauss.T, obs_features, devices, lon_count, cap, cols,
        lat_rows // BAND,
    )
    paired = send.shape
    send = send.reshape(devices, cap + META, nfeat)
    recv = lax.all_to_all(send, axes, split_axis=0, concat_axis=0, tiled=True).reshape(paired)
    back = projected(background, w_bg, wide)
    first, own_west, own_east, inner_row, outer_row = gridded(
        recv, back, w_in, w_dens.reshape(1, chans), cap, wide, lat_rows, cols
    )
    west = lax.ppermute(own_east, "lon", [(i, (i + 1) % lon_count) for i in range(lon_count)])
    east = lax.ppermute(own_west, "lon", [((i + 1) % lon_count, i) for i in range(lon_count)])
    one = conv_one.reshape(3, 3 * chans, chans)
    two = conv_two.reshape(3, 3 * chans, chans)
    upper = upper_part(first, one, own_west, UPPER)
    inner_row, outer_row = bordered(inner_row, outer_row, west, east, upper, lat_rows, cols)
    inner, outer = row_pairs(lat_count, lon_count)
    lower = lower_part(first, one, west, east, inner_row, lat_rows - UPPER, cols)
    inner_row = lax.ppermute(inner_row, axes, inner)
    outer_row = lax.ppermute(outer_row, axes, outer)
    sides = (own_west, own_east, west, east, inner_row, outer_row)
    return finished(upper, lower, first, sides, one, two, cols, lat_count)


def solution(mesh):
    rows = P(("lat", "lon"), None)
    in_specs = (rows, rows, rows, rows, P(("lat", "lon")), P("lat", "lon", None), P(), P(), P(), P(), P())
    return jax.shard_map(
        shards, mesh=mesh, in_specs=in_specs, out_specs=P("lat", "lon", None), check_vma=False
    )
```

```python
import functools

import jax
import jax.numpy as jnp
from jax import lax
from jax.experimental import pallas as pl
from jax.experimental.pallas import tpu as pltpu
from jax.sharding import PartitionSpec as P

KCELL = 4
GBINS = 32
META = 8
GROUP = 6
BAND = 18
CHUNK = 256
HEAD = 768
FINISH = 15
UPPER = 30
BF = jnp.bfloat16
F32 = jnp.float32


def params(mib):
    return pltpu.CompilerParams(vmem_limit_bytes=mib * 1024 * 1024)


def gelu(x):
    scale = 0.7978845608028654
    half = 0.5 * x
    return half + half * jnp.tanh(x * (scale + (scale * 0.044715) * (x * x)))


def dot(a, b):
    return jnp.dot(a, b, preferred_element_type=F32)


def pack_kernel(
    devices, lon_count, cap, cols, bands, count_ref, dest_ref, cells_ref, gauss_ref, feat_hbm, send_hbm,
    ext_ref, hot_ref, sorted_ref, place_ref, place_smem, send_ref, sem, feat_sem, send_sems,
):
    nrows, nfeat = feat_hbm.shape
    fetch = pltpu.make_async_copy(feat_hbm, ext_ref.at[:, pl.ds(0, nfeat)], feat_sem)
    fetch.start()
    step = 256
    classes = 2 * bands
    kinds = devices * classes
    dest = dest_ref[...]
    row_id = lax.broadcasted_iota(jnp.int32, (1, nrows), 1)
    base = cells_ref[0:1, :].astype(F32)
    lat = jnp.floor((base + 0.5) * (1.0 / cols))
    lon = base - lat * cols
    band = jnp.floor((lat + 0.5) * (1.0 / BAND))
    kind = 2.0 * band + (lat == band * BAND + (BAND - 1)).astype(F32)
    kind = dest * classes + kind.astype(jnp.int32)
    kind = jnp.where(row_id < count_ref[0], kind, kinds)
    ratio = gauss_ref[...].astype(F32) * (1.0 / GBINS)
    weight = jnp.exp(-3.0 * ratio * ratio)
    meta = jnp.concatenate([lat, lon, weight, jnp.zeros((nfeat - 2 - KCELL, nrows), F32)], axis=0)
    ext_ref[:, nfeat:] = meta.T.astype(BF)
    hot_ref[...] = (lax.broadcasted_iota(jnp.int32, (kinds, nrows), 0) == kind).astype(F32).astype(BF)
    counts = dot(hot_ref[...], jnp.ones((nrows, nfeat), BF))
    ka = lax.broadcasted_iota(jnp.int32, (kinds, kinds), 0)
    kb = lax.broadcasted_iota(jnp.int32, (kinds, kinds), 1)
    da = lax.broadcasted_iota(jnp.int32, (kinds, 1), 0) // classes
    row = lax.broadcasted_iota(jnp.int32, (1, kinds), 1)
    db = row // classes
    within = ((da == db) & (kb < ka)).astype(F32).astype(BF)
    together = (da == db).astype(F32).astype(BF)
    ahead = ((db < da) & (row == db * classes)).astype(F32).astype(BF)
    loads = dot(together, counts.astype(BF))
    padded = jnp.floor((loads + 7.0) * 0.125) * 8.0
    begins = dot(ahead, padded.astype(BF))
    mine = begins + dot(within, counts.astype(BF))
    kind_id = lax.broadcasted_iota(jnp.int32, (kinds, nfeat), 0)
    lane_id = lax.broadcasted_iota(jnp.int32, (kinds, nfeat), 1)
    lead = kind_id == lane_id * classes
    place_ref[0:1, :] = jnp.sum(jnp.where(lead, begins, 0.0), axis=0, keepdims=True).astype(jnp.int32)
    place_ref[1:2, :] = jnp.sum(jnp.where(lead, loads, 0.0), axis=0, keepdims=True).astype(jnp.int32)
    copy = pltpu.make_async_copy(place_ref, place_smem, sem)
    copy.start()
    earlier = (
        lax.broadcasted_iota(jnp.int32, (step, step), 0) < lax.broadcasted_iota(jnp.int32, (step, step), 1)
    ).astype(F32).astype(BF)
    carry = mine[:, 0:1]
    places = []
    for begin in range(0, nrows, step):
        hot = hot_ref[:, begin : begin + step]
        before = dot(hot, earlier) + carry
        hot = hot.astype(F32)
        places.append(
            jnp.sum(before * hot, axis=0, keepdims=True) + jnp.sum(hot, axis=0, keepdims=True) - 1.0
        )
        carry = carry + jnp.sum(hot, axis=1, keepdims=True)
    place = jnp.concatenate(places, axis=1)
    live = row_id < count_ref[0]
    place = jnp.where(live, place, -1.0)
    slot = lax.broadcasted_iota(jnp.int32, (step, nrows), 0).astype(F32)
    span = sorted_ref.shape[0]
    fetch.wait()
    for k in range(-(-(nrows + 8 * devices) // step)):
        pick = (slot == place - k * step).astype(F32).astype(BF)
        sorted_ref[k * step : (k + 1) * step, :] = dot(pick, ext_ref[...])
    tail = -(-(nrows + 8 * devices) // step) * step
    sorted_ref[tail:span, :] = jnp.zeros((span - tail, 2 * nfeat), F32)
    copy.wait()
    side_lane = lax.broadcasted_iota(jnp.int32, (META, nfeat), 1)
    odd = (lax.axis_index("lat") * lon_count + lax.axis_index("lon")) % 2 == 1

    def one(d):
        begin = pl.multiple_of(place_smem[0, d], 8)
        got = sorted_ref[pl.ds(begin, cap), :]
        side = got[:, nfeat:]
        if cap < nfeat:
            side = jnp.concatenate([side, jnp.zeros((nfeat - cap, nfeat), F32)], axis=0)
        return got[:, :nfeat], jnp.where(side_lane < place_smem[1, d], side.T[0:META], 0.0)

    def pair(p, _):
        (rows_a, side_a), (rows_b, side_b) = one(2 * p), one(2 * p + 1)
        plain = jnp.concatenate([rows_a, side_a, rows_b, side_b], axis=0)
        turned = jnp.concatenate([side_a, rows_a, side_b, rows_b], axis=0)
        send_ref[p] = jnp.where(odd, turned, plain).astype(BF)
        pltpu.make_async_copy(send_ref.at[p], send_hbm.at[p], send_sems.at[p]).start()
        return 0

    def sent(p, _):
        pltpu.make_async_copy(send_ref.at[p], send_hbm.at[p], send_sems.at[p]).wait()
        return 0

    lax.fori_loop(0, devices // 2, pair, 0, unroll=2)
    lax.fori_loop(0, devices // 2, sent, 0)


def pack(count, dest, cells, gauss, feats, devices, lon_count, cap, cols, bands):
    nrows, nfeat = feats.shape
    span = -(-(nrows + 8 * devices) // 256) * 256 + cap
    kinds = devices * 2 * bands
    return pl.pallas_call(
        functools.partial(pack_kernel, devices, lon_count, cap, cols, bands),
        out_shape=jax.ShapeDtypeStruct((devices // 2, 2 * (cap + META), nfeat), BF),
        in_specs=[pl.BlockSpec(memory_space=pltpu.SMEM)] + [pl.BlockSpec(memory_space=pltpu.VMEM)] * 3
        + [pl.BlockSpec(memory_space=pl.ANY)],
        out_specs=pl.BlockSpec(memory_space=pl.ANY),
        scratch_shapes=[
            pltpu.VMEM((nrows, 2 * nfeat), BF),
            pltpu.VMEM((kinds, nrows), BF),
            pltpu.VMEM((span, 2 * nfeat), F32),
            pltpu.VMEM((8, nfeat), jnp.int32),
            pltpu.SMEM((8, nfeat), jnp.int32),
            pltpu.VMEM((devices // 2, 2 * (cap + META), nfeat), BF),
            pltpu.SemaphoreType.DMA,
            pltpu.SemaphoreType.DMA,
            pltpu.SemaphoreType.DMA((devices // 2,)),
        ],
        compiler_params=params(56),
    )(count, dest, cells, gauss, feats)


def back_kernel(wide, back_ref, w_bg_ref, out_ref, scr):
    rows, cols, chans = back_ref.shape
    for i in range(rows):
        scr[i * wide : i * wide + cols, :] = back_ref[i]
    out_ref[...] = pltpu.roll(dot(scr[...], w_bg_ref[...]), 2, axis=0)


def projected(background, w_bg, wide):
    lat_rows, cols, chans = background.shape
    length = max(lat_rows * wide, 1 << 16) + 16
    return pl.pallas_call(
        functools.partial(back_kernel, wide),
        grid=(lat_rows // BAND,),
        out_shape=pltpu.HBM((length, chans), F32),
        in_specs=[
            pl.BlockSpec((BAND, cols, chans), lambda g: (g, 0, 0)),
            pl.BlockSpec(memory_space=pltpu.VMEM),
        ],
        out_specs=pl.BlockSpec((BAND * wide, chans), lambda g: (g, 0)),
        scratch_shapes=[pltpu.VMEM((BAND * wide, chans), BF)],
        compiler_params=params(24),
    )(background, w_bg)


def grid_kernel(
    devices, cap, wide, cols, lat_bands, recv_ref, back_hbm, w_in_hbm, w_dens_hbm,
    first_ref, west_ref, east_ref, inner_ref, outer_ref,
    rows_ref, sides_ref, lats_ref, feat_ref, meta_ref, acc_ref, edge_scr, ends_ref, ends_smem, sem,
    back_ref, w_in_ref, w_dens_ref, sems,
):
    band = pl.program_id(0)
    bands = pl.num_programs(0)
    nfeat = recv_ref.shape[2]
    lat_rows, _, chans = first_ref.shape
    rows = lat_rows // lat_bands
    slots = devices * cap
    span = rows * wide

    def fetch(b):
        begin = pl.multiple_of(b * span, 16)
        return pltpu.make_async_copy(back_hbm.at[pl.ds(begin, span), :], back_ref.at[b], sems.at[b])

    loads = [
        pltpu.make_async_copy(w_in_hbm, w_in_ref, sems.at[lat_bands]),
        pltpu.make_async_copy(w_dens_hbm, w_dens_ref, sems.at[lat_bands + 1]),
    ]

    @pl.when(band == 0)
    def _():
        for b in range(lat_bands):
            fetch(b).start()
        for load in loads:
            load.start()

        def read(p, _):
            both = recv_ref[p, cap : cap + 2 * META, :].astype(F32)
            for s, side in ((2 * p, both[:META]), (2 * p + 1, both[META:])):
                sides_ref[s] = side
                lats_ref[pl.ds(s, 1), :] = jnp.where(side[2:3] > 0, side[0:1], 1e6)
            return 0

        lax.fori_loop(0, devices // 2, read, 0, unroll=8)
        lats = lats_ref[...]
        lane = lax.broadcasted_iota(jnp.int32, (devices, nfeat), 1)
        ends = jnp.zeros((devices, nfeat), F32)
        for b in range(lat_bands):
            low = jnp.sum((lats < b * rows - 1.0).astype(F32), axis=1, keepdims=True)
            high = jnp.sum((lats < (b + 1.0) * rows).astype(F32), axis=1, keepdims=True)
            ends = jnp.where(lane == 2 * b, low, jnp.where(lane == 2 * b + 1, high, ends))
        ends_ref[...] = ends.astype(jnp.int32)
        copy = pltpu.make_async_copy(ends_ref, ends_smem, sem)
        copy.start()
        feat_ref[...] = jnp.zeros(feat_ref.shape, F32)
        rows_ref[slots:, :] = jnp.zeros((rows_ref.shape[0] - slots, nfeat), F32)

        def widen(p, _):
            begin = pl.multiple_of(2 * p * cap, cap)
            rows_ref[pl.ds(begin, cap), :] = recv_ref[p, 0:cap, :].astype(F32)
            rows_ref[pl.ds(begin + cap, cap), :] = recv_ref[p, cap + 2 * META :, :].astype(F32)
            return 0

        lax.fori_loop(0, devices // 2, widen, 0, unroll=2)
        copy.wait()

    meta_ref[...] = jnp.zeros(meta_ref.shape, F32)
    lane = lax.broadcasted_iota(jnp.int32, (META, nfeat), 1)

    def compact(s, out):
        out = pl.multiple_of(out, 8)
        low, high = ends_smem[s, 2 * band], ends_smem[s, 2 * band + 1]
        source = pl.multiple_of(low & -8, 8)
        feat_ref[pl.ds(out, cap), :] = rows_ref[pl.ds(pl.multiple_of(s * cap + source, 8), cap), :]
        side = sides_ref[s]
        side = jnp.where((lane >= low) & (lane < high), side, 0.0)
        shift = out - source + nfeat
        tile, shift = shift >> (nfeat.bit_length() - 1), shift & (nfeat - 1)
        moved = pltpu.roll(side, shift, axis=1)
        near, far = meta_ref[tile], meta_ref[tile + 1]
        meta_ref[tile] = near + jnp.where(lane >= shift, moved, 0.0)
        meta_ref[tile + 1] = far + jnp.where(lane < shift, moved, 0.0)
        return out + ((high - source + 7) & -8)

    total = lax.fori_loop(0, devices, compact, 0, unroll=32)

    def piece(begin, size):
        begin = pl.multiple_of(begin, CHUNK)
        col_id = lax.broadcasted_iota(jnp.int32, (wide, size), 0).astype(F32)
        side = jnp.concatenate([meta_ref[1 + begin // nfeat + q] for q in range(size // nfeat)], axis=1)
        lat, lon = side[0:1], side[1:2]
        here = (col_id == lon + 2.0).astype(F32).astype(BF)
        after = (col_id == lon + 3.0).astype(F32).astype(BF)
        parts = []
        for i in range(rows):
            row = (band * rows + i).astype(F32)
            same, above = lat == row, lat == row - 1.0
            left = jnp.where(same, side[2:3], jnp.where(above, side[4:5], 0.0)).astype(BF)
            right = jnp.where(same, side[3:4], jnp.where(above, side[5:6], 0.0)).astype(BF)
            parts.append(here * left + after * right)
        spread = jnp.concatenate(parts, axis=0)
        values = jnp.concatenate(
            [feat_ref[pl.ds(begin, size), :].astype(BF), jnp.ones((size, nfeat), BF)], axis=1
        )
        return dot(spread, values)

    def more(k, _):
        acc_ref[...] += piece(k * CHUNK, CHUNK)
        return 0

    acc_ref[...] = piece(0, HEAD)
    lax.fori_loop(HEAD // CHUNK, (total + CHUNK - 1) // CHUNK, more, 0)
    fetch(band).wait()

    @pl.when(band == 0)
    def _():
        for load in loads:
            load.wait()

    for g in range(0, rows, GROUP):
        sums = acc_ref[g * wide : (g + GROUP) * wide, :]
        start = back_ref[band, g * wide : (g + GROUP) * wide, :]
        density = sums[:, nfeat:]
        normalized = (sums[:, :nfeat] / (density + 1.0)).astype(BF)
        start = start + dot(normalized, w_in_ref[...])
        start = start + jnp.concatenate([density] * (chans // nfeat), axis=1) * w_dens_ref[...]
        first = start.astype(BF)
        for i in range(GROUP):
            first_ref[band * rows + g + i] = first[i * wide : (i + 1) * wide]
            for k, col in enumerate((2, 3, cols, cols + 1)):
                edge_scr[k, pl.ds(band * rows + g + i, 1), :] = start[i * wide + col : i * wide + col + 1]

    @pl.when(band == bands - 1)
    def _():
        west_ref[...] = edge_scr[0:2].astype(BF)
        east_ref[...] = edge_scr[2:4].astype(BF)
        even = lax.axis_index("lat") % 2 == 0
        for k in range(2):
            top, bottom = first_ref[k].astype(F32), first_ref[lat_rows - 1 - k].astype(F32)
            inner = jnp.where(even, bottom, top).astype(BF)
            outer = jnp.where(even, top, bottom).astype(BF)
            inner_ref[k] = inner
            outer_ref[k] = outer


def gridded(recv, back, w_in, w_dens, cap, wide, lat_rows, cols):
    devices, nfeat = 2 * recv.shape[0], recv.shape[2]
    chans = back.shape[1]
    slots = devices * cap
    tall = -(-lat_rows // 16) * 16
    whole = pl.BlockSpec(memory_space=pltpu.VMEM)
    return pl.pallas_call(
        functools.partial(grid_kernel, devices, cap, wide, cols, lat_rows // BAND),
        grid=(lat_rows // BAND,),
        out_shape=(
            jax.ShapeDtypeStruct((lat_rows, wide, chans), BF),
            jax.ShapeDtypeStruct((2, tall, chans), BF),
            jax.ShapeDtypeStruct((2, tall, chans), BF),
            jax.ShapeDtypeStruct((2, wide, chans), BF),
            jax.ShapeDtypeStruct((2, wide, chans), BF),
        ),
        in_specs=[whole] + [pl.BlockSpec(memory_space=pltpu.HBM)] * 3,
        out_specs=(whole,) * 5,
        scratch_shapes=[
            pltpu.VMEM((slots + cap, nfeat), F32),
            pltpu.VMEM((devices, META, nfeat), F32),
            pltpu.VMEM((devices, nfeat), F32),
            pltpu.VMEM((slots + cap + HEAD, nfeat), F32),
            pltpu.VMEM((slots // nfeat + 8, META, nfeat), F32),
            pltpu.VMEM((BAND * wide, 2 * nfeat), F32),
            pltpu.VMEM((4, tall, chans), F32),
            pltpu.VMEM((devices, nfeat), jnp.int32),
            pltpu.SMEM((devices, nfeat), jnp.int32),
            pltpu.SemaphoreType.DMA,
            pltpu.VMEM((lat_rows // BAND, BAND * wide, chans), F32),
            pltpu.VMEM(w_in.shape, BF),
            pltpu.VMEM(w_dens.shape, F32),
            pltpu.SemaphoreType.DMA((lat_rows // BAND + 2,)),
        ],
        compiler_params=params(42),
    )(recv, back, w_in, w_dens)


def put(ref, begin, value):
    size, chans = value.shape
    plain = value.astype(BF)
    parts = plain, pltpu.roll(value, size - 1, axis=0).astype(BF), pltpu.roll(plain, size - 2, axis=0)
    for b, part in enumerate(parts):
        ref[pl.ds(begin, size), b * chans : (b + 1) * chans] = part


def taps(ref, begin, size, wide, w_ref):
    field = jnp.concatenate([ref[pl.ds(begin + a * wide, size), :] for a in range(3)], axis=1)
    return dot(field, w_ref[...].reshape(field.shape[1], w_ref.shape[2]))


def border_kernel(lat_rows, cols, inner_ref, outer_ref, west_ref, east_ref, after_ref, inner_out, outer_out):
    _, wide, chans = inner_ref.shape
    even = lax.axis_index("lat") % 2 == 0
    row_id = lax.broadcasted_iota(jnp.int32, (wide, chans), 0)
    sides = [west_ref[0], west_ref[1], east_ref[0], east_ref[1]]
    sides = [side.astype(F32) for side in sides]
    for k in range(2):
        inner, outer = inner_ref[k].astype(F32), outer_ref[k].astype(F32)
        for side, col in zip(sides, (0, 1, cols + 2, cols + 3)):
            top = side[k : k + 1]
            bottom = side[lat_rows - 1 - k : lat_rows - k]
            inner = jnp.where(row_id == col, jnp.where(even, bottom, top), inner)
            outer = jnp.where(row_id == col, jnp.where(even, top, bottom), outer)
        inner_out[k] = inner.astype(BF)
        outer_out[k] = outer.astype(BF)


def bordered(inner, outer, west, east, after, lat_rows, cols):
    whole = pl.BlockSpec(memory_space=pltpu.VMEM)
    shape = jax.ShapeDtypeStruct(inner.shape, BF)
    return pl.pallas_call(
        functools.partial(border_kernel, lat_rows, cols),
        out_shape=(shape, shape),
        in_specs=[whole] * 4 + [pl.BlockSpec(memory_space=pl.ANY)],
        out_specs=(whole, whole),
        compiler_params=params(24),
    )(inner, outer, west, east, after)


def with_sides(value, sides, cols):
    wide, chans = value.shape
    last = wide - 16
    row_id = lax.broadcasted_iota(jnp.int32, (16, chans), 0)
    head, tail = value[:16], value[last:]
    for k in range(2):
        head = jnp.where(row_id == k, sides[k], head)
        tail = jnp.where(row_id == cols + 2 + k - last, sides[2 + k], tail)
    return jnp.concatenate([head, value[16:last], tail], axis=0)


def convolve_rows(field, one_ref, hid_ref, place, count, wide):
    size = FINISH * wide

    def hidden(g, _):
        begin = pl.multiple_of(g * size, 16)
        total = taps(field, begin, size, wide, one_ref)
        put(hid_ref, pl.multiple_of(begin + place * wide, 16), gelu(total))
        return 0

    lax.fori_loop(0, count // FINISH, hidden, 0)


def upper_kernel(first_ref, one_ref, after_ref, hid_ref, field):
    wide = first_ref.shape[1]
    count = field.shape[0] // wide

    def load(r, _):
        put(field, pl.multiple_of(r * wide, 16), first_ref[r].astype(F32))
        return 0

    lax.fori_loop(0, count, load, 0, unroll=4)
    convolve_rows(field, one_ref, hid_ref, 2, count - 2, wide)


def lower_kernel(cols, first_ref, one_ref, west_ref, east_ref, after_ref, hid_ref, field, side_scr):
    lat_rows, wide, _ = first_ref.shape
    count = field.shape[0] // wide
    lead = lat_rows - count
    side_scr[0:2] = west_ref[...].astype(F32)
    side_scr[2:4] = east_ref[...].astype(F32)

    def load(r, _):
        sides = [side_scr[k, pl.ds(lead + r, 1), :] for k in range(4)]
        value = with_sides(first_ref[lead + r].astype(F32), sides, cols)
        put(field, pl.multiple_of(r * wide, 16), value)
        return 0

    lax.fori_loop(0, count, load, 0, unroll=2)
    convolve_rows(field, one_ref, hid_ref, 0, count - 2, wide)


def upper_part(first, one, after, rows):
    _, wide, chans = first.shape
    whole = pl.BlockSpec(memory_space=pltpu.VMEM)
    shape = ((rows + 2) * wide, 3 * chans)
    return pl.pallas_call(
        upper_kernel,
        out_shape=jax.ShapeDtypeStruct(shape, BF),
        in_specs=[whole, whole, pl.BlockSpec(memory_space=pl.ANY)],
        out_specs=whole,
        scratch_shapes=[pltpu.VMEM(shape, BF)],
        compiler_params=params(24),
    )(first, one, after)


def lower_part(first, one, west, east, after, rows, cols):
    _, wide, chans = first.shape
    whole = pl.BlockSpec(memory_space=pltpu.VMEM)
    shape = ((rows + 2) * wide, 3 * chans)
    return pl.pallas_call(
        functools.partial(lower_kernel, cols),
        out_shape=jax.ShapeDtypeStruct(shape, BF),
        in_specs=[whole] * 4 + [pl.BlockSpec(memory_space=pl.ANY)],
        out_specs=whole,
        scratch_shapes=[pltpu.VMEM(shape, BF), pltpu.VMEM((4, west.shape[1], chans), F32)],
        compiler_params=params(24),
    )(first, one, west, east, after)


def finish_kernel(
    lat_count, upper_in, lower_in, first_ref, own_west, own_east, west_ref, east_ref, inner_ref, outer_ref,
    one_ref, two_ref, out_ref, upper_ref, lower_ref, rim, cols_scr,
):
    group = pl.program_id(0)
    lat_rows, wide, chans = first_ref.shape
    rows, cols, _ = out_ref.shape
    block = rows * wide
    above = upper_ref.shape[0] // wide - 2
    below = lat_rows - above

    @pl.when(group == 0)
    def _():
        lat_index = lax.axis_index("lat")
        even = lat_index % 2 == 0
        short_id = lax.broadcasted_iota(jnp.int32, (16, chans), 0)
        lines = [west_ref[0], west_ref[1], own_west[0], own_west[1]]
        lines += [own_east[0], own_east[1], east_ref[0], east_ref[1]]
        lines = [line.astype(F32) for line in lines]

        def edge_row(north, k):
            return jnp.where(even == north, outer_ref[k].astype(F32), inner_ref[k].astype(F32))

        def own_row(r):
            sides = [lines[n][r : r + 1] for n in (0, 1, 6, 7)]
            return with_sides(first_ref[r].astype(F32), sides, cols)

        rims = [edge_row(True, 1), edge_row(True, 0), own_row(0), own_row(1)]
        rims += [own_row(lat_rows - 2), own_row(lat_rows - 1), edge_row(False, 0), edge_row(False, 1)]
        for n, line in enumerate(rims):
            put(rim, n * wide, line)
        size = cols_scr.shape[1]
        fields = []
        for a in range(3):
            top = jnp.where(lat_index == 0, 2 - a, a)
            bottom = jnp.where(lat_index == lat_count - 1, 7 - a, 5 + a)
            parts = [
                rim[pl.ds(pl.multiple_of(n * wide, 16), wide), :] for n in (top, 1 + a, 4 + a, bottom)
            ]
            for n in (0, 1, 4, 5):
                window = [lines[n + b][a : a + size].astype(BF) for b in range(3)]
                parts.append(jnp.concatenate(window, axis=1))
            fields.append(jnp.concatenate(parts, axis=0))
        total = jnp.zeros((4 * wide + 4 * size, chans), F32)
        for a in range(3):
            total = total + dot(fields[a], one_ref[a])
        total = gelu(total)
        put(upper_ref, 0, total[:wide])
        put(upper_ref, wide, total[wide : 2 * wide])
        put(lower_ref, below * wide, total[2 * wide : 3 * wide])
        put(lower_ref, (below + 1) * wide, total[3 * wide : 4 * wide])
        for n in range(4):
            cols_scr[n] = total[4 * wide + n * size : 4 * wide + (n + 1) * size]
        last = wide - 16

        def patch(r, _):
            fixes = [cols_scr[n, pl.ds(r, 1), :] for n in range(4)]
            begin = pl.multiple_of((r + 2) * wide, 16)
            for b in range(3):
                lanes = slice(b * chans, (b + 1) * chans)
                for start in (0, last):
                    edits = [
                        (col - b - start, fix)
                        for col, fix in zip((0, 1, cols, cols + 1), fixes)
                        if 0 <= col - b - start < 16
                    ]
                    if edits:
                        value = upper_ref[pl.ds(begin + start, 16), lanes].astype(F32)
                        for at, fix in edits:
                            value = jnp.where(short_id == at, fix, value)
                        upper_ref[pl.ds(begin + start, 16), lanes] = value.astype(BF)
            return 0

        lax.fori_loop(0, above, patch, 0, unroll=10)

    def second(ref, first_group):
        begin = pl.multiple_of((group - first_group) * block, 16)
        total = taps(ref, begin, block, wide, two_ref)
        own = first_ref[pl.ds(group * rows, rows)].reshape(block, chans).astype(F32)
        total = total + pltpu.roll(own, block - 2, axis=0)
        result = total.astype(BF)
        for i in range(rows):
            out_ref[i] = result[i * wide : i * wide + cols]

    pl.when(group < above // rows)(lambda: second(upper_ref, 0))
    pl.when(group >= above // rows)(lambda: second(lower_ref, above // rows))


def finished(upper, lower, first, sides, one, two, cols, lat_count):
    lat_rows, wide, chans = first.shape
    whole = pl.BlockSpec(memory_space=pltpu.VMEM)
    out, _, _ = pl.pallas_call(
        functools.partial(finish_kernel, lat_count),
        grid=(lat_rows // FINISH,),
        out_shape=(
            jax.ShapeDtypeStruct((lat_rows, cols, chans), BF),
            jax.ShapeDtypeStruct(upper.shape, BF),
            jax.ShapeDtypeStruct(lower.shape, BF),
        ),
        in_specs=[whole] * (5 + len(sides)),
        out_specs=(pl.BlockSpec((FINISH, cols, chans), lambda g: (g, 0, 0)), whole, whole),
        input_output_aliases={0: 1, 1: 2},
        scratch_shapes=[
            pltpu.VMEM((8 * wide, 3 * chans), BF),
            pltpu.VMEM((4, -(-UPPER // 16) * 16, chans), F32),
        ],
        compiler_params=params(26),
    )(upper, lower, first, *sides, one, two)
    return out


def row_pairs(lat_count, lon_count):
    half = lon_count // 2

    def flat(lat, lon):
        return lat * lon_count + lon % lon_count

    inner, outer = [], []
    for lon in range(lon_count):
        for lat in range(0, lat_count, 2):
            inner += [(flat(lat, lon), flat(lat + 1, lon)), (flat(lat + 1, lon), flat(lat, lon))]
        for lat in range(1, lat_count - 1, 2):
            outer += [(flat(lat, lon), flat(lat + 1, lon)), (flat(lat + 1, lon), flat(lat, lon))]
        outer += [(flat(lat, lon), flat(lat, lon + half)) for lat in (0, lat_count - 1)]
    return inner, outer


def shards(
    obs_features,
    obs_dest,
    obs_cells,
    obs_gauss,
    row_counts,
    background,
    w_in,
    w_bg,
    w_dens,
    conv_one,
    conv_two,
):
    nrows, nfeat = obs_features.shape
    lat_rows, cols, chans = background.shape
    axes = ("lat", "lon")
    devices = lax.axis_size(axes)
    lat_count, lon_count = lax.axis_size("lat"), lax.axis_size("lon")
    cap = 2 * nrows // devices
    wide = -(-(cols + 4) // 16) * 16
    send = pack(
        row_counts, obs_dest.reshape(1, nrows), obs_cells.T, obs_gauss.T, obs_features, devices, lon_count, cap, cols,
        lat_rows // BAND,
    )
    paired = send.shape
    send = send.reshape(devices, cap + META, nfeat)
    recv = lax.all_to_all(send, axes, split_axis=0, concat_axis=0, tiled=True).reshape(paired)
    back = projected(background, w_bg, wide)
    first, own_west, own_east, inner_row, outer_row = gridded(
        recv, back, w_in, w_dens.reshape(1, chans), cap, wide, lat_rows, cols
    )
    west = lax.ppermute(own_east, "lon", [(i, (i + 1) % lon_count) for i in range(lon_count)])
    east = lax.ppermute(own_west, "lon", [((i + 1) % lon_count, i) for i in range(lon_count)])
    one = conv_one.reshape(3, 3 * chans, chans)
    two = conv_two.reshape(3, 3 * chans, chans)
    upper = upper_part(first, one, own_west, UPPER)
    inner_row, outer_row = bordered(inner_row, outer_row, west, east, upper, lat_rows, cols)
    inner, outer = row_pairs(lat_count, lon_count)
    lower = lower_part(first, one, west, east, inner_row, lat_rows - UPPER, cols)
    inner_row = lax.ppermute(inner_row, axes, inner)
    outer_row = lax.ppermute(outer_row, axes, outer)
    sides = (own_west, own_east, west, east, inner_row, outer_row)
    return finished(upper, lower, first, sides, one, two, cols, lat_count)


def solution(mesh):
    rows = P(("lat", "lon"), None)
    in_specs = (rows, rows, rows, rows, P(("lat", "lon")), P("lat", "lon", None), P(), P(), P(), P(), P())
    return jax.shard_map(
        shards, mesh=mesh, in_specs=in_specs, out_specs=P("lat", "lon", None), check_vma=False
    )
```
